32 devices in a mesh: sec: 2 (over x), batch: 16 (over z, y, core), head: 1.
Axes of the slice: x: 2, y: 2, z: 4, core: 2. Of those that a mesh axis runs over, the one named last changes fastest.
Arguments:
- hidden_in: bfloat16 [512, 7168], P('batch'), may hold values from -6 to 6
- queries: bfloat16 [512, 128, 576], P('batch', ('sec', 'head')), may hold values from -8 to 8
- latent_cache: bfloat16 [512, 192, 576], P('batch'), may hold values from -8 to 8
- new_latent: bfloat16 [512, 576], P('batch'), may hold values from -8 to 8
- cache_lengths: int32 [512], P('batch'), may hold values from 1 to 192, 49152 in all
- value_up: bfloat16 [128, 512, 128], P(('sec', 'head')), may hold values from -0.25 to 0.25
- out_proj: bfloat16 [16384, 7168], P(('sec', 'head'), 'batch'), may hold values from -0.046875 to 0.046875
- norm_gain: float32 [7168], replicated, may hold values from 0.1 to 1.9
- router: bfloat16 [7168, 16], replicated, may hold values from -0.03125 to 0.03125
- expert_ids: int32 [512, 8], P('batch'), may hold values from 0 to 15, all different within a row; in each aligned block of 32 rows (0 to 31, 32 to 63, ...) at most 32 rows name the same one
- w_gate_up: bfloat16 [16, 7168, 2, 1024], P('batch', None, None, ('sec', 'head')), may hold values from -0.0625 to 0.0625
- w_down: bfloat16 [16, 1024, 7168], P('batch', ('sec', 'head')), may hold values from -0.1875 to 0.1875
Outputs:
- mixed_out: bfloat16 [512, 7168], P('batch', ('sec', 'head'))
The draws below stay inside these ranges and needn't reach their ends.
Inputs may be any that keep to these rules, and one draw needn't show every extreme that they name: `expert_ids`: each row names 8 different experts. Among the 32 rows of one index of batch (aligned blocks) no expert is named by more than 32 rows, a bound that some block reaches. `cache_lengths`: the lengths of all rows add up to 49152, and one row has exactly 192.
All inputs are finite; a program needn't handle non-finite values. No bound on the sum of `cache_lengths` on one device may be relied on, other than what follows from the above.
Results may differ from the reference program's by a relative error of at most 0.007.
Values may be sent and summed in bfloat16 or wider, within the bound.
No kernel may reach another device: no remote copies, remote signals or barrier semaphores. Data moves between devices by JAX's collectives and lax.ppermute only.
A program may use at most 128 MiB of HBM per device.

```python
import math
import jax
import jax.numpy as jnp
import numpy as np
from jax import lax

D = 7168
HEADS = 128
LAT = 512
HD = 128
QKD = 192
FF = 1024
TOP = 8
TOK_DEV = 32
CTX = 192
TOKENS = 512
EXPERTS = 16
KVW = 576
CAP = 32
N_BATCH = 16


def draw_latent_cache(key, part):
    noise = jnp.clip(jax.random.normal(jax.random.fold_in(key, 1), (TOKENS, CTX, KVW), jnp.float32), -4.0, 4.0)
    return noise.astype(jnp.bfloat16)


def draw_new_latent(key, part):
    noise = jnp.clip(jax.random.normal(jax.random.fold_in(key, 2), (TOKENS, KVW), jnp.float32), -4.0, 4.0)
    return noise.astype(jnp.bfloat16)


def draw_queries(key, part):
    noise = jnp.clip(jax.random.normal(jax.random.fold_in(key, 3), (TOKENS, HEADS, KVW), jnp.float32), -4.0, 4.0)
    return noise.astype(jnp.bfloat16)


def levels(own_key, extent, cuts, smallest, top_value):
    def one(axis_at, parts):
        heights = jax.random.uniform(jax.random.fold_in(jax.random.fold_in(own_key, 6), axis_at), (parts,), jnp.float32, smallest / len(cuts), top_value / len(cuts))
        return jnp.repeat(jnp.exp(heights), extent[axis_at] // parts).reshape((-1,) + (1,) * (len(extent) - axis_at - 1))

    loudness = one(*cuts[0])
    for cut in cuts[1:]:
        loudness = loudness * one(*cut)
    return loudness


def length_profile(number_of, total, most, skew):
    weights = [(1 << 20) // math.isqrt(rank ** skew) + 1 for rank in range(2, number_of + 1)]
    spare, given = total - most - (number_of - 1), [1] * (number_of - 1)
    while spare > 0:
        free = [i for i in range(number_of - 1) if given[i] < most]
        pool, remaining = sum([weights[i] for i in free]), spare
        for i in free:
            addition = min(most - given[i], max(1, remaining * weights[i] // pool), spare)
            given[i] = given[i] + addition
            spare = spare - addition
    return np.array([most] + given)


def uneven(key, count, total, most, skew):
    if count == 2:
        one = jax.random.randint(key, (), max(1, total - most), min(most, total - 1) + 1)
        return jnp.stack([one, total - one])
    lengths = jnp.asarray(length_profile(count, total, most, skew), jnp.int32)
    twos = (count - 1) // 2
    source_of, sink = lengths[1:1 + 2 * twos:2], lengths[2:2 + 2 * twos:2]
    room = jnp.minimum(source_of - 1, most - sink)
    moved = jax.random.randint(jax.random.fold_in(key, 1), (twos,), 0, 1 << 20) % (room + 1)
    lengths = lengths.at[1:1 + 2 * twos:2].set(source_of - moved).at[2:2 + 2 * twos:2].set(sink + moved)
    return lengths[jax.random.permutation(jax.random.fold_in(key, 2), count)]


def shared_out(stream_key, own, number, rows, count, top, limit, lean):
    order = jax.random.permutation(stream_key, count)
    packed, usual = load_shares(count, rows * top, limit, lean, True), load_shares(count, rows * top, limit, lean, False)
    places = jnp.arange(count)

    def named(sizes, offset_by):
        used = int((sizes > 0).sum())
        fixed = max(1, used // 4)
        moved = fixed + (places - fixed + offset_by * (used - fixed)) % max(1, count - fixed)
        return jnp.zeros((count,), jnp.int32).at[order[jnp.where(places < fixed, places, moved)]].set(jnp.asarray(sizes, jnp.int32))

    sizes = jnp.where(number % 4 == 0, named(packed, number // 4), named(usual, number - number // 4 - 1))
    mixed = jax.random.permutation(jax.random.fold_in(own, 3), count)
    donor, receiver = mixed[0:count // 2 * 2:2], mixed[1:count // 2 * 2:2]
    margin = jnp.minimum(sizes[donor] - 1, limit - sizes[receiver]) // 2
    margin = jnp.where((donor == order[0]) | (receiver == order[0]) | (sizes[receiver] == 0), 0, jnp.maximum(margin, 0))
    moved = jax.random.randint(jax.random.fold_in(own, 4), (count // 2,), 0, 1 << 20) % (margin + 1)
    sizes = sizes.at[donor].add(-moved).at[receiver].add(moved)
    members = jnp.searchsorted(jnp.cumsum(sizes), jnp.arange(rows * top), side="right").astype(jnp.int32)
    table = members.reshape(top, rows).T
    table = table[jax.random.permutation(jax.random.fold_in(own, 1), rows)]
    offset_by = jax.random.randint(jax.random.fold_in(own, 2), (rows, 1), 0, top)
    return jnp.take_along_axis(table, (jnp.arange(top)[None, :] + offset_by) % top, axis=1)


def load_shares(amount, total, limit, lean, full):
    portions = [(1 << 20) // math.isqrt(rank ** lean) + 1 for rank in range(1, amount + 1)]
    largest = limit if full else min(limit, max(-(-total // amount), total * portions[0] // sum(portions)))
    least = 1 if total - largest >= amount - 1 else 0
    holding, spare = [largest] + [least] * (amount - 1), total - largest - least * (amount - 1)
    while spare > 0:
        free = [i for i in range(1, amount) if holding[i] < largest] or [i for i in range(1, amount) if holding[i] < limit]
        pool, budget = sum([portions[i] for i in free]), spare
        for i in free:
            more = min(limit - holding[i], max(1, budget * portions[i] // pool), spare)
            holding[i] = holding[i] + more
            spare = spare - more
    return np.array(holding)


def centred(key, shape, scale, bound, cuts=(), kind=jnp.bfloat16):
    entries = scale * jax.random.normal(key, shape, jnp.float32)
    if cuts:
        entries = entries * levels(key, shape, cuts, -0.22, 0.18)
    return jnp.clip(entries, -bound, bound).astype(kind)


def setup_inputs(seed: int = 0) -> dict:
    splits = jax.random.split(jax.random.key(seed), 13)
    hidden_in = centred(splits[0], (TOKENS, D), 1.0, 6.0, ((0, 16),))
    queries = draw_queries(jax.random.fold_in(splits[12], 71), 0)
    latent_cache = draw_latent_cache(jax.random.fold_in(splits[12], 71), 0)
    new_latent = draw_new_latent(jax.random.fold_in(splits[12], 71), 0)
    cache_lengths = uneven(splits[4], TOKENS, TOKENS * CTX // 2, CTX, 2).astype(jnp.int32)
    value_up = centred(splits[5], (HEADS, LAT, HD), LAT ** -0.5, 0.25, ((0, 2),))
    out_proj = centred(splits[6], (HEADS * HD, D), (HEADS * HD) ** -0.5, 0.046875, ((0, 2), (1, 16)))
    norm_gain = jnp.clip(1.0 + 0.18 * jax.random.normal(splits[7], (D,), jnp.float32), 0.1, 1.9)
    router = centred(splits[8], (D, EXPERTS), (4 * D) ** -0.5, 0.03125)
    expert_ids_keys = jax.random.split(jax.random.fold_in(splits[9], 1), TOKENS // TOK_DEV)
    expert_ids_turns = jax.random.permutation(jax.random.fold_in(splits[9], 3), TOKENS // TOK_DEV)
    expert_ids = jax.vmap(lambda own, number: shared_out(jax.random.fold_in(splits[9], 2), own, number, TOK_DEV, EXPERTS, TOP, CAP, 2))(expert_ids_keys, expert_ids_turns).reshape((TOKENS, TOP))
    w_gate_up = centred(splits[10], (EXPERTS, D, 2, FF), D ** -0.5, 0.0625, ((0, 16), (3, 2)))
    w_down = centred(splits[11], (EXPERTS, FF, D), FF ** -0.5, 0.1875, ((0, 16), (1, 2)))
    return {"hidden_in": hidden_in, "queries": queries, "latent_cache": latent_cache, "new_latent": new_latent, "cache_lengths": cache_lengths, "value_up": value_up, "out_proj": out_proj, "norm_gain": norm_gain, "router": router, "expert_ids": expert_ids, "w_gate_up": w_gate_up, "w_down": w_down}


norm_epsilon = 1e-06
route_scale = 2.5

def reference(hidden_in, queries, latent_cache, new_latent, cache_lengths, value_up, out_proj, norm_gain, router, expert_ids, w_gate_up, w_down):
    score_scale = QKD ** (-0.5)
    query_full = queries.astype(jnp.float32)
    cache_full = latent_cache.astype(jnp.float32)
    newest = new_latent.astype(jnp.float32)
    scores = jnp.einsum('thk,tjk->thj', query_full, cache_full) * score_scale
    own_score = jnp.einsum('thk,tk->th', query_full, newest) * score_scale
    positions = jnp.arange(CTX, dtype=jnp.int32)
    in_cache = positions[None, None, :] < cache_lengths[:, None, None]
    scores = jnp.where(in_cache, scores, -jnp.inf)
    top_score = jnp.maximum(lax.optimization_barrier(jnp.max(scores, axis=2)), own_score)
    cache_exp = jnp.exp(scores - top_score[:, :, None])
    own_exp = jnp.exp(own_score - top_score)
    softmax_sum = lax.optimization_barrier(jnp.sum(cache_exp, axis=2)) + own_exp
    cache_weights = (cache_exp / softmax_sum[:, :, None]).astype(jnp.bfloat16)
    own_weights = (own_exp / softmax_sum).astype(jnp.bfloat16)
    latent_out = jnp.einsum('thj,tjc->thc', cache_weights.astype(jnp.float32), cache_full[:, :, :LAT])
    latent_out = latent_out + own_weights.astype(jnp.float32)[:, :, None] * newest[:, None, :LAT]
    latent_out = latent_out.astype(jnp.bfloat16)
    head_out = jnp.einsum('thc,hcd->thd', latent_out.astype(jnp.float32), value_up.astype(jnp.float32))
    head_out = head_out.astype(jnp.bfloat16).reshape(TOKENS, HEADS * HD)
    attention = jnp.dot(head_out, out_proj, preferred_element_type=jnp.float32)
    residual = hidden_in.astype(jnp.float32) + attention
    mean_square = lax.optimization_barrier(jnp.mean(residual * residual, axis=1, keepdims=True))
    normed = (residual * lax.rsqrt(mean_square + norm_epsilon) * norm_gain).astype(jnp.bfloat16)
    logits = jnp.dot(normed, router, preferred_element_type=jnp.float32)
    affinity = jax.nn.sigmoid(logits)
    picked = jnp.take_along_axis(affinity, expert_ids, axis=1)
    route_weights = route_scale * picked / lax.optimization_barrier(jnp.sum(picked, axis=1, keepdims=True))
    slot_limit = N_BATCH * CAP

    def one_expert(mixture, expert):
        hit_mask = expert_ids == expert
        token_weight = lax.optimization_barrier(jnp.sum(jnp.where(hit_mask, route_weights, jnp.zeros_like(route_weights)), axis=1))
        routed = jnp.any(hit_mask, axis=1)
        chosen = jnp.nonzero(routed, size=slot_limit, fill_value=0)[0].astype(jnp.int32)
        occupied = jnp.arange(slot_limit, dtype=jnp.int32) < jnp.sum(routed.astype(jnp.int32))
        inputs = normed[chosen]
        gate_up = jnp.dot(inputs, w_gate_up[expert].reshape(D, 2 * FF), preferred_element_type=jnp.float32)
        activated = (jax.nn.silu(gate_up[:, :FF]) * gate_up[:, FF:]).astype(jnp.bfloat16)
        expert_out = jnp.dot(activated, w_down[expert], preferred_element_type=jnp.float32)
        slot_weight = jnp.where(occupied, token_weight[chosen], jnp.zeros_like(token_weight[chosen]))
        mixture = mixture.at[chosen].add(slot_weight[:, None] * expert_out)
        return (mixture, None)
    mixture, unused = lax.scan(one_expert, jnp.zeros((TOKENS, D), jnp.float32), jnp.arange(EXPERTS, dtype=jnp.int32))
    return (residual + mixture).astype(jnp.bfloat16)
```

```python
import jax
import jax.numpy as jnp
from jax import lax
from jax.sharding import Mesh, PartitionSpec as P

QKD = 192
TOP = 8

norm_epsilon = 1e-06
route_scale = 2.5

GROUP = ("sec", "head")
SWAP = [(0, 1), (1, 0)]


def attend(queries, latent_cache, new_latent, cache_lengths, value_up):
    row_count = queries.shape[0]
    latent_width = value_up.shape[1]
    cache_depth = latent_cache.shape[1]
    score_scale = QKD ** (-0.5)
    scores = (
        jnp.einsum("thk,tjk->thj", queries, latent_cache, preferred_element_type=jnp.float32)
        * score_scale
    )
    own_score = (
        jnp.einsum("thk,tk->th", queries, new_latent, preferred_element_type=jnp.float32)
        * score_scale
    )
    positions = lax.broadcasted_iota(jnp.int32, (1, 1, cache_depth), 2)
    in_cache = positions < cache_lengths[:, None, None]
    scores = jnp.where(in_cache, scores, -jnp.inf)
    top_score = jnp.maximum(jnp.max(scores, axis=2), own_score)
    cache_exp = jnp.exp(scores - top_score[:, :, None])
    own_exp = jnp.exp(own_score - top_score)
    softmax_sum = jnp.sum(cache_exp, axis=2) + own_exp
    cache_weights = (cache_exp / softmax_sum[:, :, None]).astype(jnp.bfloat16)
    own_weights = (own_exp / softmax_sum).astype(jnp.bfloat16)
    latent_out = jnp.einsum(
        "thj,tjc->thc",
        cache_weights,
        latent_cache[:, :, :latent_width],
        preferred_element_type=jnp.float32,
    )
    latent_out = latent_out + own_weights.astype(jnp.float32)[:, :, None] * new_latent[
        :, None, :latent_width
    ].astype(jnp.float32)
    latent_out = latent_out.astype(jnp.bfloat16)
    head_out = jnp.einsum(
        "thc,hcd->thd", latent_out, value_up, preferred_element_type=jnp.float32
    ).astype(jnp.bfloat16)
    return head_out.reshape(row_count, -1)


def body(
    hidden_in,
    queries,
    latent_cache,
    new_latent,
    cache_lengths,
    value_up,
    out_proj,
    norm_gain,
    router,
    expert_ids,
    w_gate_up,
    w_down,
):
    rows = hidden_in.shape[0]
    width = hidden_in.shape[1]
    chips = lax.axis_size("chip")
    cores = lax.axis_size("core")
    groups = lax.axis_size(GROUP)
    core = lax.axis_index("core")
    chip = lax.axis_index("chip")
    group = lax.axis_index(GROUP)
    expert = chip * cores + core
    chip_cols = width // chips
    share = rows // groups

    own_rows = lax.dynamic_slice_in_dim(hidden_in, group * share, share, 0)
    outgoing = own_rows.reshape(share, chips, 1, chip_cols)
    outgoing = jnp.broadcast_to(outgoing, (share, chips, cores, chip_cols)).transpose(1, 2, 0, 3)
    hidden_cols = lax.all_to_all(
        outgoing.reshape(chips * cores, share, chip_cols),
        ("chip", "core"),
        split_axis=0,
        concat_axis=0,
        tiled=True,
    ).reshape(chips, cores, share, chip_cols)
    hidden_cols = lax.dynamic_index_in_dim(hidden_cols, core, 1, keepdims=False)
    all_ids = lax.all_gather(expert_ids, ("chip", "core"), axis=0, tiled=True)

    head_out = attend(queries, latent_cache, new_latent, cache_lengths, value_up)

    near = lax.all_gather(head_out, "chip", axis=0, tiled=True)
    far = lax.ppermute(near, "core", SWAP)
    near_cols = jnp.dot(near, out_proj, preferred_element_type=jnp.float32)
    far_cols = jnp.dot(far, out_proj, preferred_element_type=jnp.float32)
    got_cols = lax.ppermute(far_cols, "core", SWAP)
    low = jnp.where(core == 0, near_cols, got_cols)
    high = jnp.where(core == 0, got_cols, near_cols)
    part = jnp.concatenate([low, high], axis=1).reshape(chips, groups, share, chip_cols)
    if groups == 2:
        other = lax.dynamic_index_in_dim(part, 1 - group, 1, keepdims=False)
        other = lax.ppermute(other.astype(jnp.bfloat16), "sec", SWAP)
        attention = lax.dynamic_index_in_dim(part, group, 1, keepdims=False) + other
    else:
        attention = lax.psum_scatter(part, GROUP, scatter_dimension=1, tiled=False)
    residual = (hidden_cols.astype(jnp.float32) + attention).astype(jnp.bfloat16)

    residual = residual.reshape(chips * share, chip_cols)
    near_res = lax.all_gather(residual, GROUP + ("chip",), axis=0, tiled=False)
    far_res = lax.ppermute(near_res, "core", SWAP)

    ids = all_ids.reshape(chips, cores, groups, share, TOP).transpose(1, 2, 0, 3, 4)
    ids = ids.reshape(cores, groups * chips * share, TOP)
    near_ids = lax.dynamic_index_in_dim(ids, core, 0, keepdims=False)
    far_ids = lax.dynamic_index_in_dim(ids, cores - 1 - core, 0, keepdims=False)
    gate_up_weight = w_gate_up[0].reshape(width, -1)
    hidden_share = w_down.shape[1]
    expert_count = router.shape[1]

    def run_expert(res, row_ids):
        res = res.reshape(groups, chips, chips * share, chip_cols).transpose(0, 2, 1, 3)
        res = res.reshape(groups * chips * share, width).astype(jnp.float32)
        mean_square = jnp.mean(res * res, axis=1, keepdims=True)
        normed = (res * lax.rsqrt(mean_square + norm_epsilon) * norm_gain).astype(jnp.bfloat16)
        affinity = jax.nn.sigmoid(jnp.dot(normed, router, preferred_element_type=jnp.float32))
        grid = lax.broadcasted_iota(jnp.int32, (1, 1, expert_count), 2)
        chosen = jnp.any(row_ids[:, :, None] == grid, axis=1)
        total = jnp.sum(jnp.where(chosen, affinity, 0.0), axis=1, keepdims=True)
        mine = lax.broadcasted_iota(jnp.int32, (1, expert_count), 1) == expert
        weight = jnp.sum(jnp.where(chosen & mine, affinity, 0.0), axis=1, keepdims=True)
        weight = route_scale * weight / total
        gate_up = jnp.dot(normed, gate_up_weight, preferred_element_type=jnp.float32)
        activated = (jax.nn.silu(gate_up[:, :hidden_share]) * gate_up[:, hidden_share:]).astype(
            jnp.bfloat16
        )
        out = jnp.dot(activated, w_down[0], preferred_element_type=jnp.float32)
        return (out * weight).astype(jnp.bfloat16)

    far_out = run_expert(far_res, far_ids)
    got_out = lax.ppermute(far_out, "core", SWAP)
    near_out = run_expert(near_res, near_ids)
    summed = (near_out.astype(jnp.float32) + got_out).astype(jnp.bfloat16)
    summed = summed.reshape(groups, chips, share, width)
    summed = lax.psum_scatter(summed, "chip", scatter_dimension=1, tiled=False)
    summed = summed.reshape(rows, groups, width // groups)
    if groups == 2:
        other = lax.ppermute(
            lax.dynamic_index_in_dim(summed, 1 - group, 1, keepdims=False), "sec", SWAP
        )
        mixture = lax.dynamic_index_in_dim(summed, group, 1, keepdims=False).astype(
            jnp.float32
        ) + other
    else:
        mixture = lax.psum_scatter(
            summed.astype(jnp.float32), GROUP, scatter_dimension=1, tiled=False
        )

    own = near_res.reshape(groups, groups, chips // groups, chips, share, chip_cols)
    own = lax.dynamic_index_in_dim(own, group, 1, keepdims=False)
    own = lax.dynamic_index_in_dim(own, chip, 2, keepdims=False)
    own = own.transpose(0, 2, 1, 3).reshape(rows, width // groups)
    return (own.astype(jnp.float32) + mixture).astype(jnp.bfloat16)


def solution(mesh):
    sec, batch, head = mesh.shape["sec"], mesh.shape["batch"], mesh.shape["head"]
    devices = mesh.devices.reshape(sec, batch // 2, 2, head)
    split = Mesh(devices, ("sec", "chip", "core", "head"))
    tokens = ("chip", "core")
    in_specs = (
        P(tokens, None),
        P(tokens, GROUP, None),
        P(tokens, None, None),
        P(tokens, None),
        P(tokens),
        P(GROUP, None, None),
        P(GROUP, tokens),
        P(),
        P(),
        P(tokens, None),
        P(tokens, None, None, GROUP),
        P(tokens, GROUP, None),
    )
    out_specs = P(tokens, GROUP)
    return jax.shard_map(body, mesh=split, in_specs=in_specs, out_specs=out_specs, check_vma=False)
```

```python
import functools

import jax
import jax.numpy as jnp
from jax import lax
from jax.experimental import pallas as pl
from jax.experimental.pallas import tpu as pltpu
from jax.sharding import Mesh, PartitionSpec as P

QKD = 192
TOP = 8

norm_epsilon = 1e-06
route_scale = 2.5

GROUP = ("sec", "head")
SWAP = [(0, 1), (1, 0)]
CHUNKS = 2
VMEM = 56 * 1024 * 1024
NT = (((1,), (1,)), ((), ()))


def attend(queries, latent_cache, new_latent, cache_lengths, value_up):
    row_count = queries.shape[0]
    latent_width = value_up.shape[1]
    cache_depth = latent_cache.shape[1]
    score_scale = QKD ** (-0.5)
    scores = (
        jnp.einsum("thk,tjk->thj", queries, latent_cache, preferred_element_type=jnp.float32)
        * score_scale
    )
    own_score = (
        jnp.einsum("thk,tk->th", queries, new_latent, preferred_element_type=jnp.float32)
        * score_scale
    )
    positions = lax.broadcasted_iota(jnp.int32, (1, 1, cache_depth), 2)
    in_cache = positions < cache_lengths[:, None, None]
    scores = jnp.where(in_cache, scores, -jnp.inf)
    top_score = jnp.maximum(jnp.max(scores, axis=2), own_score)
    cache_exp = jnp.exp(scores - top_score[:, :, None])
    own_exp = jnp.exp(own_score - top_score)
    softmax_sum = jnp.sum(cache_exp, axis=2) + own_exp
    cache_weights = (cache_exp / softmax_sum[:, :, None]).astype(jnp.bfloat16)
    own_weights = (own_exp / softmax_sum).astype(jnp.bfloat16)
    latent_out = jnp.einsum(
        "thj,tjc->thc",
        cache_weights,
        latent_cache[:, :, :latent_width],
        preferred_element_type=jnp.float32,
    )
    latent_out = latent_out + own_weights.astype(jnp.float32)[:, :, None] * new_latent[
        :, None, :latent_width
    ].astype(jnp.float32)
    latent_out = latent_out.astype(jnp.bfloat16)
    head_out = jnp.einsum(
        "thc,hcd->thd", latent_out, value_up, preferred_element_type=jnp.float32
    ).astype(jnp.bfloat16)
    return head_out.reshape(row_count, -1)


def place_of(chip, chips):
    return jnp.where(chip % 2 == 0, chip // 2, chips - 1 - chip // 2)


def chip_at(place, chips):
    place = place % chips
    return jnp.where(place < chips // 2, 2 * place, 2 * (chips - 1 - place) + 1)


def ring_steps(chips):
    ring = list(range(0, chips, 2)) + list(range(chips - 1, 0, -2))
    ahead = [(ring[i], ring[(i + 1) % chips]) for i in range(chips)]
    return ahead, [(b, a) for a, b in ahead]


def split_axis(array, axis):
    half = array.shape[axis] // 2
    return (
        lax.slice_in_dim(array, 0, half, axis=axis),
        lax.slice_in_dim(array, half, 2 * half, axis=axis),
    )


def ring_gather(block, axis):
    chips = lax.axis_size("chip")
    ahead, back = ring_steps(chips)
    behind, before = [block], [block]
    for _ in range(chips // 2 - 1):
        behind.append(lax.ppermute(behind[-1], "chip", ahead))
        before.append(lax.ppermute(before[-1], "chip", back))
    low = lax.ppermute(split_axis(behind[-1], axis)[0], "chip", ahead)
    high = lax.ppermute(split_axis(before[-1], axis)[1], "chip", back)
    pieces = [block]
    for d in range(1, chips // 2):
        pieces += [behind[d], before[d]]
    return pieces + [low, high]


def ring_places():
    chips = lax.axis_size("chip")
    place = place_of(lax.axis_index("chip"), chips)
    offsets = [0]
    for d in range(1, chips // 2):
        offsets += [-d, d]
    offsets.append(chips // 2)
    return chip_at(place + jnp.array(offsets, jnp.int32), chips).astype(jnp.int32)


def ring_reduce(blocks):
    chips = blocks.shape[0]
    ahead, back = ring_steps(chips)
    place = place_of(lax.axis_index("chip"), chips)

    def block(d):
        return lax.dynamic_index_in_dim(blocks, chip_at(place + d, chips), 0, keepdims=False)

    def add(a, b):
        return (a.astype(jnp.float32) + b.astype(jnp.float32)).astype(jnp.bfloat16)

    far_low, far_high = split_axis(block(chips // 2), 1)
    up = lax.ppermute(far_low, "chip", ahead)
    down = lax.ppermute(far_high, "chip", back)
    for d in range(chips // 2 - 1, 0, -1):
        to_up, to_down = block(d), block(-d)
        if d == chips // 2 - 1:
            low, high = split_axis(to_up, 1)
            to_up = jnp.concatenate([add(low, up), high], axis=1)
            low, high = split_axis(to_down, 1)
            to_down = jnp.concatenate([low, add(high, down)], axis=1)
        else:
            to_up, to_down = add(to_up, up), add(to_down, down)
        up = lax.ppermute(to_up, "chip", ahead)
        down = lax.ppermute(to_down, "chip", back)
    return block(0).astype(jnp.float32) + up.astype(jnp.float32) + down.astype(jnp.float32)


def piece_copies(pieces, order, dest, sems, axis):
    copies = []
    last = len(pieces) - 2
    for i, piece in enumerate(pieces):
        target = dest(order[min(i, last)])
        if i >= last:
            half = piece.shape[axis]
            span = pl.ds(0 if i == last else half, half)
            target = target.at[span, :] if axis == 0 else target.at[:, span]
        copies.append(pltpu.make_async_copy(piece, target, sems.at[i]))
    return copies


def project_kernel(count, order, weight, *refs):
    near, far = refs[:count], refs[count : 2 * count]
    out, rows, held, near_sems, far_sems, weight_sems = refs[2 * count :]
    steps, _, depth = held.shape
    copies = piece_copies(near, order, lambda c: rows.at[0, c], near_sems, 1)
    copies += piece_copies(far, order, lambda c: rows.at[1, c], far_sems, 1)

    def weight_copy(k):
        columns = pl.ds(pl.multiple_of(k * depth, depth), depth)
        return pltpu.make_async_copy(weight.at[:, columns], held.at[k], weight_sems.at[k])

    for copy in copies:
        copy.start()
    for k in range(steps):
        weight_copy(k).start()
    for copy in copies:
        copy.wait()
    out[...] = jnp.zeros_like(out)

    @pl.loop(0, steps)
    def _(k):
        weight_copy(k).wait()
        columns = pl.ds(pl.multiple_of(k * depth, depth), depth)
        block = rows[:, :, :, columns].reshape(out.shape[0], depth)
        out[...] += lax.dot_general(block, held[k], NT, preferred_element_type=jnp.float32)


def project(order, near, far, weight):
    chips = order.shape[0]
    count = len(near)
    rows, depth = near[0].shape
    columns = weight.shape[0]
    steps = 8
    any_space = pl.BlockSpec(memory_space=pl.ANY)
    total = 2 * chips * rows
    return pl.pallas_call(
        functools.partial(project_kernel, count),
        out_shape=jax.ShapeDtypeStruct((total, columns), jnp.float32),
        in_specs=[pl.BlockSpec(memory_space=pltpu.SMEM)] + [any_space] * (1 + 2 * count),
        out_specs=pl.BlockSpec(memory_space=pltpu.VMEM),
        scratch_shapes=[
            pltpu.VMEM((2, chips, rows, depth), jnp.bfloat16),
            pltpu.VMEM((steps, columns, depth // steps), jnp.bfloat16),
            pltpu.SemaphoreType.DMA((count,)),
            pltpu.SemaphoreType.DMA((count,)),
            pltpu.SemaphoreType.DMA((steps,)),
        ],
        compiler_params=pltpu.CompilerParams(vmem_limit_bytes=VMEM),
        cost_estimate=pl.CostEstimate(
            flops=2 * total * depth * columns,
            bytes_accessed=2 * depth * (total + columns) + 4 * total * columns,
            transcendentals=0,
        ),
    )(order, weight, *near, *far)


def expert_kernel(count, order, gate_up, down, gain, router, picks, *refs):
    near, far = refs[:count], refs[count : 2 * count]
    out, own, held, first, second, total, logits, squares = refs[2 * count : 2 * count + 8]
    near_sems, far_sems, first_sems, second_sem = refs[2 * count + 8 :]
    chips, _, rows, depth = held.shape
    width = out.shape[-1]
    hidden = down.shape[0]
    copies = piece_copies(near, order, lambda c: held.at[c, 0], near_sems, 0)
    copies += piece_copies(far, order, lambda c: held.at[c, 1], far_sems, 0)
    for copy in copies:
        copy.start()

    def first_copy(c):
        part = pl.ds(pl.multiple_of(c * depth, 16), depth)
        return pltpu.make_async_copy(gate_up.at[part, :], first.at[c], first_sems.at[c])

    second_copy = pltpu.make_async_copy(down, second, second_sem)
    for c in range(chips):
        first_copy(c).start()
    second_copy.start()
    for copy in copies:
        copy.wait()
    total[...] = jnp.zeros_like(total)
    logits[...] = jnp.zeros_like(logits)
    squares[...] = jnp.zeros_like(squares)

    @pl.loop(0, chips)
    def _(c):
        block = held[c].reshape(2 * rows, depth).astype(jnp.float32)
        squares[...] += jnp.sum(block * block, axis=1, keepdims=True)
        scaled = (block * gain[c]).astype(jnp.bfloat16)
        logits[...] += lax.dot_general(scaled, router[c], NT, preferred_element_type=jnp.float32)
        first_copy(c).wait()
        total[...] += jnp.dot(scaled, first[c], preferred_element_type=jnp.float32)

    norm = lax.rsqrt(squares[:, 0:1] * (1.0 / width) + norm_epsilon)
    affinity = jax.nn.sigmoid(logits[...] * norm)
    chosen = affinity * picks[0]
    mine = affinity * picks[1]
    weight = route_scale * jnp.sum(mine, axis=1, keepdims=True) / jnp.sum(chosen, axis=1, keepdims=True)
    gate = total[:, :hidden] * norm
    up = total[:, hidden:] * norm
    active = (gate * jax.nn.sigmoid(gate) * up).astype(jnp.bfloat16)
    second_copy.wait()
    span = width // 8

    @pl.loop(0, 8)
    def _(n):
        columns = pl.ds(pl.multiple_of(n * span, span), span)
        result = jnp.dot(active, second[:, columns], preferred_element_type=jnp.float32) * weight
        out[:, :, columns] = result.astype(jnp.bfloat16).reshape(2, rows, span)

    mine_rows = rows // chips
    at = pl.ds(pl.multiple_of(order[0] * mine_rows, mine_rows), mine_rows)

    @pl.loop(0, chips)
    def _(c):
        own[c] = held[c, 0, at, :]


def experts(order, near, far, gate_up, down, gain, router, picks):
    chips = order.shape[0]
    count = len(near)
    rows, depth = near[0].shape
    width = chips * depth
    hidden = down.shape[0]
    names = router.shape[1]
    any_space = pl.BlockSpec(memory_space=pl.ANY)
    vmem = pl.BlockSpec(memory_space=pltpu.VMEM)
    return pl.pallas_call(
        functools.partial(expert_kernel, count),
        out_shape=(
            jax.ShapeDtypeStruct((2, rows, width), jnp.bfloat16),
            jax.ShapeDtypeStruct((chips, rows // chips, depth), jnp.bfloat16),
        ),
        in_specs=[pl.BlockSpec(memory_space=pltpu.SMEM), any_space, any_space, vmem, vmem, vmem]
        + [any_space] * (2 * count),
        out_specs=(vmem, vmem),
        scratch_shapes=[
            pltpu.VMEM((chips, 2, rows, depth), jnp.bfloat16),
            pltpu.VMEM((chips, depth, 2 * hidden), jnp.bfloat16),
            pltpu.VMEM((hidden, width), jnp.bfloat16),
            pltpu.VMEM((2 * rows, 2 * hidden), jnp.float32),
            pltpu.VMEM((2 * rows, names), jnp.float32),
            pltpu.VMEM((2 * rows, 128), jnp.float32),
            pltpu.SemaphoreType.DMA((count,)),
            pltpu.SemaphoreType.DMA((count,)),
            pltpu.SemaphoreType.DMA((chips,)),
            pltpu.SemaphoreType.DMA(()),
        ],
        compiler_params=pltpu.CompilerParams(vmem_limit_bytes=VMEM),
        cost_estimate=pl.CostEstimate(
            flops=2 * 2 * rows * width * 3 * hidden,
            bytes_accessed=2 * width * (3 * hidden + 4 * rows),
            transcendentals=2 * rows * hidden,
        ),
    )(order, gate_up, down, gain, router, picks, *near, *far)


def body(
    hidden_in,
    queries,
    latent_cache,
    new_latent,
    cache_lengths,
    value_up,
    out_proj,
    norm_gain,
    router,
    expert_ids,
    w_gate_up,
    w_down,
):
    rows = hidden_in.shape[0]
    width = hidden_in.shape[1]
    chips = lax.axis_size("chip")
    cores = lax.axis_size("core")
    groups = lax.axis_size(GROUP)
    core = lax.axis_index("core")
    chip = lax.axis_index("chip")
    group = lax.axis_index(GROUP)
    place = chip * cores + core
    chip_cols = width // chips
    expert_count = router.shape[1]
    share = rows // CHUNKS
    order = ring_places()

    outgoing = hidden_in.reshape(rows, chips, chip_cols).transpose(1, 0, 2)
    outgoing = jnp.broadcast_to(outgoing[:, None], (chips, cores, rows, chip_cols))
    hidden_cols = lax.all_to_all(
        outgoing.reshape(chips * cores, rows, chip_cols),
        ("chip", "core"),
        split_axis=0,
        concat_axis=0,
        tiled=True,
    ).reshape(chips, cores, rows, chip_cols)
    hidden_cols = lax.dynamic_index_in_dim(hidden_cols, core, 1, keepdims=False)

    all_ids = jnp.zeros((TOP, chips * cores * rows), jnp.int32)
    all_ids = lax.dynamic_update_slice(all_ids, expert_ids.T, (0, place * rows))
    all_ids = all_ids + lax.ppermute(all_ids, "core", SWAP)
    step = 1
    while step < chips:
        all_ids = all_ids + lax.ppermute(all_ids, "chip", [(i, i ^ step) for i in range(chips)])
        step *= 2
    grid = lax.broadcasted_iota(jnp.int32, (1, expert_count), 1)
    chosen = jnp.any(all_ids[:, :, None] == grid[None], axis=0).astype(jnp.float32)
    chosen = chosen.reshape(chips, cores, CHUNKS, share, expert_count)
    chosen = jnp.where(core == 0, chosen, chosen[:, ::-1])
    chosen = chosen.transpose(2, 1, 0, 3, 4).reshape(CHUNKS, -1, expert_count)
    picks = jnp.stack([chosen, chosen * (grid == place)], axis=1)

    gate_up = w_gate_up[0].reshape(width, -1)
    gain = norm_gain.reshape(chips, 1, chip_cols)
    router_rows = router.T.reshape(expert_count, chips, chip_cols).transpose(1, 0, 2)

    outs = []
    for h in range(CHUNKS):
        mine = slice(h * share, (h + 1) * share)
        head_out = attend(
            queries[mine], latent_cache[mine], new_latent[mine], cache_lengths[mine], value_up
        )
        near = ring_gather(head_out, 1)
        far = [lax.ppermute(piece, "core", SWAP) for piece in near]
        cols = project(order, near, far, out_proj.T)
        cols = cols.reshape(2, chips * share, cols.shape[1])
        got = lax.ppermute(cols[1], "core", SWAP)
        low = jnp.where(core == 0, cols[0], got)
        high = jnp.where(core == 0, got, cols[0])
        part = jnp.concatenate([low, high], axis=1)
        if groups == 2:
            attention = part + lax.ppermute(part.astype(jnp.bfloat16), "sec", SWAP)
        else:
            attention = lax.psum(part, GROUP)
        hidden_part = hidden_cols[:, mine].reshape(chips * share, chip_cols)
        residual = (hidden_part.astype(jnp.float32) + attention).astype(jnp.bfloat16)

        near = ring_gather(residual, 0)
        far = [lax.ppermute(piece, "core", SWAP) for piece in near]
        terms, own = experts(order, near, far, gate_up, w_down[0], gain, router_rows, picks[h])
        got = lax.ppermute(terms[1], "core", SWAP)
        summed = (terms[0].astype(jnp.float32) + got.astype(jnp.float32)).astype(jnp.bfloat16)
        mixture = ring_reduce(summed.reshape(chips, share, width))
        mixture = mixture.reshape(share, groups, width // groups)
        if groups == 2:
            other = lax.dynamic_index_in_dim(mixture, 1 - group, 1, keepdims=False)
            other = lax.ppermute(other.astype(jnp.bfloat16), "sec", SWAP)
            mixture = lax.dynamic_index_in_dim(mixture, group, 1, keepdims=False) + other
        else:
            mixture = lax.psum_scatter(mixture, GROUP, scatter_dimension=1, tiled=False)
        own = own.reshape(groups, chips // groups, share, chip_cols)
        own = lax.dynamic_index_in_dim(own, group, 0, keepdims=False)
        own = own.transpose(1, 0, 2).reshape(share, width // groups)
        outs.append((own.astype(jnp.float32) + mixture).astype(jnp.bfloat16))
    return jnp.concatenate(outs, axis=0)


def solution(mesh):
    sec, batch, head = mesh.shape["sec"], mesh.shape["batch"], mesh.shape["head"]
    devices = mesh.devices.reshape(sec, batch // 2, 2, head)
    split = Mesh(devices, ("sec", "chip", "core", "head"))
    tokens = ("chip", "core")
    in_specs = (
        P(tokens, None),
        P(tokens, GROUP, None),
        P(tokens, None, None),
        P(tokens, None),
        P(tokens),
        P(GROUP, None, None),
        P(GROUP, tokens),
        P(),
        P(),
        P(tokens, None),
        P(tokens, None, None, GROUP),
        P(tokens, GROUP, None),
    )
    out_specs = P(tokens, GROUP)
    return jax.shard_map(body, mesh=split, in_specs=in_specs, out_specs=out_specs, check_vma=False)
```

```python
import jax
import jax.numpy as jnp
from jax import lax
from jax.sharding import Mesh, PartitionSpec as P

QKD = 192
TOP = 8

norm_epsilon = 1e-06
route_scale = 2.5

GROUP = ("sec", "head")
SWAP = [(0, 1), (1, 0)]
CHUNKS = 2


def attend(queries, latent_cache, new_latent, cache_lengths, value_up):
    row_count = queries.shape[0]
    latent_width = value_up.shape[1]
    cache_depth = latent_cache.shape[1]
    score_scale = QKD ** (-0.5)
    scores = (
        jnp.einsum("thk,tjk->thj", queries, latent_cache, preferred_element_type=jnp.float32)
        * score_scale
    )
    own_score = (
        jnp.einsum("thk,tk->th", queries, new_latent, preferred_element_type=jnp.float32)
        * score_scale
    )
    positions = lax.broadcasted_iota(jnp.int32, (1, 1, cache_depth), 2)
    in_cache = positions < cache_lengths[:, None, None]
    scores = jnp.where(in_cache, scores, -jnp.inf)
    top_score = jnp.maximum(jnp.max(scores, axis=2), own_score)
    cache_exp = jnp.exp(scores - top_score[:, :, None])
    own_exp = jnp.exp(own_score - top_score)
    softmax_sum = jnp.sum(cache_exp, axis=2) + own_exp
    cache_weights = (cache_exp / softmax_sum[:, :, None]).astype(jnp.bfloat16)
    own_weights = (own_exp / softmax_sum).astype(jnp.bfloat16)
    latent_out = jnp.einsum(
        "thj,tjc->thc",
        cache_weights,
        latent_cache[:, :, :latent_width],
        preferred_element_type=jnp.float32,
    )
    latent_out = latent_out + own_weights.astype(jnp.float32)[:, :, None] * new_latent[
        :, None, :latent_width
    ].astype(jnp.float32)
    latent_out = latent_out.astype(jnp.bfloat16)
    head_out = jnp.einsum(
        "thc,hcd->thd", latent_out, value_up, preferred_element_type=jnp.float32
    ).astype(jnp.bfloat16)
    return head_out.reshape(row_count, -1)


def place_of(chip, chips):
    return jnp.where(chip % 2 == 0, chip // 2, chips - 1 - chip // 2)


def chip_at(place, chips):
    place = place % chips
    return jnp.where(place < chips // 2, 2 * place, 2 * (chips - 1 - place) + 1)


def ring_step(block):
    chips = lax.axis_size("chip")
    ring = list(range(0, chips, 2)) + list(range(chips - 1, 0, -2))
    pairs = []
    for i in range(chips):
        here, there = ring[i], ring[(i + 1) % chips]
        pairs += [(2 * here, 2 * there), (2 * there + 1, 2 * here + 1)]
    return lax.ppermute(block, ("chip", "core"), pairs)


def swap_cores(block):
    return lax.ppermute(block, "core", SWAP)


def by_core(core, first, second):
    return jnp.where(core == 0, first, second), jnp.where(core == 0, second, first)


def ring_gather(block, axis):
    chips = lax.axis_size("chip")
    core = lax.axis_index("core")
    half = block.shape[axis] // 2
    pieces, moving = [block], block
    for _ in range(chips // 2 - 1):
        moving = ring_step(moving)
        pieces += [moving, swap_cores(moving)]
    part = ring_step(lax.dynamic_slice_in_dim(moving, core * half, half, axis))
    low, high = by_core(core, part, swap_cores(part))
    return pieces + [jnp.concatenate([low, high], axis=axis)]


def ring_order():
    chips = lax.axis_size("chip")
    place = place_of(lax.axis_index("chip"), chips)
    sign = 2 * lax.axis_index("core") - 1
    places = [place]
    for d in range(1, chips // 2):
        places += [place + sign * d, place - sign * d]
    places.append(place + chips // 2)
    return [chip_at(p, chips) for p in places]


def plus(a, b):
    return a.astype(jnp.float32) + b.astype(jnp.float32)


def reduce_order():
    chips = lax.axis_size("chip")
    place = place_of(lax.axis_index("chip"), chips)
    sign = 1 - 2 * lax.axis_index("core")
    keep = [chip_at(place + sign * d, chips) for d in range(chips // 2 - 1, 0, -1)]
    give = [chip_at(place - sign * d, chips) for d in range(chips // 2 - 1, 0, -1)]
    return chip_at(place + chips // 2, chips), keep, give


def reduce_rows(array):
    chips, cores, rows = array.shape[:3]
    core = lax.axis_index("core")
    chip = lax.axis_index("chip")
    far, keep, give = reduce_order()
    rest = array.shape[3:]

    def pick(at, side):
        start = (at, side, 0) + (0,) * len(rest)
        return lax.dynamic_slice(array, start, (1, 1, rows) + rest).reshape((rows,) + rest)

    def whole(at):
        return lax.dynamic_index_in_dim(array, at, 0, keepdims=False).reshape((2 * rows,) + rest)

    def order(side, middle):
        return jnp.concatenate([pick(far, side)] + [whole(c) for c in middle] + [pick(chip, side)], axis=0)

    return order(core, keep), order(1 - core, give)


def ring_reduce(kept):
    chips = lax.axis_size("chip")
    core = lax.axis_index("core")
    rows = kept.shape[0] // chips
    moving = ring_step(kept[:rows])
    moving = jnp.concatenate(
        [jnp.where(core == 0, moving, 0), jnp.where(core == 0, 0, moving)], axis=0
    )
    at = rows
    for _ in range(chips // 2 - 1):
        moving = ring_step(plus(kept[at : at + 2 * rows], moving).astype(jnp.bfloat16))
        at += 2 * rows
    mine, theirs = by_core(core, moving[:rows], moving[rows:])
    return plus(kept[at:], mine) + swap_cores(theirs).astype(jnp.float32)


def body(
    hidden_in,
    queries,
    latent_cache,
    new_latent,
    cache_lengths,
    value_up,
    out_proj,
    norm_gain,
    router,
    expert_ids,
    w_gate_up,
    w_down,
):
    rows = hidden_in.shape[0]
    width = hidden_in.shape[1]
    chips = lax.axis_size("chip")
    cores = lax.axis_size("core")
    groups = lax.axis_size(GROUP)
    core = lax.axis_index("core")
    chip = lax.axis_index("chip")
    group = lax.axis_index(GROUP)
    place = chip * cores + core
    chip_cols = width // chips
    own_cols = chip_cols // cores
    expert_count = router.shape[1]
    hidden_share = w_down.shape[1]
    share = rows // CHUNKS
    total = chips * cores * share
    order = ring_order()

    outgoing = hidden_in.reshape(rows, chips * cores, own_cols).transpose(1, 0, 2)
    hidden_cols = lax.all_to_all(
        outgoing, ("chip", "core"), split_axis=0, concat_axis=0, tiled=True
    )

    all_ids = jnp.zeros((TOP, chips * cores * rows), jnp.int32)
    all_ids = lax.dynamic_update_slice(all_ids, expert_ids.T, (0, place * rows))
    all_ids = all_ids + swap_cores(all_ids)
    step = 1
    while step < chips:
        all_ids = all_ids + lax.ppermute(all_ids, "chip", [(i, i ^ step) for i in range(chips)])
        step *= 2
    grid = lax.broadcasted_iota(jnp.int32, (1, expert_count), 1)
    chosen = jnp.any(all_ids[:, :, None] == grid[None], axis=0).astype(jnp.float32)
    chosen = chosen.reshape(chips * cores, CHUNKS, share, expert_count).transpose(1, 0, 2, 3)
    chosen = chosen.reshape(CHUNKS, total, expert_count)
    is_mine = (grid == place).astype(jnp.float32)

    raw = w_gate_up[0]
    gate_up, gains, routers = [], [], []
    for at in order:
        block = lax.dynamic_slice_in_dim(raw, at * chip_cols, chip_cols, 0)
        gate_up.append(block.reshape(chip_cols, 2 * hidden_share))
        gains.append(lax.dynamic_slice_in_dim(norm_gain, at * chip_cols, chip_cols, 0))
        routers.append(lax.dynamic_slice_in_dim(router, at * chip_cols, chip_cols, 0))

    outs = []
    for h in range(CHUNKS):
        mine = slice(h * share, (h + 1) * share)
        head_out = attend(
            queries[mine], latent_cache[mine], new_latent[mine], cache_lengths[mine], value_up
        )
        if h == 0:
            head_out, hidden_cols, all_ids = lax.optimization_barrier(
                (head_out, hidden_cols, all_ids)
            )
        depth = head_out.shape[1]
        low, high = by_core(core, head_out, swap_cores(head_out))
        pieces = ring_gather(jnp.concatenate([low, high], axis=0), 1)
        gathered = jnp.zeros((chips, cores * share, depth), jnp.bfloat16)
        for at, piece in zip(order, pieces):
            gathered = lax.dynamic_update_slice_in_dim(gathered, piece[None], at, 0)
        if h == 0:
            gathered, gate_up = lax.optimization_barrier((gathered, gate_up))
        part = jnp.dot(
            gathered.reshape(total, depth), out_proj, preferred_element_type=jnp.float32
        )
        if groups == 2:
            attention = part + lax.ppermute(part.astype(jnp.bfloat16), "sec", SWAP)
        else:
            attention = lax.psum(part, GROUP)
        hidden_part = hidden_cols[:, mine].reshape(total, own_cols)
        residual = (hidden_part.astype(jnp.float32) + attention).astype(jnp.bfloat16)
        low, high = by_core(core, residual, swap_cores(residual))
        pieces = ring_gather(jnp.concatenate([low, high], axis=1), 0)

        squares = jnp.zeros((total, 1), jnp.float32)
        logits = jnp.zeros((total, expert_count), jnp.float32)
        both = jnp.zeros((total, 2 * hidden_share), jnp.float32)
        own = []
        for piece, gain, rout, weight in zip(pieces, gains, routers, gate_up):
            block = piece.astype(jnp.float32)
            squares = squares + jnp.sum(block * block, axis=1, keepdims=True)
            scaled = (block * gain).astype(jnp.bfloat16)
            logits = logits + jnp.dot(scaled, rout, preferred_element_type=jnp.float32)
            both = both + jnp.dot(scaled, weight, preferred_element_type=jnp.float32)
            own.append(lax.dynamic_slice_in_dim(piece, place * share, share, 0))
        norm = lax.rsqrt(squares / width + norm_epsilon)
        affinity = jax.nn.sigmoid(logits * norm) * chosen[h]
        weight = jnp.sum(affinity * is_mine, axis=1, keepdims=True)
        weight = route_scale * weight / jnp.sum(affinity, axis=1, keepdims=True)
        both = both * norm
        active = jax.nn.silu(both[:, :hidden_share]) * both[:, hidden_share:]
        active = active.astype(jnp.bfloat16)

        keep_rows, give_rows = reduce_rows(active.reshape(chips, cores, share, hidden_share))
        keep_weight, give_weight = reduce_rows(weight.reshape(chips, cores, share, 1))
        give = jnp.dot(give_rows, w_down[0], preferred_element_type=jnp.float32) * give_weight
        got = swap_cores(give.astype(jnp.bfloat16))
        keep = jnp.dot(keep_rows, w_down[0], preferred_element_type=jnp.float32) * keep_weight
        mixture = ring_reduce(plus(keep, got).astype(jnp.bfloat16))
        mixture = mixture.reshape(share, groups, width // groups)
        if groups == 2:
            other = lax.dynamic_index_in_dim(mixture, 1 - group, 1, keepdims=False)
            other = lax.ppermute(other.astype(jnp.bfloat16), "sec", SWAP)
            mixture = plus(lax.dynamic_index_in_dim(mixture, group, 1, keepdims=False), other)
        else:
            mixture = lax.psum_scatter(mixture, GROUP, scatter_dimension=1, tiled=False)

        first = group * (chips // groups)
        blocks = jnp.stack(own, axis=0)
        slots = jnp.stack(order)
        columns = []
        for c in range(chips // groups):
            slot = jnp.argmax(slots == first + c)
            columns.append(lax.dynamic_index_in_dim(blocks, slot, 0, keepdims=False))
        outs.append(plus(jnp.concatenate(columns, axis=1), mixture).astype(jnp.bfloat16))
    return jnp.concatenate(outs, axis=0)


def solution(mesh):
    sec, batch, head = mesh.shape["sec"], mesh.shape["batch"], mesh.shape["head"]
    devices = mesh.devices.reshape(sec, batch // 2, 2, head)
    split = Mesh(devices, ("sec", "chip", "core", "head"))
    tokens = ("chip", "core")
    in_specs = (
        P(tokens, None),
        P(tokens, GROUP, None),
        P(tokens, None, None),
        P(tokens, None),
        P(tokens),
        P(GROUP, None, None),
        P(GROUP, tokens),
        P(),
        P(),
        P(tokens, None),
        P(tokens, None, None, GROUP),
        P(tokens, GROUP, None),
    )
    out_specs = P(tokens, GROUP)
    return jax.shard_map(body, mesh=split, in_specs=in_specs, out_specs=out_specs, check_vma=False)
```

```python
import functools

import jax
import jax.numpy as jnp
from jax import lax
from jax.experimental import pallas as pl
from jax.experimental.pallas import tpu as pltpu
from jax.sharding import Mesh, PartitionSpec as P

QKD = 192
TOP = 8

norm_epsilon = 1e-06
route_scale = 2.5

GROUP = ("sec", "head")
SWAP = [(0, 1), (1, 0)]
CHUNKS = 2
NT = (((1,), (1,)), ((), ()))
ANY = pl.BlockSpec(memory_space=pl.ANY)
IN_VMEM = pl.BlockSpec(memory_space=pltpu.VMEM)
IN_SMEM = pl.BlockSpec(memory_space=pltpu.SMEM)


def attend(queries, latent_cache, new_latent, cache_lengths, value_up):
    row_count = queries.shape[0]
    latent_width = value_up.shape[1]
    cache_depth = latent_cache.shape[1]
    score_scale = QKD ** (-0.5)
    scores = (
        jnp.einsum("thk,tjk->thj", queries, latent_cache, preferred_element_type=jnp.float32)
        * score_scale
    )
    own_score = (
        jnp.einsum("thk,tk->th", queries, new_latent, preferred_element_type=jnp.float32)
        * score_scale
    )
    positions = lax.broadcasted_iota(jnp.int32, (1, 1, cache_depth), 2)
    in_cache = positions < cache_lengths[:, None, None]
    scores = jnp.where(in_cache, scores, -jnp.inf)
    top_score = jnp.maximum(jnp.max(scores, axis=2), own_score)
    cache_exp = jnp.exp(scores - top_score[:, :, None])
    own_exp = jnp.exp(own_score - top_score)
    softmax_sum = jnp.sum(cache_exp, axis=2) + own_exp
    cache_weights = (cache_exp / softmax_sum[:, :, None]).astype(jnp.bfloat16)
    own_weights = (own_exp / softmax_sum).astype(jnp.bfloat16)
    latent_out = jnp.einsum(
        "thj,tjc->thc",
        cache_weights,
        latent_cache[:, :, :latent_width],
        preferred_element_type=jnp.float32,
    )
    latent_out = latent_out + own_weights.astype(jnp.float32)[:, :, None] * new_latent[
        :, None, :latent_width
    ].astype(jnp.float32)
    latent_out = latent_out.astype(jnp.bfloat16)
    head_out = jnp.einsum(
        "thc,hcd->thd", latent_out, value_up, preferred_element_type=jnp.float32
    ).astype(jnp.bfloat16)
    return head_out.reshape(row_count, -1)


def place_of(chip, chips):
    return jnp.where(chip % 2 == 0, chip // 2, chips - 1 - chip // 2)


def chip_at(place, chips):
    place = place % chips
    return jnp.where(place < chips // 2, 2 * place, 2 * (chips - 1 - place) + 1)


def ring_step(block):
    chips = lax.axis_size("chip")
    ring = list(range(0, chips, 2)) + list(range(chips - 1, 0, -2))
    pairs = []
    for i in range(chips):
        here, there = ring[i], ring[(i + 1) % chips]
        pairs += [(2 * here, 2 * there), (2 * there + 1, 2 * here + 1)]
    return lax.ppermute(block, ("chip", "core"), pairs)


def swap_cores(block):
    return lax.ppermute(block, "core", SWAP)


def by_core(core, first, second):
    return jnp.where(core == 0, first, second), jnp.where(core == 0, second, first)


def ring_gather(block, axis, between=None):
    chips = lax.axis_size("chip")
    core = lax.axis_index("core")
    half = block.shape[axis] // 2
    pieces, moving = [block], block
    for i in range(chips // 2 - 1):
        moving = ring_step(moving)
        if i:
            moving, pieces[-1] = lax.optimization_barrier((moving, pieces[-1]))
        pieces += [moving, swap_cores(moving)]
        if between is not None:
            moving = between(i, moving)
    part = ring_step(lax.dynamic_slice_in_dim(moving, core * half, half, axis))
    low, high = by_core(core, part, swap_cores(part))
    return pieces + [low, high]


def ring_order():
    chips = lax.axis_size("chip")
    place = place_of(lax.axis_index("chip"), chips)
    sign = 2 * lax.axis_index("core") - 1
    places = [place]
    for d in range(1, chips // 2):
        places += [place + sign * d, place - sign * d]
    places.append(place + chips // 2)
    return [chip_at(p, chips) for p in places]


def plus(a, b):
    return a.astype(jnp.float32) + b.astype(jnp.float32)


def reduce_rows():
    chips = lax.axis_size("chip")
    core = lax.axis_index("core")
    chip = lax.axis_index("chip")
    place = place_of(chip, chips)
    far = 2 * chip_at(place + chips // 2, chips)

    def way(side, sign):
        blocks = [far + side]
        for d in range(chips // 2 - 1, 0, -1):
            at = 2 * chip_at(place + sign * d, chips)
            blocks += [at, at + 1]
        return blocks + [2 * chip + side]

    sign = 1 - 2 * core
    return way(core, sign) + way(1 - core, -sign)


def ring_reduce(keep, got):
    chips = lax.axis_size("chip")
    core = lax.axis_index("core")
    rows = keep.shape[0] // chips
    moving = ring_step(plus(keep[:rows], got[:rows]).astype(jnp.bfloat16))
    moving = jnp.concatenate(
        [jnp.where(core == 0, moving, 0), jnp.where(core == 0, 0, moving)], axis=0
    )
    at = rows
    for _ in range(chips // 2 - 1):
        block = plus(keep[at : at + 2 * rows], got[at : at + 2 * rows])
        moving = ring_step(plus(block, moving).astype(jnp.bfloat16))
        at += 2 * rows
    mine, theirs = by_core(core, moving[:rows], moving[rows:])
    theirs = swap_cores(theirs)
    return plus(plus(keep[at:], got[at:]), plus(mine, theirs))


def stream(count, copy):
    for k in range(min(2, count)):
        copy(k).start()

    def ready(k):
        copy(k).wait()

        @pl.when(k + 2 < count)
        def _():
            copy(k + 2).start()

    return ready


def project_kernel(steps, order, weight, *refs):
    pieces = refs[:-5]
    out, rows, held, piece_sems, weight_sems = refs[-5:]
    depth = held.shape[2]
    last = len(pieces) - 2
    half = pieces[-1].shape[1]
    copies = []
    for i, piece in enumerate(pieces):
        target = rows.at[order[min(i, last)]]
        if i >= last:
            target = target.at[:, pl.ds((i - last) * half, half)]
        copies.append(pltpu.make_async_copy(piece, target, piece_sems.at[i]))
    for copy in copies:
        copy.start()

    def weight_copy(k):
        columns = pl.ds(pl.multiple_of(k * depth, depth), depth)
        slot = k % 3
        return pltpu.make_async_copy(weight.at[:, columns], held.at[slot], weight_sems.at[slot])

    ready = stream(steps, weight_copy)
    for copy in copies:
        copy.wait()
    out[...] = jnp.zeros_like(out)

    @pl.loop(0, steps)
    def _(k):
        ready(k)
        columns = pl.ds(pl.multiple_of(k * depth, depth), depth)
        block = rows[:, :, columns].reshape(out.shape[0], depth)
        out[...] += lax.dot_general(block, held[k % 3], NT, preferred_element_type=jnp.float32)


def project(order, pieces, weight):
    chips = len(pieces) - 1
    rows, depth = pieces[0].shape
    columns = weight.shape[0]
    steps = 8
    total = chips * rows
    return pl.pallas_call(
        functools.partial(project_kernel, steps),
        out_shape=jax.ShapeDtypeStruct((total, columns), jnp.float32),
        in_specs=[IN_SMEM] + [ANY] * (1 + len(pieces)),
        out_specs=IN_VMEM,
        scratch_shapes=[
            pltpu.VMEM((chips, rows, depth), jnp.bfloat16),
            pltpu.VMEM((3, columns, depth // steps), jnp.bfloat16),
            pltpu.SemaphoreType.DMA((len(pieces),)),
            pltpu.SemaphoreType.DMA((3,)),
        ],
        compiler_params=pltpu.CompilerParams(vmem_limit_bytes=16 * 1024 * 1024),
        cost_estimate=pl.CostEstimate(
            flops=2 * total * depth * columns,
            bytes_accessed=2 * depth * (total + columns) + 4 * total * columns,
            transcendentals=0,
        ),
    )(order, weight, *pieces)


def gate_kernel(parts, meta, gain, router, chosen, *refs):
    gate_up, pieces = refs[:parts], refs[parts:-10]
    out, own, held, weight, total, logits, squares, active, piece_sems, weight_sems = refs[-10:]
    chips, rows, depth = held.shape
    hidden = out.shape[1]
    share = own.shape[1]
    place = meta[chips]
    last = len(pieces) - 2
    half = pieces[-1].shape[0]
    per = chips // parts
    for i, piece in enumerate(pieces):
        slot = min(i, last)
        target = held.at[slot]
        if i >= last:
            target = target.at[pl.ds((i - last) * half, half), :]
        pltpu.make_async_copy(piece, target, piece_sems.at[slot]).start()

    def weight_slot(k):
        slot = k % 3
        return pltpu.make_async_copy(weight.at[slot], weight.at[slot], weight_sems.at[slot])

    def weight_start(k):
        at = meta[k]
        slot = k % 3
        for p in range(parts):

            @pl.when(at // per == p)
            def _():
                part = pl.ds(pl.multiple_of(at % per * depth, 16), depth)
                pltpu.make_async_copy(
                    gate_up[p].at[part, :], weight.at[slot], weight_sems.at[slot]
                ).start()

    weight_start(0)
    weight_start(1)
    total[...] = jnp.zeros_like(total)
    logits[...] = jnp.zeros_like(logits)
    squares[...] = jnp.zeros_like(squares)

    @pl.loop(0, chips)
    def _(k):
        pltpu.make_async_copy(held.at[k], held.at[k], piece_sems.at[k]).wait()
        weight_slot(k).wait()

        @pl.when(k + 2 < chips)
        def _():
            weight_start(k + 2)

        at = meta[k]
        block = held[k].astype(jnp.float32)
        if depth % 128 == 0:
            for j in range(0, depth, 128):
                squares[...] += block[:, j : j + 128] * block[:, j : j + 128]
        else:
            squares[...] += jnp.sum(block * block, axis=1, keepdims=True) * (1.0 / 128)
        scaled = (block * gain[at]).astype(jnp.bfloat16)
        logits[...] += lax.dot_general(scaled, router[at], NT, preferred_element_type=jnp.float32)
        total[...] += jnp.dot(scaled, weight[k % 3], preferred_element_type=jnp.float32)
        own[at] = held[k, pl.ds(pl.multiple_of(place * share, share), share), :]

    width = chips * depth
    norm = lax.rsqrt(jnp.sum(squares[...], axis=1, keepdims=True) * (1.0 / width) + norm_epsilon)
    affinity = jax.nn.sigmoid(logits[...] * norm) * chosen[...]
    mine = lax.broadcasted_iota(jnp.int32, affinity.shape, 1) == place
    share_of = jnp.sum(jnp.where(mine, affinity, 0.0), axis=1, keepdims=True)
    scale = route_scale * share_of / jnp.sum(affinity, axis=1, keepdims=True)
    gate = total[:, :hidden] * norm
    up = total[:, hidden:] * (norm * scale)
    active[...] = (gate * jax.nn.sigmoid(gate) * up).astype(jnp.bfloat16)
    for i in range(rows // share):
        at = pl.ds(pl.multiple_of(meta[chips + 1 + i] * share, share), share)
        out[i * share : (i + 1) * share, :] = active[at, :]


def gate(meta, pieces, gate_up, gain, router, chosen):
    chips = len(pieces) - 1
    rows, depth = pieces[0].shape
    wide = gate_up[0].shape[1]
    names = chosen.shape[1]
    share = rows // (2 * chips)
    return pl.pallas_call(
        functools.partial(gate_kernel, len(gate_up)),
        out_shape=(
            jax.ShapeDtypeStruct((rows, wide // 2), jnp.bfloat16),
            jax.ShapeDtypeStruct((chips, share, depth), jnp.bfloat16),
        ),
        in_specs=[IN_SMEM] + [IN_VMEM] * 3 + [ANY] * (len(gate_up) + len(pieces)),
        out_specs=(IN_VMEM, IN_VMEM),
        scratch_shapes=[
            pltpu.VMEM((chips, rows, depth), jnp.bfloat16),
            pltpu.VMEM((3, depth, wide), jnp.bfloat16),
            pltpu.VMEM((rows, wide), jnp.float32),
            pltpu.VMEM((rows, names), jnp.float32),
            pltpu.VMEM((rows, 128), jnp.float32),
            pltpu.VMEM((rows, wide // 2), jnp.bfloat16),
            pltpu.SemaphoreType.DMA((chips,)),
            pltpu.SemaphoreType.DMA((3,)),
        ],
        compiler_params=pltpu.CompilerParams(vmem_limit_bytes=24 * 1024 * 1024),
        cost_estimate=pl.CostEstimate(
            flops=2 * rows * chips * depth * wide,
            bytes_accessed=2 * chips * depth * (wide + rows),
            transcendentals=rows * wide,
        ),
    )(meta, gain, router, chosen, *gate_up, *pieces)


def down_kernel(steps, active, weight, keep, give, held, sems):
    rows = keep.shape[0]
    span = held.shape[2]

    def copy(k):
        columns = pl.ds(pl.multiple_of(k * span, span), span)
        return pltpu.make_async_copy(weight.at[:, columns], held.at[k % 3], sems.at[k % 3])

    ready = stream(steps, copy)

    @pl.loop(0, steps)
    def _(k):
        ready(k)
        columns = pl.ds(pl.multiple_of(k * span, span), span)
        result = jnp.dot(active[...], held[k % 3], preferred_element_type=jnp.float32)
        keep[:, columns] = result[:rows].astype(jnp.bfloat16)
        give[:, columns] = result[rows:].astype(jnp.bfloat16)


def down(active, weight):
    rows, hidden = active.shape
    width = weight.shape[1]
    steps = max(1, width // 1024)
    shape = jax.ShapeDtypeStruct((rows // 2, width), jnp.bfloat16)
    return pl.pallas_call(
        functools.partial(down_kernel, steps),
        out_shape=(shape, shape),
        in_specs=[IN_VMEM, ANY],
        out_specs=(IN_VMEM, IN_VMEM),
        scratch_shapes=[
            pltpu.VMEM((3, hidden, width // steps), jnp.bfloat16),
            pltpu.SemaphoreType.DMA((3,)),
        ],
        compiler_params=pltpu.CompilerParams(vmem_limit_bytes=16 * 1024 * 1024),
        cost_estimate=pl.CostEstimate(
            flops=2 * rows * hidden * width,
            bytes_accessed=2 * width * (hidden + rows),
            transcendentals=0,
        ),
    )(active, weight)


def body(
    hidden_in,
    queries,
    latent_cache,
    new_latent,
    cache_lengths,
    value_up,
    out_proj,
    norm_gain,
    router,
    expert_ids,
    w_gate_up,
    w_down,
):
    rows = hidden_in.shape[0]
    width = hidden_in.shape[1]
    chips = lax.axis_size("chip")
    cores = lax.axis_size("core")
    groups = lax.axis_size(GROUP)
    core = lax.axis_index("core")
    chip = lax.axis_index("chip")
    group = lax.axis_index(GROUP)
    place = chip * cores + core
    chip_cols = width // chips
    own_cols = chip_cols // cores
    expert_count = router.shape[1]
    share = rows // CHUNKS
    total = chips * cores * share
    order = ring_order()

    outgoing = hidden_in.reshape(rows, chips * cores, own_cols).transpose(1, 0, 2)
    names = jnp.broadcast_to(expert_ids.astype(jnp.bfloat16)[None], (chips * cores, rows, TOP))
    arrived = lax.all_to_all(
        jnp.concatenate([outgoing, names], axis=2),
        ("chip", "core"),
        split_axis=0,
        concat_axis=0,
        tiled=True,
    )

    span = width // (2 * CHUNKS)
    gate_up = [None] * (2 * CHUNKS)

    def relayout(h):
        def between(i, moving):
            if i in (1, 2):
                p = (i - 1) * CHUNKS + h
                moving, gate_up[p] = lax.optimization_barrier((moving, gate_up[p]))
            if i in (0, 1):
                p = i * CHUNKS + h
                moving, raw = lax.optimization_barrier((moving, w_gate_up))
                gate_up[p] = raw[0, p * span : (p + 1) * span].reshape(span, -1)
            return moving

        return between

    gain = norm_gain.reshape(chips, 1, chip_cols)
    router_rows = router.T.reshape(expert_count, chips, chip_cols).transpose(1, 0, 2)
    meta = jnp.stack(order + [place] + reduce_rows()).astype(jnp.int32)

    gathers = []
    for h in range(CHUNKS):
        mine = slice(h * share, (h + 1) * share)
        head_out = attend(
            queries[mine], latent_cache[mine], new_latent[mine], cache_lengths[mine], value_up
        )
        if h == 0:
            head_out, arrived = lax.optimization_barrier((head_out, arrived))
        low, high = by_core(core, head_out, swap_cores(head_out))
        block = jnp.concatenate([low, high], axis=0)
        pieces = ring_gather(block, 1, relayout(h))
        part = project(meta, pieces, out_proj.T)
        if groups == 2:
            attention = part + lax.ppermute(part.astype(jnp.bfloat16), "sec", SWAP)
        else:
            attention = lax.psum(part, GROUP)
        hidden_part = arrived[:, mine, :own_cols].reshape(total, own_cols)
        residual = (hidden_part.astype(jnp.float32) + attention).astype(jnp.bfloat16)
        low, high = by_core(core, residual, swap_cores(residual))
        gathers.append(ring_gather(jnp.concatenate([low, high], axis=1), 0))

    outs = []
    for h in range(CHUNKS):
        mine = slice(h * share, (h + 1) * share)
        pieces = gathers[h]

        ids = arrived[:, mine, own_cols:].reshape(total, TOP, 1).astype(jnp.int32)
        grid = lax.broadcasted_iota(jnp.int32, (1, 1, expert_count), 2)
        chosen = jnp.any(ids == grid, axis=1).astype(jnp.float32)
        active, own = gate(meta, pieces, gate_up, gain, router_rows, chosen)
        keep, give = down(active, w_down[0])
        mixture = ring_reduce(keep, swap_cores(give))
        mixture = mixture.reshape(share, groups, width // groups)
        if groups == 2:
            other = lax.dynamic_index_in_dim(mixture, 1 - group, 1, keepdims=False)
            other = lax.ppermute(other.astype(jnp.bfloat16), "sec", SWAP)
            mixture = plus(lax.dynamic_index_in_dim(mixture, group, 1, keepdims=False), other)
        else:
            mixture = lax.psum_scatter(mixture, GROUP, scatter_dimension=1, tiled=False)
        own = own.reshape(groups, chips // groups, share, chip_cols)
        own = lax.dynamic_index_in_dim(own, group, 0, keepdims=False)
        own = own.transpose(1, 0, 2).reshape(share, width // groups)
        outs.append(plus(own, mixture).astype(jnp.bfloat16))
    return jnp.concatenate(outs, axis=0)


def solution(mesh):
    sec, batch, head = mesh.shape["sec"], mesh.shape["batch"], mesh.shape["head"]
    devices = mesh.devices.reshape(sec, batch // 2, 2, head)
    split = Mesh(devices, ("sec", "chip", "core", "head"))
    tokens = ("chip", "core")
    in_specs = (
        P(tokens, None),
        P(tokens, GROUP, None),
        P(tokens, None, None),
        P(tokens, None),
        P(tokens),
        P(GROUP, None, None),
        P(GROUP, tokens),
        P(),
        P(),
        P(tokens, None),
        P(tokens, None, None, GROUP),
        P(tokens, GROUP, None),
    )
    out_specs = P(tokens, GROUP)
    return jax.shard_map(body, mesh=split, in_specs=in_specs, out_specs=out_specs, check_vma=False)
```

```python
import functools

import jax
import jax.numpy as jnp
from jax import lax
from jax.experimental import pallas as pl
from jax.experimental.pallas import tpu as pltpu
from jax.sharding import Mesh, PartitionSpec as P

QKD = 192
TOP = 8

norm_epsilon = 1e-06
route_scale = 2.5

GROUP = ("sec", "head")
SWAP = [(0, 1), (1, 0)]
STREAMS = 2
NT = (((1,), (1,)), ((), ()))
ANY = pl.BlockSpec(memory_space=pl.ANY)
IN_HBM = pl.BlockSpec(memory_space=pltpu.HBM)
IN_VMEM = pl.BlockSpec(memory_space=pltpu.VMEM)
IN_SMEM = pl.BlockSpec(memory_space=pltpu.SMEM)


def attend(queries, latent_cache, new_latent, cache_lengths, value_up):
    row_count = queries.shape[0]
    latent_width = value_up.shape[1]
    cache_depth = latent_cache.shape[1]
    score_scale = QKD ** (-0.5)
    scores = (
        jnp.einsum("thk,tjk->thj", queries, latent_cache, preferred_element_type=jnp.float32)
        * score_scale
    )
    own_score = (
        jnp.einsum("thk,tk->th", queries, new_latent, preferred_element_type=jnp.float32)
        * score_scale
    )
    positions = lax.broadcasted_iota(jnp.int32, (1, 1, cache_depth), 2)
    in_cache = positions < cache_lengths[:, None, None]
    scores = jnp.where(in_cache, scores, -jnp.inf)
    top_score = jnp.maximum(jnp.max(scores, axis=2), own_score)
    cache_exp = jnp.exp(scores - top_score[:, :, None])
    own_exp = jnp.exp(own_score - top_score)
    softmax_sum = jnp.sum(cache_exp, axis=2) + own_exp
    cache_weights = (cache_exp / softmax_sum[:, :, None]).astype(jnp.bfloat16)
    own_weights = (own_exp / softmax_sum).astype(jnp.bfloat16)
    latent_out = jnp.einsum(
        "thj,tjc->thc",
        cache_weights,
        latent_cache[:, :, :latent_width],
        preferred_element_type=jnp.float32,
    )
    latent_out = latent_out + own_weights.astype(jnp.float32)[:, :, None] * new_latent[
        :, None, :latent_width
    ].astype(jnp.float32)
    latent_out = latent_out.astype(jnp.bfloat16)
    head_out = jnp.einsum(
        "thc,hcd->thd", latent_out, value_up, preferred_element_type=jnp.float32
    ).astype(jnp.bfloat16)
    return head_out.reshape(row_count, -1)


def place_of(chip, chips):
    return jnp.where(chip % 2 == 0, chip // 2, chips - 1 - chip // 2)


def chip_at(place, chips):
    place = place % chips
    return jnp.where(place < chips // 2, 2 * place, 2 * (chips - 1 - place) + 1)


def ring_step(block):
    chips = lax.axis_size("chip")
    ring = list(range(0, chips, 2)) + list(range(chips - 1, 0, -2))
    pairs = []
    for i in range(chips):
        here, there = ring[i], ring[(i + 1) % chips]
        pairs += [(2 * here, 2 * there), (2 * there + 1, 2 * here + 1)]
    return lax.ppermute(block, ("chip", "core"), pairs)


def swap_cores(block):
    return lax.ppermute(block, "core", SWAP)


def by_core(core, first, second):
    return jnp.where(core == 0, first, second), jnp.where(core == 0, second, first)


def ring_gather(blocks, between=None):
    chips = lax.axis_size("chip")
    core = lax.axis_index("core")
    pieces, moving = [[block] for block in blocks], list(blocks)
    for i in range(chips // 2 - 1):
        for s in range(STREAMS):
            moving[s] = ring_step(moving[s])
            if i:
                moving[s], pieces[s][-1] = lax.optimization_barrier((moving[s], pieces[s][-1]))
            pieces[s] += [moving[s], swap_cores(moving[s])]
            if between is not None:
                moving[s] = between(s, i, moving[s])
    last = ring_step(jnp.where(core == 0, moving[0], moving[1]))
    for s, piece in enumerate(by_core(core, last, swap_cores(last))):
        pieces[s].append(piece)
    return pieces


def ring_order():
    chips = lax.axis_size("chip")
    place = place_of(lax.axis_index("chip"), chips)
    sign = 2 * lax.axis_index("core") - 1
    places = [place]
    for d in range(1, chips // 2):
        places += [place + sign * d, place - sign * d]
    places.append(place + chips // 2)
    return [chip_at(p, chips) for p in places]


def plus(a, b):
    return a.astype(jnp.float32) + b.astype(jnp.float32)


def reduce_rows():
    chips = lax.axis_size("chip")
    core = lax.axis_index("core")
    chip = lax.axis_index("chip")
    place = place_of(chip, chips)
    far = 2 * chip_at(place + chips // 2, chips)

    def way(side, sign):
        blocks = []
        for d in range(chips // 2 - 1, 0, -1):
            at = 2 * chip_at(place + sign * d, chips)
            blocks += [at, at + 1]
        return [far + side] + blocks[:2], blocks[2:] + [2 * chip + side]

    sign = 1 - 2 * core
    keep, give = way(core, sign), way(1 - core, -sign)
    return keep[0] + give[0], keep[1] + give[1]


def ring_reduce(keep, got):
    core = lax.axis_index("core")
    rows = keep[0].shape[0] // 3

    def cut(at, size, s):
        def one(parts):
            part, start = (parts[0], at) if at < 3 * rows else (parts[1], at - 3 * rows)
            half = part.shape[1] // STREAMS
            return part[start : start + size, s * half : (s + 1) * half]

        return plus(one(keep), one(got))

    moving = [ring_step(cut(0, rows, s).astype(jnp.bfloat16)) for s in range(STREAMS)]
    moving = [
        jnp.concatenate([jnp.where(core == 0, m, 0), jnp.where(core == 0, 0, m)], axis=0)
        for m in moving
    ]
    at = rows
    total = 3 * rows + keep[1].shape[0]
    while at < total - rows:
        for s in range(STREAMS):
            moving[s] = ring_step(plus(cut(at, 2 * rows, s), moving[s]).astype(jnp.bfloat16))
        at += 2 * rows
    sums = []
    for s in range(STREAMS):
        mine, theirs = by_core(core, moving[s][:rows], moving[s][rows:])
        sums.append(plus(cut(at, rows, s), plus(mine, swap_cores(theirs))))
    return sums


def stream(count, copy):
    for k in range(min(2, count)):
        copy(k).start()

    def ready(k):
        copy(k).wait()

        @pl.when(k + 2 < count)
        def _():
            copy(k + 2).start()

    return ready


def project_kernel(steps, count, weight, *refs):
    pieces, (out, rows, held, piece_sems, weight_sems) = refs[:-5], refs[-5:]
    depth = held.shape[2]
    block, half = pieces[0].shape
    copies = []
    for i, piece in enumerate(pieces):
        at, s = i % count, i // count
        target = rows.at[pl.ds(at * block, block), pl.ds(s * half, half)]
        copies.append(pltpu.make_async_copy(piece, target, piece_sems.at[i]))
    for copy in copies:
        copy.start()

    def weight_copy(k):
        columns = pl.ds(pl.multiple_of(k * depth, depth), depth)
        slot = k % 3
        return pltpu.make_async_copy(weight.at[:, columns], held.at[slot], weight_sems.at[slot])

    ready = stream(steps, weight_copy)
    for copy in copies:
        copy.wait()
    out[...] = jnp.zeros_like(out)

    @pl.loop(0, steps)
    def _(k):
        ready(k)
        columns = pl.ds(pl.multiple_of(k * depth, depth), depth)
        out[...] += lax.dot_general(
            rows[:, columns], held[k % 3], NT, preferred_element_type=jnp.float32
        )


def project(pieces, weight):
    count = len(pieces[0])
    rows, half = pieces[0][0].shape
    depth = STREAMS * half
    columns = weight.shape[0]
    steps = 8
    total = count * rows
    return pl.pallas_call(
        functools.partial(project_kernel, steps, count),
        out_shape=jax.ShapeDtypeStruct((total, columns), jnp.float32),
        in_specs=[ANY] * (1 + STREAMS * count),
        out_specs=IN_VMEM,
        scratch_shapes=[
            pltpu.VMEM((total, depth), jnp.bfloat16),
            pltpu.VMEM((3, columns, depth // steps), jnp.bfloat16),
            pltpu.SemaphoreType.DMA((STREAMS * count,)),
            pltpu.SemaphoreType.DMA((3,)),
        ],
        compiler_params=pltpu.CompilerParams(vmem_limit_bytes=20 * 1024 * 1024),
        cost_estimate=pl.CostEstimate(
            flops=2 * total * depth * columns,
            bytes_accessed=2 * depth * (total + columns) + 4 * total * columns,
            transcendentals=0,
        ),
    )(weight, *[piece for part in pieces for piece in part])


def finish_kernel(count, meta, arrived, *refs):
    parts, got, out = refs[:count], refs[count : 2 * count], refs[2 * count]
    chips, rows, columns = out.shape
    i = 0
    for part, other in zip(parts, got):
        for j in range(part.shape[0] // rows):
            at = meta[i]
            block = part[j * rows : (j + 1) * rows, :] + other[j * rows : (j + 1) * rows, :].astype(jnp.float32)
            hidden = arrived[at][:, :columns].astype(jnp.float32)
            out[at] = (hidden + block).astype(jnp.bfloat16)
            i += 1


def finish(meta, parts, got, arrived):
    columns = parts[0].shape[1]
    return pl.pallas_call(
        functools.partial(finish_kernel, len(parts)),
        out_shape=jax.ShapeDtypeStruct(arrived.shape[:2] + (columns,), jnp.bfloat16),
        in_specs=[IN_SMEM] + [IN_VMEM] * (1 + 2 * len(parts)),
        out_specs=IN_VMEM,
        compiler_params=pltpu.CompilerParams(vmem_limit_bytes=16 * 1024 * 1024),
    )(meta, arrived, *parts, *got)


def own_kernel(count, meta, *refs):
    pieces, (out, sems) = refs[:-2], refs[-2:]
    chips, share, _ = out.shape
    half = pieces[0].shape[0]
    place = meta[chips]
    for s in range(STREAMS):

        @pl.when(place * share // half == s)
        def _():
            at = pl.ds(pl.multiple_of(place * share - s * half, share), share)
            copies = [
                pltpu.make_async_copy(pieces[s * count + i].at[at, :], out.at[meta[i]], sems.at[i])
                for i in range(count)
            ]
            for copy in copies:
                copy.start()
            for copy in copies:
                copy.wait()


def own_residual(meta, pieces):
    chips = len(pieces[0])
    half, depth = pieces[0][0].shape
    share = half // chips
    return pl.pallas_call(
        functools.partial(own_kernel, chips),
        out_shape=jax.ShapeDtypeStruct((chips, share, depth), jnp.bfloat16),
        in_specs=[IN_SMEM] + [ANY] * (STREAMS * chips),
        out_specs=IN_VMEM,
        scratch_shapes=[pltpu.SemaphoreType.DMA((chips,))],
        compiler_params=pltpu.CompilerParams(vmem_limit_bytes=8 * 1024 * 1024),
    )(meta, *[piece for part in pieces for piece in part])


def gate_kernel(parts, first, count, chips, last, meta, gain, router, *refs):
    rest = list(refs)

    def take(n):
        head = rest[:n]
        del rest[:n]
        return head

    chosen = take(1)[0] if last else None
    before = take(3) if first else None
    gate_up, pieces = take(parts), take(STREAMS * count)
    outs = take(2 if last else 3)
    held, weight = take(2)
    if last:
        active, total, logits, squares = take(4)
    else:
        total, logits, squares = outs
    piece_sems, weight_sems = take(2)
    rows, depth = held.shape[1:]
    half = pieces[0].shape[0]
    per = chips // parts
    for i in range(count):
        for s in range(STREAMS):
            target = held.at[i, pl.ds(s * half, half), :]
            pltpu.make_async_copy(pieces[s * count + i], target, piece_sems.at[i]).start()

    def weight_start(k):
        at = meta[first + k]
        slot = k % 3
        for p in range(parts):

            @pl.when(at // per == p)
            def _():
                part = pl.ds(pl.multiple_of(at % per * depth, 16), depth)
                pltpu.make_async_copy(
                    gate_up[p].at[part, :], weight.at[slot], weight_sems.at[slot]
                ).start()

    for k in range(min(2, count)):
        weight_start(k)
    for i, ref in enumerate((total, logits, squares)):
        ref[...] = before[i][...] if first else jnp.zeros_like(ref)

    @pl.loop(0, count)
    def _(k):
        pltpu.make_async_copy(held.at[k], held.at[k], piece_sems.at[k]).wait()
        slot = k % 3
        pltpu.make_async_copy(weight.at[slot], weight.at[slot], weight_sems.at[slot]).wait()

        @pl.when(k + 2 < count)
        def _():
            weight_start(k + 2)

        at = meta[first + k]
        block = held[k].astype(jnp.float32)
        if depth % 128 == 0:
            for j in range(0, depth, 128):
                squares[...] += block[:, j : j + 128] * block[:, j : j + 128]
        else:
            squares[...] += jnp.sum(block * block, axis=1, keepdims=True) * (1.0 / 128)
        scaled = (block * gain[at]).astype(jnp.bfloat16)
        logits[...] += lax.dot_general(scaled, router[at], NT, preferred_element_type=jnp.float32)
        total[...] += jnp.dot(scaled, weight[slot], preferred_element_type=jnp.float32)

    if not last:
        return
    hidden = active.shape[1]
    place = meta[chips]
    width = chips * depth
    norm = lax.rsqrt(jnp.sum(squares[...], axis=1, keepdims=True) * (1.0 / width) + norm_epsilon)
    affinity = jax.nn.sigmoid(logits[...] * norm) * chosen[...]
    mine = lax.broadcasted_iota(jnp.int32, affinity.shape, 1) == place
    share_of = jnp.sum(jnp.where(mine, affinity, 0.0), axis=1, keepdims=True)
    scale = route_scale * share_of / jnp.sum(affinity, axis=1, keepdims=True)
    gate = total[:, :hidden] * norm
    up = total[:, hidden:] * (norm * scale)
    active[...] = (gate * jax.nn.sigmoid(gate) * up).astype(jnp.bfloat16)
    share = rows // (2 * chips)
    i = chips + 1
    for out in outs:
        for j in range(0, out.shape[0], share):
            at = pl.ds(pl.multiple_of(meta[i] * share, share), share)
            out[j : j + share, :] = active[at, :]
            i += 1


def gate(meta, first, pieces, gate_up, gain, router, before=None, chosen=None):
    chips = gain.shape[0]
    names = router.shape[1]
    count = len(pieces[0])
    half, depth = pieces[0][0].shape
    rows = STREAMS * half
    wide = gate_up[0].shape[1]
    last = chosen is not None
    share = rows // (2 * chips)
    sums = (
        jax.ShapeDtypeStruct((rows, wide), jnp.float32),
        jax.ShapeDtypeStruct((rows, names), jnp.float32),
        jax.ShapeDtypeStruct((rows, 128), jnp.float32),
    )
    ends = (
        jax.ShapeDtypeStruct((6 * share, wide // 2), jnp.bfloat16),
        jax.ShapeDtypeStruct((rows - 6 * share, wide // 2), jnp.bfloat16),
    )
    own = [chosen] * last + list(before or ())
    scratch = [
        pltpu.VMEM((count, rows, depth), jnp.bfloat16),
        pltpu.VMEM((3, depth, wide), jnp.bfloat16),
    ]
    if last:
        scratch += [pltpu.VMEM((rows, wide // 2), jnp.bfloat16)]
        scratch += [pltpu.VMEM(t.shape, t.dtype) for t in sums]
    scratch += [pltpu.SemaphoreType.DMA((count,)), pltpu.SemaphoreType.DMA((3,))]
    return pl.pallas_call(
        functools.partial(gate_kernel, len(gate_up), first, count, chips, last),
        out_shape=ends if last else sums,
        in_specs=[IN_SMEM] + [IN_VMEM] * (2 + len(own)) + [IN_HBM] * len(gate_up) + [ANY] * (STREAMS * count),
        out_specs=(IN_VMEM,) * (2 if last else 3),
        scratch_shapes=scratch,
        compiler_params=pltpu.CompilerParams(vmem_limit_bytes=28 * 1024 * 1024),
        cost_estimate=pl.CostEstimate(
            flops=2 * rows * count * depth * wide,
            bytes_accessed=2 * count * depth * (wide + rows),
            transcendentals=rows * wide if last else 0,
        ),
    )(meta, gain, router, *own, *gate_up, *[piece for part in pieces for piece in part])


def down_kernel(steps, active, weight, keep, give, held, sems):
    rows = keep.shape[0]
    span = held.shape[2]

    def copy(k):
        columns = pl.ds(pl.multiple_of(k * span, span), span)
        return pltpu.make_async_copy(weight.at[:, columns], held.at[k % 3], sems.at[k % 3])

    ready = stream(steps, copy)

    @pl.loop(0, steps)
    def _(k):
        ready(k)
        columns = pl.ds(pl.multiple_of(k * span, span), span)
        result = jnp.dot(active[...], held[k % 3], preferred_element_type=jnp.float32)
        keep[:, columns] = result[:rows].astype(jnp.bfloat16)
        give[:, columns] = result[rows:].astype(jnp.bfloat16)


def down(active, weight):
    rows, hidden = active.shape
    width = weight.shape[1]
    steps = max(1, width // 1024)
    shape = jax.ShapeDtypeStruct((rows // 2, width), jnp.bfloat16)
    return pl.pallas_call(
        functools.partial(down_kernel, steps),
        out_shape=(shape, shape),
        in_specs=[IN_VMEM, IN_HBM],
        out_specs=(IN_VMEM, IN_VMEM),
        scratch_shapes=[
            pltpu.VMEM((3, hidden, width // steps), jnp.bfloat16),
            pltpu.SemaphoreType.DMA((3,)),
        ],
        compiler_params=pltpu.CompilerParams(vmem_limit_bytes=20 * 1024 * 1024),
        cost_estimate=pl.CostEstimate(
            flops=2 * rows * hidden * width,
            bytes_accessed=2 * width * (hidden + rows),
            transcendentals=0,
        ),
    )(active, weight)


def body(
    hidden_in,
    queries,
    latent_cache,
    new_latent,
    cache_lengths,
    value_up,
    out_proj,
    norm_gain,
    router,
    expert_ids,
    w_gate_up,
    w_down,
):
    rows = hidden_in.shape[0]
    width = hidden_in.shape[1]
    chips = lax.axis_size("chip")
    cores = lax.axis_size("core")
    groups = lax.axis_size(GROUP)
    core = lax.axis_index("core")
    chip = lax.axis_index("chip")
    group = lax.axis_index(GROUP)
    place = chip * cores + core
    chip_cols = width // chips
    own_cols = chip_cols // cores
    expert_count = router.shape[1]
    total = chips * cores * rows
    order = ring_order()

    outgoing = hidden_in.reshape(rows, chips * cores, own_cols).transpose(1, 0, 2)
    names = jnp.broadcast_to(expert_ids.astype(jnp.bfloat16)[None], (chips * cores, rows, TOP))
    arrived = lax.all_to_all(
        jnp.concatenate([outgoing, names], axis=2),
        ("chip", "core"),
        split_axis=0,
        concat_axis=0,
        tiled=True,
    )

    span = width // (2 * STREAMS)
    gate_up = [None] * (2 * STREAMS)

    def relayout(s, i, moving):
        if i in (1, 2):
            p = (i - 1) * STREAMS + s
            moving, gate_up[p] = lax.optimization_barrier((moving, gate_up[p]))
        if i in (0, 1):
            p = i * STREAMS + s
            moving, raw = lax.optimization_barrier((moving, w_gate_up))
            gate_up[p] = raw[0, p * span : (p + 1) * span].reshape(span, -1)
        return moving

    gain = norm_gain.reshape(chips, 1, chip_cols)
    router_rows = router.T.reshape(expert_count, chips, chip_cols).transpose(1, 0, 2)
    first_rows, then_rows = reduce_rows()
    meta = jnp.stack(order + [place] + first_rows + then_rows).astype(jnp.int32)

    head_out = attend(queries, latent_cache, new_latent, cache_lengths, value_up)
    head_out, arrived = lax.optimization_barrier((head_out, arrived))
    low, high = by_core(core, head_out, swap_cores(head_out))
    block = jnp.concatenate([low, high], axis=0)
    half = block.shape[1] // STREAMS
    pieces = ring_gather([block[:, s * half : (s + 1) * half] for s in range(STREAMS)], relayout)
    parts, got = [], []
    for blocks in (slice(0, chips - 1), slice(chips - 1, chips)):
        part = project([piece[blocks] for piece in pieces], out_proj.T)
        if groups == 2:
            parts.append(part)
            got.append(lax.ppermute(part.astype(jnp.bfloat16), "sec", SWAP))
        else:
            parts.append(lax.psum(part, GROUP))
            got.append(jnp.zeros(part.shape, jnp.bfloat16))
    arrived = arrived.reshape(chips, cores * rows, own_cols + TOP)
    residual = finish(meta, parts, got, arrived).reshape(total, own_cols)
    low, high = by_core(core, residual, swap_cores(residual))
    block = jnp.concatenate([low, high], axis=1)
    half = total // STREAMS
    pieces = ring_gather([block[s * half : (s + 1) * half] for s in range(STREAMS)])

    ids = arrived[:, :, own_cols:].reshape(total, TOP, 1).astype(jnp.int32)
    grid = lax.broadcasted_iota(jnp.int32, (1, 1, expert_count), 2)
    chosen = jnp.any(ids == grid, axis=1).astype(jnp.float32)
    sums, at = None, 0
    for end in (chips - 3, chips - 1, chips):
        sums = gate(
            meta,
            at,
            [piece[at:end] for piece in pieces],
            gate_up,
            gain,
            router_rows,
            before=sums,
            chosen=chosen if end == chips else None,
        )
        at = end
    own = own_residual(meta, pieces)

    keep, got = [], []
    for active in sums:
        kept, given = down(active, w_down[0])
        keep.append(kept)
        got.append(swap_cores(given))
    mixture = jnp.concatenate(ring_reduce(keep, got), axis=1).reshape(rows, groups, width // groups)
    if groups == 2:
        other = lax.dynamic_index_in_dim(mixture, 1 - group, 1, keepdims=False)
        other = lax.ppermute(other.astype(jnp.bfloat16), "sec", SWAP)
        mixture = plus(lax.dynamic_index_in_dim(mixture, group, 1, keepdims=False), other)
    else:
        mixture = lax.psum_scatter(mixture, GROUP, scatter_dimension=1, tiled=False)
    own = own.reshape(groups, chips // groups, rows, chip_cols)
    own = lax.dynamic_index_in_dim(own, group, 0, keepdims=False)
    own = own.transpose(1, 0, 2).reshape(rows, width // groups)
    return plus(own, mixture).astype(jnp.bfloat16)


def solution(mesh):
    sec, batch, head = mesh.shape["sec"], mesh.shape["batch"], mesh.shape["head"]
    devices = mesh.devices.reshape(sec, batch // 2, 2, head)
    split = Mesh(devices, ("sec", "chip", "core", "head"))
    tokens = ("chip", "core")
    in_specs = (
        P(tokens, None),
        P(tokens, GROUP, None),
        P(tokens, None, None),
        P(tokens, None),
        P(tokens),
        P(GROUP, None, None),
        P(GROUP, tokens),
        P(),
        P(),
        P(tokens, None),
        P(tokens, None, None, GROUP),
        P(tokens, GROUP, None),
    )
    out_specs = P(tokens, GROUP)
    return jax.shard_map(body, mesh=split, in_specs=in_specs, out_specs=out_specs, check_vma=False)
```

```python
import functools

import jax
import jax.numpy as jnp
from jax import lax
from jax.experimental import pallas as pl
from jax.experimental.pallas import tpu as pltpu
from jax.sharding import Mesh, PartitionSpec as P

QKD = 192
TOP = 8

norm_epsilon = 1e-06
route_scale = 2.5

GROUP = ("sec", "head")
SWAP = [(0, 1), (1, 0)]
STREAMS = 2
VMEM = 56 * 1024 * 1024
NT = (((1,), (1,)), ((), ()))
ANY = pl.BlockSpec(memory_space=pl.ANY)
IN_HBM = pl.BlockSpec(memory_space=pltpu.HBM)
IN_VMEM = pl.BlockSpec(memory_space=pltpu.VMEM)
IN_SMEM = pl.BlockSpec(memory_space=pltpu.SMEM)


def attend(queries, latent_cache, new_latent, cache_lengths, value_up):
    row_count = queries.shape[0]
    latent_width = value_up.shape[1]
    cache_depth = latent_cache.shape[1]
    score_scale = QKD ** (-0.5)
    scores = (
        jnp.einsum("thk,tjk->thj", queries, latent_cache, preferred_element_type=jnp.float32)
        * score_scale
    )
    own_score = (
        jnp.einsum("thk,tk->th", queries, new_latent, preferred_element_type=jnp.float32)
        * score_scale
    )
    positions = lax.broadcasted_iota(jnp.int32, (1, 1, cache_depth), 2)
    in_cache = positions < cache_lengths[:, None, None]
    scores = jnp.where(in_cache, scores, -jnp.inf)
    top_score = jnp.maximum(jnp.max(scores, axis=2), own_score)
    cache_exp = jnp.exp(scores - top_score[:, :, None])
    own_exp = jnp.exp(own_score - top_score)
    softmax_sum = jnp.sum(cache_exp, axis=2) + own_exp
    cache_weights = (cache_exp / softmax_sum[:, :, None]).astype(jnp.bfloat16)
    own_weights = (own_exp / softmax_sum).astype(jnp.bfloat16)
    latent_out = jnp.einsum(
        "thj,tjc->thc",
        cache_weights,
        latent_cache[:, :, :latent_width],
        preferred_element_type=jnp.float32,
    )
    latent_out = latent_out + own_weights.astype(jnp.float32)[:, :, None] * new_latent[
        :, None, :latent_width
    ].astype(jnp.float32)
    latent_out = latent_out.astype(jnp.bfloat16)
    head_out = jnp.einsum(
        "thc,hcd->thd", latent_out, value_up, preferred_element_type=jnp.float32
    ).astype(jnp.bfloat16)
    return head_out.reshape(row_count, -1)


def place_of(chip, chips):
    return jnp.where(chip % 2 == 0, chip // 2, chips - 1 - chip // 2)


def chip_at(place, chips):
    place = place % chips
    return jnp.where(place < chips // 2, 2 * place, 2 * (chips - 1 - place) + 1)


def ring_step(block):
    chips = lax.axis_size("chip")
    ring = list(range(0, chips, 2)) + list(range(chips - 1, 0, -2))
    pairs = []
    for i in range(chips):
        here, there = ring[i], ring[(i + 1) % chips]
        pairs += [(2 * here, 2 * there), (2 * there + 1, 2 * here + 1)]
    return lax.ppermute(block, ("chip", "core"), pairs)


def swap_cores(block):
    return lax.ppermute(block, "core", SWAP)


def by_core(core, first, second):
    return jnp.where(core == 0, first, second), jnp.where(core == 0, second, first)


def ring_gather(blocks, between):
    chips = lax.axis_size("chip")
    core = lax.axis_index("core")
    pieces, moving = [[block] for block in blocks], list(blocks)
    for i in range(chips // 2 - 1):
        for s in range(STREAMS):
            moving[s] = ring_step(between(s, i, moving[s], pieces))
            if i:
                moving[s], pieces[s][-1] = lax.optimization_barrier((moving[s], pieces[s][-1]))
            pieces[s] += [moving[s], swap_cores(moving[s])]
    last = between(None, chips // 2 - 1, jnp.where(core == 0, moving[0], moving[1]), pieces)
    last = between(None, None, ring_step(last), pieces)
    for s, piece in enumerate(by_core(core, last, swap_cores(last))):
        pieces[s].append(piece)
    return pieces


def ring_order():
    chips = lax.axis_size("chip")
    place = place_of(lax.axis_index("chip"), chips)
    sign = 2 * lax.axis_index("core") - 1
    places = [place]
    for d in range(1, chips // 2):
        places += [place + sign * d, place - sign * d]
    places.append(place + chips // 2)
    return [chip_at(p, chips) for p in places]


def plus(a, b):
    return a.astype(jnp.float32) + b.astype(jnp.float32)


def reduce_rows():
    chips = lax.axis_size("chip")
    core = lax.axis_index("core")
    chip = lax.axis_index("chip")
    place = place_of(chip, chips)
    far = 2 * chip_at(place + chips // 2, chips)

    def way(side, sign):
        blocks = []
        for d in range(chips // 2 - 1, 0, -1):
            at = 2 * chip_at(place + sign * d, chips)
            blocks += [at, at + 1]
        return [far + side] + blocks[:2], blocks[2:] + [2 * chip + side]

    sign = 1 - 2 * core
    keep, give = way(core, sign), way(1 - core, -sign)
    return keep[0] + give[0], keep[1] + give[1]


def ring_reduce(keep, got):
    core = lax.axis_index("core")
    rows = keep[0].shape[0] // 3

    def cut(at, size, s):
        def one(parts):
            part, start = (parts[0], at) if at < 3 * rows else (parts[1], at - 3 * rows)
            half = part.shape[1] // STREAMS
            return part[start : start + size, s * half : (s + 1) * half]

        return plus(one(keep), one(got))

    moving = [ring_step(cut(0, rows, s).astype(jnp.bfloat16)) for s in range(STREAMS)]
    moving = [
        jnp.concatenate([jnp.where(core == 0, m, 0), jnp.where(core == 0, 0, m)], axis=0)
        for m in moving
    ]
    at, ahead = rows, None
    total = 3 * rows + keep[1].shape[0]
    while at < total - rows:
        for s in range(STREAMS):
            if ahead is not None:
                moving[s], _ = lax.optimization_barrier((moving[s], ahead))
            ahead = plus(cut(at, 2 * rows, s), moving[s]).astype(jnp.bfloat16)
            moving[s] = ring_step(ahead)
        at += 2 * rows
    sums = []
    for s in range(STREAMS):
        mine, theirs = by_core(core, moving[s][:rows], moving[s][rows:])
        sums.append(plus(cut(at, rows, s), plus(mine, swap_cores(theirs))))
    return sums


def stream(count, copy):
    for k in range(min(2, count)):
        copy(k).start()

    def ready(k):
        copy(k).wait()

        @pl.when(k + 2 < count)
        def _():
            copy(k + 2).start()

    return ready


def project_kernel(steps, count, weight, *refs):
    pieces, (out, rows, held, piece_sems, weight_sems) = refs[:-5], refs[-5:]
    depth = held.shape[2]
    block, half = pieces[0].shape
    copies = []
    for i, piece in enumerate(pieces):
        at, s = i % count, i // count
        target = rows.at[pl.ds(at * block, block), pl.ds(s * half, half)]
        copies.append(pltpu.make_async_copy(piece, target, piece_sems.at[i]))
    for copy in copies:
        copy.start()

    def weight_copy(k):
        columns = pl.ds(pl.multiple_of(k * depth, depth), depth)
        slot = k % 3
        return pltpu.make_async_copy(weight.at[:, columns], held.at[slot], weight_sems.at[slot])

    ready = stream(steps, weight_copy)
    for copy in copies:
        copy.wait()
    out[...] = jnp.zeros_like(out)

    @pl.loop(0, steps)
    def _(k):
        ready(k)
        columns = pl.ds(pl.multiple_of(k * depth, depth), depth)
        out[...] += lax.dot_general(
            rows[:, columns], held[k % 3], NT, preferred_element_type=jnp.float32
        )


def project(pieces, weight):
    count = len(pieces[0])
    rows, half = pieces[0][0].shape
    depth = STREAMS * half
    columns = weight.shape[0]
    steps = 8
    total = count * rows
    return pl.pallas_call(
        functools.partial(project_kernel, steps, count),
        out_shape=jax.ShapeDtypeStruct((total, columns), jnp.float32),
        in_specs=[ANY] * (1 + STREAMS * count),
        out_specs=IN_VMEM,
        scratch_shapes=[
            pltpu.VMEM((total, depth), jnp.bfloat16),
            pltpu.VMEM((3, columns, depth // steps), jnp.bfloat16),
            pltpu.SemaphoreType.DMA((STREAMS * count,)),
            pltpu.SemaphoreType.DMA((3,)),
        ],
        compiler_params=pltpu.CompilerParams(vmem_limit_bytes=VMEM),
        cost_estimate=pl.CostEstimate(
            flops=2 * total * depth * columns,
            bytes_accessed=2 * depth * (total + columns) + 4 * total * columns,
            transcendentals=0,
        ),
    )(weight, *[piece for part in pieces for piece in part])


def finish_kernel(count, meta, arrived, *refs):
    parts, got, out = refs[:count], refs[count : 2 * count], refs[2 * count]
    chips, rows, columns = out.shape
    i = 0
    for part, other in zip(parts, got):
        for j in range(part.shape[0] // rows):
            at = meta[i]
            block = part[j * rows : (j + 1) * rows, :] + other[j * rows : (j + 1) * rows, :].astype(jnp.float32)
            hidden = arrived[at][:, :columns].astype(jnp.float32)
            out[at] = (hidden + block).astype(jnp.bfloat16)
            i += 1


def finish(meta, parts, got, arrived):
    columns = parts[0].shape[1]
    return pl.pallas_call(
        functools.partial(finish_kernel, len(parts)),
        out_shape=jax.ShapeDtypeStruct(arrived.shape[:2] + (columns,), jnp.bfloat16),
        in_specs=[IN_SMEM] + [IN_VMEM] * (1 + 2 * len(parts)),
        out_specs=IN_VMEM,
        compiler_params=pltpu.CompilerParams(vmem_limit_bytes=16 * 1024 * 1024),
    )(meta, arrived, *parts, *got)


def own_kernel(count, meta, *refs):
    pieces, (out, sems) = refs[:-2], refs[-2:]
    chips, share, _ = out.shape
    half = pieces[0].shape[0]
    place = meta[chips]
    for s in range(STREAMS):

        @pl.when(place * share // half == s)
        def _():
            at = pl.ds(pl.multiple_of(place * share - s * half, share), share)
            copies = [
                pltpu.make_async_copy(pieces[s * count + i].at[at, :], out.at[meta[i]], sems.at[i])
                for i in range(count)
            ]
            for copy in copies:
                copy.start()
            for copy in copies:
                copy.wait()


def own_residual(meta, pieces):
    chips = len(pieces[0])
    half, depth = pieces[0][0].shape
    share = half // chips
    return pl.pallas_call(
        functools.partial(own_kernel, chips),
        out_shape=jax.ShapeDtypeStruct((chips, share, depth), jnp.bfloat16),
        in_specs=[IN_SMEM] + [ANY] * (STREAMS * chips),
        out_specs=IN_VMEM,
        scratch_shapes=[pltpu.SemaphoreType.DMA((chips,))],
        compiler_params=pltpu.CompilerParams(vmem_limit_bytes=VMEM),
    )(meta, *[piece for part in pieces for piece in part])


def gate_kernel(parts, first, count, chips, last, meta, gain, router, *refs):
    rest = list(refs)

    def take(n):
        head = rest[:n]
        del rest[:n]
        return head

    chosen = take(1)[0] if last else None
    before = take(3) if first else None
    gate_up, pieces = take(parts), take(STREAMS * count)
    outs = take(2 if last else 3)
    held, weight = take(2)
    if last:
        active, total, logits, squares = take(4)
    else:
        total, logits, squares = outs
    piece_sems, weight_sems = take(2)
    rows, depth = held.shape[1:]
    half = pieces[0].shape[0]
    per = chips // parts
    for i in range(count):
        for s in range(STREAMS):
            target = held.at[i, pl.ds(s * half, half), :]
            pltpu.make_async_copy(pieces[s * count + i], target, piece_sems.at[i]).start()

    def weight_start(k):
        at = meta[first + k]
        slot = k % 3
        for p in range(parts):

            @pl.when(at // per == p)
            def _():
                part = pl.ds(pl.multiple_of(at % per * depth, 16), depth)
                pltpu.make_async_copy(
                    gate_up[p].at[part, :], weight.at[slot], weight_sems.at[slot]
                ).start()

    for k in range(min(2, count)):
        weight_start(k)
    for i, ref in enumerate((total, logits, squares)):
        ref[...] = before[i][...] if first else jnp.zeros_like(ref)

    @pl.loop(0, count)
    def _(k):
        pltpu.make_async_copy(held.at[k], held.at[k], piece_sems.at[k]).wait()
        slot = k % 3
        pltpu.make_async_copy(weight.at[slot], weight.at[slot], weight_sems.at[slot]).wait()

        @pl.when(k + 2 < count)
        def _():
            weight_start(k + 2)

        at = meta[first + k]
        block = held[k].astype(jnp.float32)
        if depth % 128 == 0:
            for j in range(0, depth, 128):
                squares[...] += block[:, j : j + 128] * block[:, j : j + 128]
        else:
            squares[...] += jnp.sum(block * block, axis=1, keepdims=True) * (1.0 / 128)
        scaled = (block * gain[at]).astype(jnp.bfloat16)
        logits[...] += lax.dot_general(scaled, router[at], NT, preferred_element_type=jnp.float32)
        total[...] += jnp.dot(scaled, weight[slot], preferred_element_type=jnp.float32)

    if not last:
        return
    hidden = active.shape[1]
    place = meta[chips]
    width = chips * depth
    norm = lax.rsqrt(jnp.sum(squares[...], axis=1, keepdims=True) * (1.0 / width) + norm_epsilon)
    affinity = jax.nn.sigmoid(logits[...] * norm) * chosen[...]
    mine = lax.broadcasted_iota(jnp.int32, affinity.shape, 1) == place
    share_of = jnp.sum(jnp.where(mine, affinity, 0.0), axis=1, keepdims=True)
    scale = route_scale * share_of / jnp.sum(affinity, axis=1, keepdims=True)
    gate = total[:, :hidden] * norm
    up = total[:, hidden:] * (norm * scale)
    active[...] = (gate * jax.nn.sigmoid(gate) * up).astype(jnp.bfloat16)
    share = rows // (2 * chips)
    i = chips + 1
    for out in outs:
        for j in range(0, out.shape[0], share):
            at = pl.ds(pl.multiple_of(meta[i] * share, share), share)
            out[j : j + share, :] = active[at, :]
            i += 1


def gate(meta, first, pieces, gate_up, gain, router, before=None, chosen=None):
    chips = gain.shape[0]
    names = router.shape[1]
    count = len(pieces[0])
    half, depth = pieces[0][0].shape
    rows = STREAMS * half
    wide = gate_up[0].shape[1]
    last = chosen is not None
    share = rows // (2 * chips)
    sums = (
        jax.ShapeDtypeStruct((rows, wide), jnp.float32),
        jax.ShapeDtypeStruct((rows, names), jnp.float32),
        jax.ShapeDtypeStruct((rows, 128), jnp.float32),
    )
    ends = (
        jax.ShapeDtypeStruct((6 * share, wide // 2), jnp.bfloat16),
        jax.ShapeDtypeStruct((rows - 6 * share, wide // 2), jnp.bfloat16),
    )
    own = [chosen] * last + list(before or ())
    scratch = [
        pltpu.VMEM((count, rows, depth), jnp.bfloat16),
        pltpu.VMEM((3, depth, wide), jnp.bfloat16),
    ]
    if last:
        scratch += [pltpu.VMEM((rows, wide // 2), jnp.bfloat16)]
        scratch += [pltpu.VMEM(t.shape, t.dtype) for t in sums]
    scratch += [pltpu.SemaphoreType.DMA((count,)), pltpu.SemaphoreType.DMA((3,))]
    return pl.pallas_call(
        functools.partial(gate_kernel, len(gate_up), first, count, chips, last),
        out_shape=ends if last else sums,
        in_specs=[IN_SMEM] + [IN_VMEM] * (2 + len(own)) + [IN_HBM] * len(gate_up) + [ANY] * (STREAMS * count),
        out_specs=(IN_VMEM,) * (2 if last else 3),
        scratch_shapes=scratch,
        compiler_params=pltpu.CompilerParams(vmem_limit_bytes=VMEM),
        cost_estimate=pl.CostEstimate(
            flops=2 * rows * count * depth * wide,
            bytes_accessed=2 * count * depth * (wide + rows),
            transcendentals=rows * wide if last else 0,
        ),
    )(meta, gain, router, *own, *gate_up, *[piece for part in pieces for piece in part])


def down_kernel(steps, active, weight, keep, give, held, sems):
    rows = keep.shape[0]
    span = held.shape[2]

    def copy(k):
        columns = pl.ds(pl.multiple_of(k * span, span), span)
        return pltpu.make_async_copy(weight.at[:, columns], held.at[k % 3], sems.at[k % 3])

    ready = stream(steps, copy)

    @pl.loop(0, steps)
    def _(k):
        ready(k)
        columns = pl.ds(pl.multiple_of(k * span, span), span)
        result = jnp.dot(active[...], held[k % 3], preferred_element_type=jnp.float32)
        keep[:, columns] = result[:rows].astype(jnp.bfloat16)
        give[:, columns] = result[rows:].astype(jnp.bfloat16)


def down(active, weight):
    rows, hidden = active.shape
    width = weight.shape[1]
    steps = max(1, width // 1024)
    shape = jax.ShapeDtypeStruct((rows // 2, width), jnp.bfloat16)
    return pl.pallas_call(
        functools.partial(down_kernel, steps),
        out_shape=(shape, shape),
        in_specs=[IN_VMEM, IN_HBM],
        out_specs=(IN_VMEM, IN_VMEM),
        scratch_shapes=[
            pltpu.VMEM((3, hidden, width // steps), jnp.bfloat16),
            pltpu.SemaphoreType.DMA((3,)),
        ],
        compiler_params=pltpu.CompilerParams(vmem_limit_bytes=VMEM),
        cost_estimate=pl.CostEstimate(
            flops=2 * rows * hidden * width,
            bytes_accessed=2 * width * (hidden + rows),
            transcendentals=0,
        ),
    )(active, weight)


def body(
    hidden_in,
    queries,
    latent_cache,
    new_latent,
    cache_lengths,
    value_up,
    out_proj,
    norm_gain,
    router,
    expert_ids,
    w_gate_up,
    w_down,
):
    rows = hidden_in.shape[0]
    width = hidden_in.shape[1]
    chips = lax.axis_size("chip")
    cores = lax.axis_size("core")
    groups = lax.axis_size(GROUP)
    core = lax.axis_index("core")
    chip = lax.axis_index("chip")
    group = lax.axis_index(GROUP)
    place = chip * cores + core
    chip_cols = width // chips
    own_cols = chip_cols // cores
    expert_count = router.shape[1]
    total = chips * cores * rows
    order = ring_order()

    outgoing = hidden_in.reshape(rows, chips * cores, own_cols).transpose(1, 0, 2)
    names = jnp.broadcast_to(expert_ids.astype(jnp.bfloat16)[None], (chips * cores, rows, TOP))
    arrived = lax.all_to_all(
        jnp.concatenate([outgoing, names], axis=2),
        ("chip", "core"),
        split_axis=0,
        concat_axis=0,
        tiled=True,
    )

    parts = 4
    span = width // parts
    gate_up = []
    stages = [None, (0, 0), (1, 0), (0, 1)]
    final = chips // 2 - 1
    ends = [(1, 1), (0, 2), (1, 2), (None, final)]
    projected = []

    def during_first(s, i, moving, pieces):
        if i is None:
            part = project([piece[: chips - 1] for piece in pieces], out_proj.T)
            moving, part = lax.optimization_barrier((moving, part))
            projected.append(part)
        if (s, i) in ends:
            p = ends.index((s, i))
            raw = w_gate_up
            if stages[p] is not None:
                raw, _ = lax.optimization_barrier((raw, pieces[stages[p][0]][1 + 2 * stages[p][1]]))
            quarter = raw[0, p * span : (p + 1) * span].reshape(span, -1)
            moving, quarter = lax.optimization_barrier((moving, quarter))
            gate_up.append(quarter)
        return moving

    gain = norm_gain.reshape(chips, 1, chip_cols)
    router_rows = router.T.reshape(expert_count, chips, chip_cols).transpose(1, 0, 2)
    first_rows, then_rows = reduce_rows()
    meta = jnp.stack(order + [place] + first_rows + then_rows).astype(jnp.int32)

    head_out = attend(queries, latent_cache, new_latent, cache_lengths, value_up)
    head_out, arrived = lax.optimization_barrier((head_out, arrived))
    low, high = by_core(core, head_out, swap_cores(head_out))
    block = jnp.concatenate([low, high], axis=0)
    half = block.shape[1] // STREAMS
    pieces = ring_gather([block[:, s * half : (s + 1) * half] for s in range(STREAMS)], during_first)
    projected.append(project([piece[chips - 1 :] for piece in pieces], out_proj.T))
    parts, got = [], []
    for part in projected:
        if groups == 2:
            parts.append(part)
            got.append(lax.ppermute(part.astype(jnp.bfloat16), "sec", SWAP))
        else:
            parts.append(lax.psum(part, GROUP))
            got.append(jnp.zeros(part.shape, jnp.bfloat16))
    arrived = arrived.reshape(chips, cores * rows, own_cols + TOP)
    residual = finish(meta, parts, got, arrived).reshape(total, own_cols)
    low, high = by_core(core, residual, swap_cores(residual))
    block = jnp.concatenate([low, high], axis=1)
    half = total // STREAMS

    ids = arrived[:, :, own_cols:].reshape(total, TOP, 1).astype(jnp.int32)
    grid = lax.broadcasted_iota(jnp.int32, (1, 1, expert_count), 2)
    chosen = jnp.any(ids == grid, axis=1).astype(jnp.float32)
    sums = [None]

    def add_blocks(pieces, at, end, chosen=None):
        blocks = [piece[at:end] for piece in pieces]
        return gate(meta, at, blocks, gate_up, gain, router_rows, sums[-1], chosen)

    spans = {
        (0, final - 1): (0, chips - 5),
        (None, final): (chips - 5, chips - 3),
        (None, None): (chips - 3, chips - 1),
    }

    def during_second(s, i, moving, pieces):
        if (s, i) in spans:
            moving, added = lax.optimization_barrier((moving, add_blocks(pieces, *spans[s, i])))
            sums.append(added)
        return moving

    pieces = ring_gather([block[s * half : (s + 1) * half] for s in range(STREAMS)], during_second)
    actives = add_blocks(pieces, chips - 1, chips, chosen)
    own = own_residual(meta, pieces)

    keep, got = [], []
    for active in actives:
        kept, given = down(active, w_down[0])
        keep.append(kept)
        got.append(swap_cores(given))
    mixture = jnp.concatenate(ring_reduce(keep, got), axis=1).reshape(rows, groups, width // groups)
    if groups == 2:
        other = lax.dynamic_index_in_dim(mixture, 1 - group, 1, keepdims=False)
        other = lax.ppermute(other.astype(jnp.bfloat16), "sec", SWAP)
        mixture = plus(lax.dynamic_index_in_dim(mixture, group, 1, keepdims=False), other)
    else:
        mixture = lax.psum_scatter(mixture, GROUP, scatter_dimension=1, tiled=False)
    own = own.reshape(groups, chips // groups, rows, chip_cols)
    own = lax.dynamic_index_in_dim(own, group, 0, keepdims=False)
    own = own.transpose(1, 0, 2).reshape(rows, width // groups)
    return plus(own, mixture).astype(jnp.bfloat16)


def solution(mesh):
    sec, batch, head = mesh.shape["sec"], mesh.shape["batch"], mesh.shape["head"]
    devices = mesh.devices.reshape(sec, batch // 2, 2, head)
    split = Mesh(devices, ("sec", "chip", "core", "head"))
    tokens = ("chip", "core")
    in_specs = (
        P(tokens, None),
        P(tokens, GROUP, None),
        P(tokens, None, None),
        P(tokens, None),
        P(tokens),
        P(GROUP, None, None),
        P(GROUP, tokens),
        P(),
        P(),
        P(tokens, None),
        P(tokens, None, None, GROUP),
        P(tokens, GROUP, None),
    )
    out_specs = P(tokens, GROUP)
    return jax.shard_map(body, mesh=split, in_specs=in_specs, out_specs=out_specs, check_vma=False)
```

```python
import functools

import jax
import jax.numpy as jnp
from jax import lax
from jax.experimental import pallas as pl
from jax.experimental.pallas import tpu as pltpu
from jax.sharding import Mesh, PartitionSpec as P

QKD = 192
TOP = 8

norm_epsilon = 1e-06
route_scale = 2.5

GROUP = ("sec", "head")
SWAP = [(0, 1), (1, 0)]
STREAMS = 2
VMEM = 56 * 1024 * 1024
NT = (((1,), (1,)), ((), ()))
ANY = pl.BlockSpec(memory_space=pl.ANY)
IN_HBM = pl.BlockSpec(memory_space=pltpu.HBM)
IN_VMEM = pl.BlockSpec(memory_space=pltpu.VMEM)
IN_SMEM = pl.BlockSpec(memory_space=pltpu.SMEM)


def attend(queries, latent_cache, new_latent, cache_lengths, value_up):
    row_count = queries.shape[0]
    latent_width = value_up.shape[1]
    cache_depth = latent_cache.shape[1]
    score_scale = QKD ** (-0.5)
    scores = (
        jnp.einsum("thk,tjk->thj", queries, latent_cache, preferred_element_type=jnp.float32)
        * score_scale
    )
    own_score = (
        jnp.einsum("thk,tk->th", queries, new_latent, preferred_element_type=jnp.float32)
        * score_scale
    )
    positions = lax.broadcasted_iota(jnp.int32, (1, 1, cache_depth), 2)
    in_cache = positions < cache_lengths[:, None, None]
    scores = jnp.where(in_cache, scores, -jnp.inf)
    top_score = jnp.maximum(jnp.max(scores, axis=2), own_score)
    cache_exp = jnp.exp(scores - top_score[:, :, None])
    own_exp = jnp.exp(own_score - top_score)
    softmax_sum = jnp.sum(cache_exp, axis=2) + own_exp
    cache_weights = (cache_exp / softmax_sum[:, :, None]).astype(jnp.bfloat16)
    own_weights = (own_exp / softmax_sum).astype(jnp.bfloat16)
    latent_out = jnp.einsum(
        "thj,tjc->thc",
        cache_weights,
        latent_cache[:, :, :latent_width],
        preferred_element_type=jnp.float32,
    )
    latent_out = latent_out + own_weights.astype(jnp.float32)[:, :, None] * new_latent[
        :, None, :latent_width
    ].astype(jnp.float32)
    latent_out = latent_out.astype(jnp.bfloat16)
    head_out = jnp.einsum(
        "thc,hcd->thd", latent_out, value_up, preferred_element_type=jnp.float32
    ).astype(jnp.bfloat16)
    return head_out.reshape(row_count, -1)


def place_of(chip, chips):
    return jnp.where(chip % 2 == 0, chip // 2, chips - 1 - chip // 2)


def chip_at(place, chips):
    place = place % chips
    return jnp.where(place < chips // 2, 2 * place, 2 * (chips - 1 - place) + 1)


def ring_step(block):
    chips = lax.axis_size("chip")
    ring = list(range(0, chips, 2)) + list(range(chips - 1, 0, -2))
    pairs = []
    for i in range(chips):
        here, there = ring[i], ring[(i + 1) % chips]
        pairs += [(2 * here, 2 * there), (2 * there + 1, 2 * here + 1)]
    return lax.ppermute(block, ("chip", "core"), pairs)


def swap_cores(block):
    return lax.ppermute(block, "core", SWAP)


def by_core(core, first, second):
    return jnp.where(core == 0, first, second), jnp.where(core == 0, second, first)


def ring_gather(blocks, between):
    chips = lax.axis_size("chip")
    core = lax.axis_index("core")
    pieces, moving = [[block] for block in blocks], list(blocks)
    for i in range(chips // 2 - 1):
        for s in range(STREAMS):
            moving[s] = ring_step(between(s, i, moving[s], pieces))
            if i:
                moving[s], pieces[s][-1] = lax.optimization_barrier((moving[s], pieces[s][-1]))
            pieces[s] += [moving[s], swap_cores(moving[s])]
    last = between(None, chips // 2 - 1, jnp.where(core == 0, moving[0], moving[1]), pieces)
    last = between(None, None, ring_step(last), pieces)
    for s, piece in enumerate(by_core(core, last, swap_cores(last))):
        pieces[s].append(piece)
    return pieces


def ring_order():
    chips = lax.axis_size("chip")
    place = place_of(lax.axis_index("chip"), chips)
    sign = 2 * lax.axis_index("core") - 1
    places = [place]
    for d in range(1, chips // 2):
        places += [place + sign * d, place - sign * d]
    places.append(place + chips // 2)
    return [chip_at(p, chips) for p in places]


def plus(a, b):
    return a.astype(jnp.float32) + b.astype(jnp.float32)


def reduce_rows():
    chips = lax.axis_size("chip")
    core = lax.axis_index("core")
    chip = lax.axis_index("chip")
    place = place_of(chip, chips)
    far = 2 * chip_at(place + chips // 2, chips)

    def way(side, sign):
        blocks = []
        for d in range(chips // 2 - 1, 0, -1):
            at = 2 * chip_at(place + sign * d, chips)
            blocks += [at, at + 1]
        return [far + side] + blocks[:2], blocks[2:] + [2 * chip + side]

    sign = 1 - 2 * core
    keep, give = way(core, sign), way(1 - core, -sign)
    return keep[0] + give[0], keep[1] + give[1]


def ring_reduce(keep, got, ready):
    core = lax.axis_index("core")
    rows = keep[0].shape[0] // 3

    def cut(at, size, s):
        def one(parts):
            part, start = (parts[0], at) if at < 3 * rows else (parts[1], at - 3 * rows)
            half = part.shape[1] // STREAMS
            return part[start : start + size, s * half : (s + 1) * half]

        return plus(one(keep), one(got))

    moving = [ring_step(cut(0, rows, s).astype(jnp.bfloat16)) for s in range(STREAMS)]
    moving = [
        jnp.concatenate([jnp.where(core == 0, m, 0), jnp.where(core == 0, 0, m)], axis=0)
        for m in moving
    ]
    at, ahead = rows, ready
    total = 3 * rows + keep[1].shape[0]
    while at < total - rows:
        for s in range(STREAMS):
            if at > rows or s > 0:
                moving[s], _ = lax.optimization_barrier((moving[s], ahead))
            ahead = plus(cut(at, 2 * rows, s), moving[s]).astype(jnp.bfloat16)
            if at > rows and s == STREAMS - 1:
                ahead, ready = lax.optimization_barrier((ahead, ready))
            moving[s] = ring_step(ahead)
        at += 2 * rows
    sums = []
    for s in range(STREAMS):
        mine, theirs = by_core(core, moving[s][:rows], moving[s][rows:])
        sums.append(plus(cut(at, rows, s), plus(mine, swap_cores(theirs))))
    return sums


def stream(count, copy):
    for k in range(min(2, count)):
        copy(k).start()

    def ready(k):
        copy(k).wait()

        @pl.when(k + 2 < count)
        def _():
            copy(k + 2).start()

    return ready


def project_kernel(steps, count, weight, *refs):
    pieces, (out, rows, held, piece_sems, weight_sems) = refs[:-5], refs[-5:]
    depth = held.shape[2]
    block, half = pieces[0].shape
    copies = []
    for i, piece in enumerate(pieces):
        at, s = i % count, i // count
        target = rows.at[pl.ds(at * block, block), pl.ds(s * half, half)]
        copies.append(pltpu.make_async_copy(piece, target, piece_sems.at[i]))
    for copy in copies:
        copy.start()

    def weight_copy(k):
        columns = pl.ds(pl.multiple_of(k * depth, depth), depth)
        slot = k % 3
        return pltpu.make_async_copy(weight.at[:, columns], held.at[slot], weight_sems.at[slot])

    ready = stream(steps, weight_copy)
    for copy in copies:
        copy.wait()
    out[...] = jnp.zeros_like(out)

    @pl.loop(0, steps)
    def _(k):
        ready(k)
        columns = pl.ds(pl.multiple_of(k * depth, depth), depth)
        out[...] += lax.dot_general(
            rows[:, columns], held[k % 3], NT, preferred_element_type=jnp.float32
        )


def project(pieces, weight):
    count = len(pieces[0])
    rows, half = pieces[0][0].shape
    depth = STREAMS * half
    columns = weight.shape[0]
    steps = 8
    total = count * rows
    return pl.pallas_call(
        functools.partial(project_kernel, steps, count),
        out_shape=jax.ShapeDtypeStruct((total, columns), jnp.float32),
        in_specs=[ANY] * (1 + STREAMS * count),
        out_specs=IN_VMEM,
        scratch_shapes=[
            pltpu.VMEM((total, depth), jnp.bfloat16),
            pltpu.VMEM((3, columns, depth // steps), jnp.bfloat16),
            pltpu.SemaphoreType.DMA((STREAMS * count,)),
            pltpu.SemaphoreType.DMA((3,)),
        ],
        compiler_params=pltpu.CompilerParams(vmem_limit_bytes=20 * 1024 * 1024),
        cost_estimate=pl.CostEstimate(
            flops=2 * total * depth * columns,
            bytes_accessed=2 * depth * (total + columns) + 4 * total * columns,
            transcendentals=0,
        ),
    )(weight, *[piece for part in pieces for piece in part])


def finish_kernel(count, meta, arrived, gain, router, *refs):
    parts, got, (out, stats) = refs[:count], refs[count : 2 * count], refs[2 * count :]
    chips, rows, columns = out.shape
    names = router.shape[0]
    i = 0
    for part, other in zip(parts, got):
        for j in range(part.shape[0] // rows):
            at = meta[i]
            block = part[j * rows : (j + 1) * rows, :] + other[j * rows : (j + 1) * rows, :].astype(jnp.float32)
            block = arrived[at][:, :columns].astype(jnp.float32) + block
            scaled = (block * gain[...]).astype(jnp.bfloat16)
            out[at] = scaled
            stats[at, :, :names] = lax.dot_general(
                scaled, router[...], NT, preferred_element_type=jnp.float32
            )
            stats[at, :, names : names + 1] = jnp.sum(block * block, axis=1, keepdims=True)
            i += 1


def finish(meta, parts, got, arrived, gain, router):
    columns = parts[0].shape[1]
    chips, rows, _ = arrived.shape
    return pl.pallas_call(
        functools.partial(finish_kernel, len(parts)),
        out_shape=(
            jax.ShapeDtypeStruct((chips, rows, columns), jnp.bfloat16),
            jax.ShapeDtypeStruct((chips, rows, router.shape[0] + 1), jnp.float32),
        ),
        in_specs=[IN_SMEM] + [IN_VMEM] * (3 + 2 * len(parts)),
        out_specs=(IN_VMEM, IN_VMEM),
        compiler_params=pltpu.CompilerParams(vmem_limit_bytes=16 * 1024 * 1024),
    )(meta, arrived, gain, router, *parts, *got)


def own_kernel(count, meta, *refs):
    pieces, (out, sems) = refs[:-2], refs[-2:]
    chips, share, _ = out.shape
    half = pieces[0].shape[0]
    place = meta[chips]
    for s in range(STREAMS):

        @pl.when(place * share // half == s)
        def _():
            at = pl.ds(pl.multiple_of(place * share - s * half, share), share)
            copies = [
                pltpu.make_async_copy(pieces[s * count + i].at[at, :], out.at[meta[i]], sems.at[i])
                for i in range(count)
            ]
            for copy in copies:
                copy.start()
            for copy in copies:
                copy.wait()


def own_residual(meta, pieces):
    chips = len(pieces[0])
    half, depth = pieces[0][0].shape
    share = half // chips
    return pl.pallas_call(
        functools.partial(own_kernel, chips),
        out_shape=jax.ShapeDtypeStruct((chips, share, depth), jnp.bfloat16),
        in_specs=[IN_SMEM] + [ANY] * (STREAMS * chips),
        out_specs=IN_VMEM,
        scratch_shapes=[pltpu.SemaphoreType.DMA((chips,))],
        compiler_params=pltpu.CompilerParams(vmem_limit_bytes=VMEM),
    )(meta, *[piece for part in pieces for piece in part])


def piece_starts(pieces, count, held, sems):
    half = pieces[0].shape[0]
    for i in range(count):
        for s in range(STREAMS):
            target = held.at[i, pl.ds(s * half, half), :]
            pltpu.make_async_copy(pieces[s * count + i], target, sems.at[i]).start()


def weight_start(at, gate_up, depth, per, target, sem):
    for p, part in enumerate(gate_up):

        @pl.when(at // per == p)
        def _():
            span = pl.ds(pl.multiple_of(at % per * depth, 16), depth)
            pltpu.make_async_copy(part.at[span, :], target, sem).start()


def wait_for(ref, sem):
    pltpu.make_async_copy(ref, ref, sem).wait()


def gate_kernel(parts, first, count, chips, meta, *refs):
    gate_up, pieces = refs[:parts], refs[parts:-5]
    total, held, weight, piece_sems, weight_sems = refs[-5:]
    depth = held.shape[2]
    for k in range(count):
        weight_start(
            meta[first + k], gate_up, depth, chips // parts, weight.at[k], weight_sems.at[k]
        )
        if k == 0:
            piece_starts(pieces, count, held, piece_sems)

    @pl.loop(0, count)
    def _(k):
        wait_for(held.at[k], piece_sems.at[k])
        wait_for(weight.at[k], weight_sems.at[k])
        result = jnp.dot(held[k], weight[k], preferred_element_type=jnp.float32)

        @pl.when(k == 0)
        def _():
            total[...] = result

        @pl.when(k > 0)
        def _():
            total[...] += result


def gate(meta, first, pieces, gate_up, chips):
    count = len(pieces[0])
    half, depth = pieces[0][0].shape
    rows = STREAMS * half
    wide = gate_up[0].shape[1]
    return pl.pallas_call(
        functools.partial(gate_kernel, len(gate_up), first, count, chips),
        out_shape=jax.ShapeDtypeStruct((rows, wide), jnp.float32),
        in_specs=[IN_SMEM] + [IN_HBM] * len(gate_up) + [ANY] * (STREAMS * count),
        out_specs=IN_VMEM,
        scratch_shapes=[
            pltpu.VMEM((count, rows, depth), jnp.bfloat16),
            pltpu.VMEM((count, depth, wide), jnp.bfloat16),
            pltpu.SemaphoreType.DMA((count,)),
            pltpu.SemaphoreType.DMA((count,)),
        ],
        compiler_params=pltpu.CompilerParams(vmem_limit_bytes=VMEM),
        cost_estimate=pl.CostEstimate(
            flops=2 * rows * count * depth * wide,
            bytes_accessed=2 * count * depth * (wide + rows),
            transcendentals=0,
        ),
    )(meta, *gate_up, *[piece for part in pieces for piece in part])


def tail_kernel(parts, first, count, chips, meta, norm, scale, before, down, *refs):
    gate_up, pieces = refs[:parts], refs[parts : parts + STREAMS * count]
    rest = refs[parts + STREAMS * count :]
    outs = rest[:4]
    held, weight, total, earlier, active, ordered, second, staged = rest[4:12]
    piece_sems, weight_sems, earlier_sem, second_sems, out_sems = rest[12:]
    rows, depth = held.shape[1:]
    hidden = active.shape[1]
    steps, _, span = second.shape
    for k in range(count):
        weight_start(
            meta[first + k], gate_up, depth, chips // parts, weight.at[k], weight_sems.at[k]
        )
        if k == 0:
            piece_starts(pieces, count, held, piece_sems)
    pltpu.make_async_copy(before, earlier, earlier_sem).start()

    def columns(n):
        return pl.ds(pl.multiple_of(n * span, span), span)

    @pl.loop(0, steps)
    def _(n):
        pltpu.make_async_copy(down.at[:, columns(n)], second.at[n], second_sems.at[n]).start()

    @pl.loop(0, count)
    def _(k):
        wait_for(held.at[k], piece_sems.at[k])
        wait_for(weight.at[k], weight_sems.at[k])
        result = jnp.dot(held[k], weight[k], preferred_element_type=jnp.float32)

        @pl.when(k == 0)
        def _():
            total[...] = result

        @pl.when(k > 0)
        def _():
            total[...] += result

    pltpu.make_async_copy(before, earlier, earlier_sem).wait()
    gate = (total[:, :hidden] + earlier[:, :hidden]) * norm[...]
    up = (total[:, hidden:] + earlier[:, hidden:]) * (norm[...] * scale[...])
    active[...] = (gate * jax.nn.sigmoid(gate) * up).astype(jnp.bfloat16)
    share = rows // (2 * chips)
    for i in range(2 * chips):
        at = pl.ds(pl.multiple_of(meta[chips + 1 + i] * share, share), share)
        ordered[i * share : (i + 1) * share, :] = active[at, :]

    def out_copies(n):
        copies, at = [], 0
        slot = n % 2
        for i, out in enumerate(outs):
            size = out.shape[0]
            source = staged.at[slot, pl.ds(at, size), :]
            copies.append(
                pltpu.make_async_copy(source, out.at[:, columns(n)], out_sems.at[slot, i])
            )
            at += size
        return copies

    @pl.loop(0, steps)
    def _(n):
        pltpu.make_async_copy(down.at[:, columns(n)], second.at[n], second_sems.at[n]).wait()

        @pl.when(n >= 2)
        def _():
            for copy in out_copies(n - 2):
                copy.wait()

        result = jnp.dot(ordered[...], second[n], preferred_element_type=jnp.float32)
        staged[n % 2] = result.astype(jnp.bfloat16)
        for copy in out_copies(n):
            copy.start()

    for n in range(max(0, steps - 2), steps):
        for copy in out_copies(n):
            copy.wait()


def tail(meta, first, pieces, gate_up, before, norm, scale, down, chips):
    count = len(pieces[0])
    half, depth = pieces[0][0].shape
    rows = STREAMS * half
    wide = gate_up[0].shape[1]
    hidden, width = down.shape
    share = rows // (2 * chips)
    steps = max(1, width // 1024)
    shapes = [3 * share, 3 * share, rows // 2 - 3 * share, rows // 2 - 3 * share]
    return pl.pallas_call(
        functools.partial(tail_kernel, len(gate_up), first, count, chips),
        out_shape=tuple(jax.ShapeDtypeStruct((n, width), jnp.bfloat16) for n in shapes),
        in_specs=[IN_SMEM, IN_VMEM, IN_VMEM, ANY, IN_HBM]
        + [IN_HBM] * len(gate_up)
        + [ANY] * (STREAMS * count),
        out_specs=(ANY,) * 4,
        scratch_shapes=[
            pltpu.VMEM((count, rows, depth), jnp.bfloat16),
            pltpu.VMEM((count, depth, wide), jnp.bfloat16),
            pltpu.VMEM((rows, wide), jnp.float32),
            pltpu.VMEM((rows, wide), jnp.float32),
            pltpu.VMEM((rows, hidden), jnp.bfloat16),
            pltpu.VMEM((rows, hidden), jnp.bfloat16),
            pltpu.VMEM((steps, hidden, width // steps), jnp.bfloat16),
            pltpu.VMEM((2, rows, width // steps), jnp.bfloat16),
            pltpu.SemaphoreType.DMA((count,)),
            pltpu.SemaphoreType.DMA((count,)),
            pltpu.SemaphoreType.DMA(()),
            pltpu.SemaphoreType.DMA((steps,)),
            pltpu.SemaphoreType.DMA((2, 4)),
        ],
        compiler_params=pltpu.CompilerParams(vmem_limit_bytes=VMEM),
        cost_estimate=pl.CostEstimate(
            flops=2 * rows * (count * depth * wide + hidden * width),
            bytes_accessed=2 * (count * depth * (wide + rows) + width * (hidden + rows)),
            transcendentals=rows * wide,
        ),
    )(meta, norm, scale, before, down, *gate_up, *[piece for part in pieces for piece in part])


def body(
    hidden_in,
    queries,
    latent_cache,
    new_latent,
    cache_lengths,
    value_up,
    out_proj,
    norm_gain,
    router,
    expert_ids,
    w_gate_up,
    w_down,
):
    rows = hidden_in.shape[0]
    width = hidden_in.shape[1]
    chips = lax.axis_size("chip")
    cores = lax.axis_size("core")
    groups = lax.axis_size(GROUP)
    core = lax.axis_index("core")
    chip = lax.axis_index("chip")
    group = lax.axis_index(GROUP)
    place = chip * cores + core
    chip_cols = width // chips
    own_cols = chip_cols // cores
    expert_count = router.shape[1]
    total = chips * cores * rows
    order = ring_order()

    outgoing = hidden_in.reshape(rows, chips * cores, own_cols).transpose(1, 0, 2)
    names = jnp.broadcast_to(expert_ids.astype(jnp.bfloat16)[None], (chips * cores, rows, TOP))
    arrived = lax.all_to_all(
        jnp.concatenate([outgoing, names], axis=2),
        ("chip", "core"),
        split_axis=0,
        concat_axis=0,
        tiled=True,
    )

    parts = 4
    span = width // parts
    gate_up = []
    stages = [None, (0, 0), (1, 0), (0, 1)]
    final = chips // 2 - 1
    ends = [(1, 1), (0, 2), (1, 2), (None, final)]
    projected = []

    def during_first(s, i, moving, pieces):
        if i is None:
            part = project([piece[: chips - 1] for piece in pieces], out_proj.T)
            moving, part = lax.optimization_barrier((moving, part))
            projected.append(part)
        if (s, i) in ends:
            p = ends.index((s, i))
            raw = w_gate_up
            if stages[p] is not None:
                raw, _ = lax.optimization_barrier((raw, pieces[stages[p][0]][1 + 2 * stages[p][1]]))
            quarter = raw[0, p * span : (p + 1) * span].reshape(span, -1)
            moving, quarter = lax.optimization_barrier((moving, quarter))
            gate_up.append(quarter)
        return moving

    own_gain = lax.dynamic_slice_in_dim(norm_gain, place * own_cols, own_cols, 0)[None]
    own_router = lax.dynamic_slice_in_dim(router.T, place * own_cols, own_cols, 1)
    first_rows, then_rows = reduce_rows()
    meta = jnp.stack(order + [place] + first_rows + then_rows).astype(jnp.int32)

    head_out = attend(queries, latent_cache, new_latent, cache_lengths, value_up)
    head_out, arrived = lax.optimization_barrier((head_out, arrived))
    low, high = by_core(core, head_out, swap_cores(head_out))
    block = jnp.concatenate([low, high], axis=0)
    half = block.shape[1] // STREAMS
    pieces = ring_gather([block[:, s * half : (s + 1) * half] for s in range(STREAMS)], during_first)
    projected.append(project([piece[chips - 1 :] for piece in pieces], out_proj.T))
    parts, got = [], []
    for part in projected:
        if groups == 2:
            parts.append(part)
            got.append(lax.ppermute(part.astype(jnp.bfloat16), "sec", SWAP))
        else:
            parts.append(lax.psum(part, GROUP))
            got.append(jnp.zeros(part.shape, jnp.bfloat16))
    arrived = arrived.reshape(chips, cores * rows, own_cols + TOP)
    residual, stats = finish(meta, parts, got, arrived, own_gain, own_router)
    residual = residual.reshape(total, own_cols)
    stats = stats.reshape(total, expert_count + 1).T
    stats = stats + swap_cores(stats)
    step = 1
    while step < chips:
        stats = stats + lax.ppermute(stats, "chip", [(i, i ^ step) for i in range(chips)])
        step *= 2
    low, high = by_core(core, residual, swap_cores(residual))
    block = jnp.concatenate([low, high], axis=1)
    half = total // STREAMS

    ids = arrived[:, :, own_cols:].reshape(total, TOP).T.astype(jnp.int32)
    grid = lax.broadcasted_iota(jnp.int32, (1, expert_count, 1), 1)
    chosen = jnp.any(ids[:, None, :] == grid, axis=0)
    norm = lax.rsqrt(stats[expert_count:] / width + norm_epsilon)
    affinity = jnp.where(chosen, jax.nn.sigmoid(stats[:expert_count] * norm), 0.0)
    scale = jnp.sum(jnp.where(grid[0] == place, affinity, 0.0), axis=0, keepdims=True)
    scale = route_scale * scale / jnp.sum(affinity, axis=0, keepdims=True)

    sums, weights = [], [norm.T, scale.T]

    def during_second(s, i, moving, pieces):
        if (s, i) == (STREAMS - 1, final - 1):
            blocks = [piece[: chips - 3] for piece in pieces]
            blocks, moving = lax.optimization_barrier((blocks, moving))
            sums.append(gate(meta, 0, blocks, gate_up, chips))
        if (s, i) == (None, final):
            moving, sums[0], weights[:] = lax.optimization_barrier((moving, sums[0], weights))
        return moving

    pieces = ring_gather([block[s * half : (s + 1) * half] for s in range(STREAMS)], during_second)
    keep_first, give_first, keep_then, give_then = tail(
        meta,
        chips - 3,
        [piece[chips - 3 :] for piece in pieces],
        gate_up,
        sums[0],
        *weights,
        w_down[0],
        chips,
    )

    own = own_residual(meta, pieces).reshape(groups, chips // groups, rows, chip_cols)
    own = lax.dynamic_index_in_dim(own, group, 0, keepdims=False)
    own = own.transpose(1, 0, 2).reshape(rows, width // groups).astype(jnp.float32)
    own = own / lax.dynamic_slice_in_dim(norm_gain, group * (width // groups), width // groups, 0)

    got = [swap_cores(give_first), swap_cores(give_then)]
    mixture = ring_reduce([keep_first, keep_then], got, own)
    if groups == 2:
        mine, other = jnp.where(group == 0, mixture[0], mixture[1]), jnp.where(group == 0, mixture[1], mixture[0])
        mixture = plus(mine, lax.ppermute(other.astype(jnp.bfloat16), "sec", SWAP))
    else:
        mixture = jnp.concatenate(mixture, axis=1).reshape(rows, groups, width // groups)
        mixture = lax.psum_scatter(mixture, GROUP, scatter_dimension=1, tiled=False)
    return plus(own, mixture).astype(jnp.bfloat16)


def solution(mesh):
    sec, batch, head = mesh.shape["sec"], mesh.shape["batch"], mesh.shape["head"]
    devices = mesh.devices.reshape(sec, batch // 2, 2, head)
    split = Mesh(devices, ("sec", "chip", "core", "head"))
    tokens = ("chip", "core")
    in_specs = (
        P(tokens, None),
        P(tokens, GROUP, None),
        P(tokens, None, None),
        P(tokens, None),
        P(tokens),
        P(GROUP, None, None),
        P(GROUP, tokens),
        P(),
        P(),
        P(tokens, None),
        P(tokens, None, None, GROUP),
        P(tokens, GROUP, None),
    )
    out_specs = P(tokens, GROUP)
    return jax.shard_map(body, mesh=split, in_specs=in_specs, out_specs=out_specs, check_vma=False)
```

```python
import functools

import jax
import jax.numpy as jnp
from jax import lax
from jax.experimental import pallas as pl
from jax.experimental.pallas import tpu as pltpu
from jax.sharding import Mesh, PartitionSpec as P

QKD = 192
TOP = 8

norm_epsilon = 1e-06
route_scale = 2.5

GROUP = ("sec", "head")
SWAP = [(0, 1), (1, 0)]
STREAMS = 2
VMEM = 56 * 1024 * 1024
NT = (((1,), (1,)), ((), ()))
ANY = pl.BlockSpec(memory_space=pl.ANY)
IN_HBM = pl.BlockSpec(memory_space=pltpu.HBM)
IN_VMEM = pl.BlockSpec(memory_space=pltpu.VMEM)
IN_SMEM = pl.BlockSpec(memory_space=pltpu.SMEM)


def attend(queries, latent_cache, new_latent, cache_lengths, value_up):
    row_count = queries.shape[0]
    latent_width = value_up.shape[1]
    cache_depth = latent_cache.shape[1]
    score_scale = QKD ** (-0.5)
    scores = (
        jnp.einsum("thk,tjk->thj", queries, latent_cache, preferred_element_type=jnp.float32)
        * score_scale
    )
    own_score = (
        jnp.einsum("thk,tk->th", queries, new_latent, preferred_element_type=jnp.float32)
        * score_scale
    )
    positions = lax.broadcasted_iota(jnp.int32, (1, 1, cache_depth), 2)
    in_cache = positions < cache_lengths[:, None, None]
    scores = jnp.where(in_cache, scores, -jnp.inf)
    top_score = jnp.maximum(jnp.max(scores, axis=2), own_score)
    cache_exp = jnp.exp(scores - top_score[:, :, None])
    own_exp = jnp.exp(own_score - top_score)
    softmax_sum = jnp.sum(cache_exp, axis=2) + own_exp
    cache_weights = (cache_exp / softmax_sum[:, :, None]).astype(jnp.bfloat16)
    own_weights = (own_exp / softmax_sum).astype(jnp.bfloat16)
    latent_out = jnp.einsum(
        "thj,tjc->thc",
        cache_weights,
        latent_cache[:, :, :latent_width],
        preferred_element_type=jnp.float32,
    )
    latent_out = latent_out + own_weights.astype(jnp.float32)[:, :, None] * new_latent[
        :, None, :latent_width
    ].astype(jnp.float32)
    latent_out = latent_out.astype(jnp.bfloat16)
    head_out = jnp.einsum(
        "thc,hcd->thd", latent_out, value_up, preferred_element_type=jnp.float32
    ).astype(jnp.bfloat16)
    return head_out.reshape(row_count, -1)


def place_of(chip, chips):
    return jnp.where(chip % 2 == 0, chip // 2, chips - 1 - chip // 2)


def chip_at(place, chips):
    place = place % chips
    return jnp.where(place < chips // 2, 2 * place, 2 * (chips - 1 - place) + 1)


def ring_step(block):
    chips = lax.axis_size("chip")
    ring = list(range(0, chips, 2)) + list(range(chips - 1, 0, -2))
    pairs = []
    for i in range(chips):
        here, there = ring[i], ring[(i + 1) % chips]
        pairs += [(2 * here, 2 * there), (2 * there + 1, 2 * here + 1)]
    return lax.ppermute(block, ("chip", "core"), pairs)


def swap_cores(block):
    return lax.ppermute(block, "core", SWAP)


def by_core(core, first, second):
    return jnp.where(core == 0, first, second), jnp.where(core == 0, second, first)


def ring_gather(blocks, between):
    chips = lax.axis_size("chip")
    core = lax.axis_index("core")
    pieces, moving = [[block] for block in blocks], list(blocks)
    for i in range(chips // 2 - 1):
        for s in range(STREAMS):
            moving[s] = ring_step(between(s, i, moving[s], pieces))
            if i:
                moving[s], pieces[s][-1] = lax.optimization_barrier((moving[s], pieces[s][-1]))
            pieces[s] += [moving[s], swap_cores(moving[s])]
    last = between(None, chips // 2 - 1, jnp.where(core == 0, moving[0], moving[1]), pieces)
    last = between(None, None, ring_step(last), pieces)
    for s, piece in enumerate(by_core(core, last, swap_cores(last))):
        pieces[s].append(piece)
    return pieces


def ring_order():
    chips = lax.axis_size("chip")
    place = place_of(lax.axis_index("chip"), chips)
    sign = 2 * lax.axis_index("core") - 1
    places = [place]
    for d in range(1, chips // 2):
        places += [place + sign * d, place - sign * d]
    places.append(place + chips // 2)
    return [chip_at(p, chips) for p in places]


def plus(a, b):
    return a.astype(jnp.float32) + b.astype(jnp.float32)


def reduce_rows():
    chips = lax.axis_size("chip")
    core = lax.axis_index("core")
    chip = lax.axis_index("chip")
    place = place_of(chip, chips)
    far = 2 * chip_at(place + chips // 2, chips)

    def way(side, sign):
        blocks = []
        for d in range(chips // 2 - 1, 0, -1):
            at = 2 * chip_at(place + sign * d, chips)
            blocks += [at, at + 1]
        return [far + side] + blocks[:2], blocks[2:] + [2 * chip + side]

    sign = 1 - 2 * core
    keep, give = way(core, sign), way(1 - core, -sign)
    return keep[0] + give[0], keep[1] + give[1]


def ring_reduce(keep, got, ready):
    core = lax.axis_index("core")
    group, groups = lax.axis_index(GROUP), lax.axis_size(GROUP)
    rows = keep[0].shape[0] // 3

    def cut(at, size, s):
        def one(parts):
            part, start = (parts[0], at) if at < 3 * rows else (parts[1], at - 3 * rows)
            half = part.shape[1] // STREAMS
            first = (group + 1 + s) % STREAMS if groups == STREAMS else s
            return lax.dynamic_slice(part, (start, first * half), (size, half))

        return plus(one(keep), one(got))

    moving = [ring_step(cut(0, rows, s).astype(jnp.bfloat16)) for s in range(STREAMS)]
    moving = [
        jnp.concatenate([jnp.where(core == 0, m, 0), jnp.where(core == 0, 0, m)], axis=0)
        for m in moving
    ]
    at, ahead = rows, ready
    total = 3 * rows + keep[1].shape[0]
    while at < total - rows:
        for s in range(STREAMS):
            if at > rows or s > 0:
                moving[s], _ = lax.optimization_barrier((moving[s], ahead))
            ahead = plus(cut(at, 2 * rows, s), moving[s]).astype(jnp.bfloat16)
            if at > rows and s == STREAMS - 1:
                ahead, ready = lax.optimization_barrier((ahead, ready))
            moving[s] = ring_step(ahead)
        at += 2 * rows
    sums = []
    for s in range(STREAMS):
        mine, theirs = by_core(core, moving[s][:rows], moving[s][rows:])
        sums.append(plus(cut(at, rows, s), plus(mine, swap_cores(theirs))))
    return sums


def stream(count, ahead, copy):
    for k in range(min(ahead, count)):
        copy(k).start()

    def ready(k):
        copy(k).wait()

        @pl.when(k + ahead < count)
        def _():
            copy(k + ahead).start()

    return ready


def project_kernel(steps, ahead, count, weight, *refs):
    pieces, (out, rows, held, piece_sems, weight_sems) = refs[:-5], refs[-5:]
    depth = held.shape[2]
    block, half = pieces[0].shape
    copies = []
    for i, piece in enumerate(pieces):
        at, s = i % count, i // count
        target = rows.at[pl.ds(at * block, block), pl.ds(s * half, half)]
        copies.append(pltpu.make_async_copy(piece, target, piece_sems.at[i]))
    for copy in copies:
        copy.start()

    def weight_copy(k):
        columns = pl.ds(pl.multiple_of(k * depth, depth), depth)
        slot = k % (ahead + 1)
        return pltpu.make_async_copy(weight.at[:, columns], held.at[slot], weight_sems.at[slot])

    ready = stream(steps, ahead, weight_copy)
    for copy in copies:
        copy.wait()
    out[...] = jnp.zeros_like(out)

    @pl.loop(0, steps)
    def _(k):
        ready(k)
        columns = pl.ds(pl.multiple_of(k * depth, depth), depth)
        out[...] += lax.dot_general(
            rows[:, columns], held[k % (ahead + 1)], NT, preferred_element_type=jnp.float32
        )


def project(pieces, weight, ahead, grant):
    count = len(pieces[0])
    rows, half = pieces[0][0].shape
    depth = STREAMS * half
    columns = weight.shape[0]
    steps = 8
    total = count * rows
    return pl.pallas_call(
        functools.partial(project_kernel, steps, ahead, count),
        out_shape=jax.ShapeDtypeStruct((total, columns), jnp.float32),
        in_specs=[ANY] * (1 + STREAMS * count),
        out_specs=IN_VMEM,
        scratch_shapes=[
            pltpu.VMEM((total, depth), jnp.bfloat16),
            pltpu.VMEM((ahead + 1, columns, depth // steps), jnp.bfloat16),
            pltpu.SemaphoreType.DMA((STREAMS * count,)),
            pltpu.SemaphoreType.DMA((ahead + 1,)),
        ],
        compiler_params=pltpu.CompilerParams(vmem_limit_bytes=grant),
        cost_estimate=pl.CostEstimate(
            flops=2 * total * depth * columns,
            bytes_accessed=2 * depth * (total + columns) + 4 * total * columns,
            transcendentals=0,
        ),
    )(weight, *[piece for part in pieces for piece in part])


def finish_kernel(count, meta, arrived, gain, router, *refs):
    parts, got, (out, stats) = refs[:count], refs[count : 2 * count], refs[2 * count :]
    chips, rows, columns = out.shape
    names = router.shape[0]
    core = meta[chips] % 2
    i = 0
    for part, other in zip(parts, got):
        for j in range(part.shape[0] // rows):
            at = meta[i]
            block = part[j * rows : (j + 1) * rows, :] + other[j * rows : (j + 1) * rows, :].astype(jnp.float32)
            hidden = arrived[at].astype(jnp.float32)
            hidden = jnp.where(core == 0, hidden[:, :columns], hidden[:, columns : 2 * columns])
            block = hidden + block
            scaled = (block * gain[...]).astype(jnp.bfloat16)
            out[at] = scaled
            stats[at, :, :names] = lax.dot_general(
                scaled, router[...], NT, preferred_element_type=jnp.float32
            )
            stats[at, :, names : names + 1] = jnp.sum(block * block, axis=1, keepdims=True)
            i += 1


def finish(meta, parts, got, arrived, gain, router):
    columns = parts[0].shape[1]
    chips, rows, _ = arrived.shape
    return pl.pallas_call(
        functools.partial(finish_kernel, len(parts)),
        out_shape=(
            jax.ShapeDtypeStruct((chips, rows, columns), jnp.bfloat16),
            jax.ShapeDtypeStruct((chips, rows, router.shape[0] + 1), jnp.float32),
        ),
        in_specs=[IN_SMEM] + [IN_VMEM] * (3 + 2 * len(parts)),
        out_specs=(IN_VMEM, IN_VMEM),
        compiler_params=pltpu.CompilerParams(vmem_limit_bytes=16 * 1024 * 1024),
    )(meta, arrived, gain, router, *parts, *got)


def own_kernel(count, meta, *refs):
    pieces, (out, sems) = refs[:-2], refs[-2:]
    chips, share, _ = out.shape
    half = chips * share
    place = meta[chips]
    for s in range(STREAMS):

        @pl.when(place * share // half == s)
        def _():
            at = pl.ds(pl.multiple_of(place * share - s * half, share), share)
            copies = [
                pltpu.make_async_copy(pieces[s * count + i].at[at, :], out.at[meta[i]], sems.at[i])
                for i in range(count)
            ]
            for copy in copies:
                copy.start()
            for copy in copies:
                copy.wait()


def own_residual(meta, pieces, share):
    chips = len(pieces[0])
    depth = pieces[0][0].shape[1]
    return pl.pallas_call(
        functools.partial(own_kernel, chips),
        out_shape=jax.ShapeDtypeStruct((chips, share, depth), jnp.bfloat16),
        in_specs=[IN_SMEM] + [ANY] * (STREAMS * chips),
        out_specs=IN_VMEM,
        scratch_shapes=[pltpu.SemaphoreType.DMA((chips,))],
        compiler_params=pltpu.CompilerParams(vmem_limit_bytes=VMEM),
    )(meta, *[piece for part in pieces for piece in part])


def piece_starts(pieces, count, held, sems):
    half = held.shape[1] // STREAMS
    for i in range(count):
        for s in range(STREAMS):
            target = held.at[i, pl.ds(s * half, half), :]
            source = pieces[s * count + i].at[pl.ds(0, half), :]
            pltpu.make_async_copy(source, target, sems.at[i]).start()


def weight_start(at, gate_up, depth, per, target, sem):
    for p, part in enumerate(gate_up):

        @pl.when(at // per == p)
        def _():
            span = pl.ds(pl.multiple_of(at % per * depth, 16), depth)
            pltpu.make_async_copy(part.at[span, :], target, sem).start()


def wait_for(ref, sem):
    pltpu.make_async_copy(ref, ref, sem).wait()


def gate_kernel(parts, first, count, chips, meta, *refs):
    gate_up, pieces = refs[:parts], refs[parts:-5]
    total, held, weight, piece_sems, weight_sems = refs[-5:]
    depth = held.shape[2]
    for k in range(count):
        weight_start(
            meta[first + k], gate_up, depth, chips // parts, weight.at[k], weight_sems.at[k]
        )
        if k == 0:
            piece_starts(pieces, count, held, piece_sems)

    total[...] = jnp.zeros_like(total)

    @pl.loop(0, count)
    def _(k):
        wait_for(held.at[k], piece_sems.at[k])
        wait_for(weight.at[k], weight_sems.at[k])
        for at in range(0, total.shape[1], 256):
            total[:, at : at + 256] += jnp.dot(
                held[k], weight[k, :, at : at + 256], preferred_element_type=jnp.float32
            )


def gate(meta, first, pieces, rows, gate_up, chips):
    count = len(pieces[0])
    depth = pieces[0][0].shape[1]
    wide = gate_up[0].shape[1]
    return pl.pallas_call(
        functools.partial(gate_kernel, len(gate_up), first, count, chips),
        out_shape=jax.ShapeDtypeStruct((rows, wide), jnp.float32),
        in_specs=[IN_SMEM] + [IN_HBM] * len(gate_up) + [ANY] * (STREAMS * count),
        out_specs=IN_VMEM,
        scratch_shapes=[
            pltpu.VMEM((count, rows, depth), jnp.bfloat16),
            pltpu.VMEM((count, depth, wide), jnp.bfloat16),
            pltpu.SemaphoreType.DMA((count,)),
            pltpu.SemaphoreType.DMA((count,)),
        ],
        compiler_params=pltpu.CompilerParams(vmem_limit_bytes=VMEM),
        cost_estimate=pl.CostEstimate(
            flops=2 * rows * count * depth * wide,
            bytes_accessed=2 * count * depth * (wide + rows),
            transcendentals=0,
        ),
    )(meta, *gate_up, *[piece for part in pieces for piece in part])


def tail_kernel(parts, first, count, chips, meta, norm, scale, before, down, *refs):
    gate_up, pieces = refs[:parts], refs[parts : parts + STREAMS * count]
    rest = refs[parts + STREAMS * count :]
    outs = rest[:4]
    held, weight, total, earlier, active, ordered, second, staged = rest[4:12]
    piece_sems, weight_sems, earlier_sem, second_sems, out_sems = rest[12:]
    rows, depth = held.shape[1:]
    hidden = active.shape[1]
    steps, _, span = second.shape
    for k in range(count):
        weight_start(
            meta[first + k], gate_up, depth, chips // parts, weight.at[k], weight_sems.at[k]
        )
        if k == 0:
            piece_starts(pieces, count, held, piece_sems)
    pltpu.make_async_copy(before, earlier, earlier_sem).start()

    def columns(n):
        return pl.ds(pl.multiple_of(n * span, span), span)

    @pl.loop(0, steps)
    def _(n):
        pltpu.make_async_copy(down.at[:, columns(n)], second.at[n], second_sems.at[n]).start()

    total[...] = jnp.zeros_like(total)

    @pl.loop(0, count)
    def _(k):
        wait_for(held.at[k], piece_sems.at[k])
        wait_for(weight.at[k], weight_sems.at[k])
        for at in range(0, total.shape[1], 256):
            total[:, at : at + 256] += jnp.dot(
                held[k], weight[k, :, at : at + 256], preferred_element_type=jnp.float32
            )

    pltpu.make_async_copy(before, earlier, earlier_sem).wait()
    gate = (total[:, :hidden] + earlier[:, :hidden]) * norm[...]
    up = (total[:, hidden:] + earlier[:, hidden:]) * (norm[...] * scale[...])
    active[...] = (gate * jax.nn.sigmoid(gate) * up).astype(jnp.bfloat16)
    share = rows // (2 * chips)
    for i in range(2 * chips):
        at = pl.ds(pl.multiple_of(meta[chips + 1 + i] * share, share), share)
        ordered[i * share : (i + 1) * share, :] = active[at, :]

    def out_copies(n):
        copies, at = [], 0
        slot = n % 2
        for i, out in enumerate(outs):
            size = out.shape[0]
            source = staged.at[slot, pl.ds(at, size), :]
            copies.append(
                pltpu.make_async_copy(source, out.at[:, columns(n)], out_sems.at[slot, i])
            )
            at += size
        return copies

    @pl.loop(0, steps)
    def _(n):
        pltpu.make_async_copy(down.at[:, columns(n)], second.at[n], second_sems.at[n]).wait()

        @pl.when(n >= 2)
        def _():
            for copy in out_copies(n - 2):
                copy.wait()

        result = jnp.dot(ordered[...], second[n], preferred_element_type=jnp.float32)
        staged[n % 2] = result.astype(jnp.bfloat16)
        for copy in out_copies(n):
            copy.start()

    for n in range(max(0, steps - 2), steps):
        for copy in out_copies(n):
            copy.wait()


def tail(meta, first, pieces, rows, gate_up, before, norm, scale, down, chips):
    count = len(pieces[0])
    depth = pieces[0][0].shape[1]
    wide = gate_up[0].shape[1]
    hidden, width = down.shape
    share = rows // (2 * chips)
    steps = max(1, width // 1024)
    shapes = [3 * share, 3 * share, rows // 2 - 3 * share, rows // 2 - 3 * share]
    return pl.pallas_call(
        functools.partial(tail_kernel, len(gate_up), first, count, chips),
        out_shape=tuple(jax.ShapeDtypeStruct((n, width), jnp.bfloat16) for n in shapes),
        in_specs=[IN_SMEM, IN_VMEM, IN_VMEM, ANY, IN_HBM]
        + [IN_HBM] * len(gate_up)
        + [ANY] * (STREAMS * count),
        out_specs=(ANY,) * 4,
        scratch_shapes=[
            pltpu.VMEM((count, rows, depth), jnp.bfloat16),
            pltpu.VMEM((count, depth, wide), jnp.bfloat16),
            pltpu.VMEM((rows, wide), jnp.float32),
            pltpu.VMEM((rows, wide), jnp.float32),
            pltpu.VMEM((rows, hidden), jnp.bfloat16),
            pltpu.VMEM((rows, hidden), jnp.bfloat16),
            pltpu.VMEM((steps, hidden, width // steps), jnp.bfloat16),
            pltpu.VMEM((2, rows, width // steps), jnp.bfloat16),
            pltpu.SemaphoreType.DMA((count,)),
            pltpu.SemaphoreType.DMA((count,)),
            pltpu.SemaphoreType.DMA(()),
            pltpu.SemaphoreType.DMA((steps,)),
            pltpu.SemaphoreType.DMA((2, 4)),
        ],
        compiler_params=pltpu.CompilerParams(vmem_limit_bytes=VMEM),
        cost_estimate=pl.CostEstimate(
            flops=2 * rows * (count * depth * wide + hidden * width),
            bytes_accessed=2 * (count * depth * (wide + rows) + width * (hidden + rows)),
            transcendentals=rows * wide,
        ),
    )(meta, norm, scale, before, down, *gate_up, *[piece for part in pieces for piece in part])


def body(
    hidden_in,
    queries,
    latent_cache,
    new_latent,
    cache_lengths,
    value_up,
    out_proj,
    norm_gain,
    router,
    expert_ids,
    w_gate_up,
    w_down,
):
    rows = hidden_in.shape[0]
    width = hidden_in.shape[1]
    chips = lax.axis_size("chip")
    cores = lax.axis_size("core")
    groups = lax.axis_size(GROUP)
    core = lax.axis_index("core")
    chip = lax.axis_index("chip")
    group = lax.axis_index(GROUP)
    place = chip * cores + core
    chip_cols = width // chips
    own_cols = chip_cols // cores
    expert_count = router.shape[1]
    total = chips * cores * rows
    order = ring_order()

    outgoing = hidden_in.reshape(rows, chips, chip_cols).transpose(1, 0, 2)
    names = jnp.broadcast_to(expert_ids.astype(jnp.bfloat16)[None], (chips, rows, TOP))
    arrived = lax.all_to_all(
        jnp.concatenate([outgoing, names], axis=2), "chip", split_axis=0, concat_axis=0, tiled=True
    )

    parts = 4
    span = width // parts
    gate_up = []
    stages = [None, (0, 0), (1, 0), (0, 1)]
    final = chips // 2 - 1
    ends = [(1, 1), (0, 2), (1, 2), (None, final)]
    projected = []

    def during_first(s, i, moving, pieces):
        if i is None:
            part = project([piece[: chips - 1] for piece in pieces], out_proj.T, 2, 20 * 1024 * 1024)
            moving, part = lax.optimization_barrier((moving, part))
            projected.append(part)
        if (s, i) in ends:
            p = ends.index((s, i))
            raw = w_gate_up
            if stages[p] is not None:
                raw, _ = lax.optimization_barrier((raw, pieces[stages[p][0]][1 + 2 * stages[p][1]]))
            quarter = raw[0, p * span : (p + 1) * span].reshape(span, -1)
            moving, quarter = lax.optimization_barrier((moving, quarter))
            gate_up.append(quarter)
        return moving

    own_gain = lax.dynamic_slice_in_dim(norm_gain, place * own_cols, own_cols, 0)[None]
    own_router = lax.dynamic_slice_in_dim(router.T, place * own_cols, own_cols, 1)
    first_rows, then_rows = reduce_rows()
    meta = jnp.stack(order + [place] + first_rows + then_rows).astype(jnp.int32)

    head_out = attend(queries, latent_cache, new_latent, cache_lengths, value_up)
    head_out, arrived = lax.optimization_barrier((head_out, arrived))
    other_arrived = swap_cores(arrived)
    low, high = by_core(core, head_out, swap_cores(head_out))
    block = jnp.concatenate([low, high], axis=0)
    half = block.shape[1] // STREAMS
    pieces = ring_gather([block[:, s * half : (s + 1) * half] for s in range(STREAMS)], during_first)
    projected.append(project([piece[chips - 1 :] for piece in pieces], out_proj.T, 8, VMEM))
    parts, got = [], []
    for part in projected:
        if groups == 2:
            parts.append(part)
            got.append(lax.ppermute(part.astype(jnp.bfloat16), "sec", SWAP))
        else:
            parts.append(lax.psum(part, GROUP))
            got.append(jnp.zeros(part.shape, jnp.bfloat16))
    arrived = jnp.stack(by_core(core, arrived, other_arrived), axis=1)
    arrived = arrived.reshape(chips, cores * rows, chip_cols + TOP)
    residual, stats = finish(meta, parts, got, arrived, own_gain, own_router)
    residual = residual.reshape(total, own_cols)
    stats = stats.reshape(total, expert_count + 1).T
    stats = stats + swap_cores(stats)
    low, high = by_core(core, residual, swap_cores(residual))
    block = jnp.concatenate([low, high], axis=1)
    half = total // STREAMS

    ids = arrived[:, :, chip_cols:].reshape(total, TOP).T.astype(jnp.int32)
    grid = lax.broadcasted_iota(jnp.int32, (1, expert_count, 1), 1)
    chosen = jnp.any(ids[:, None, :] == grid, axis=0)

    def packed(sums):
        high = lax.reduce_precision(sums, 8, 7)
        flat = jnp.stack([high, sums - high]).astype(jnp.bfloat16).reshape(-1)
        extra = -(-flat.size // (16 * chip_cols)) * 16
        return jnp.pad(flat, (0, extra * chip_cols - flat.size)).reshape(extra, chip_cols)

    def unpacked(pieces):
        count = expert_count + 1
        added = sum(piece[half:].astype(jnp.float32) for piece in pieces).reshape(-1)
        return jnp.sum(added[: 2 * count * half].reshape(2, count, half), axis=0)

    blocks = []
    for s in range(STREAMS):
        span = slice(s * half, (s + 1) * half)
        blocks.append(jnp.concatenate([block[span], packed(stats[:, span])], axis=0))

    def route(stats):
        norm = lax.rsqrt(stats[expert_count:] / width + norm_epsilon)
        affinity = jnp.where(chosen, jax.nn.sigmoid(stats[:expert_count] * norm), 0.0)
        scale = jnp.sum(jnp.where(grid[0] == place, affinity, 0.0), axis=0, keepdims=True)
        scale = route_scale * scale / jnp.sum(affinity, axis=0, keepdims=True)
        return norm.T, scale.T

    sums = []
    def during_second(s, i, moving, pieces):
        if (s, i) == (None, final):
            moving, sums[0] = lax.optimization_barrier((moving, sums[0]))
        if (s, i) == (STREAMS - 1, final - 1):
            blocks = [piece[: chips - 3] for piece in pieces]
            blocks, moving = lax.optimization_barrier((blocks, moving))
            sums.append(gate(meta, 0, blocks, total, gate_up, chips))
        return moving

    pieces = ring_gather(blocks, during_second)
    stats = jnp.concatenate([unpacked(part) for part in pieces], axis=1)
    keep_first, give_first, keep_then, give_then = tail(
        meta,
        chips - 3,
        [piece[chips - 3 :] for piece in pieces],
        total,
        gate_up,
        sums[0],
        *route(stats),
        w_down[0],
        chips,
    )

    got = [swap_cores(give_first), swap_cores(give_then)]
    pieces, _ = lax.optimization_barrier((pieces, got[0]))
    own = own_residual(meta, pieces, rows).reshape(groups, chips // groups, rows, chip_cols)
    own = lax.dynamic_index_in_dim(own, group, 0, keepdims=False)
    own = own.transpose(1, 0, 2).reshape(rows, width // groups).astype(jnp.float32)
    own = own / lax.dynamic_slice_in_dim(norm_gain, group * (width // groups), width // groups, 0)

    mixture = ring_reduce([keep_first, keep_then], got, own)
    if groups == 2:
        mixture = plus(mixture[1], lax.ppermute(mixture[0].astype(jnp.bfloat16), "sec", SWAP))
    else:
        mixture = jnp.concatenate(mixture, axis=1).reshape(rows, groups, width // groups)
        mixture = lax.psum_scatter(mixture, GROUP, scatter_dimension=1, tiled=False)
    return plus(own, mixture).astype(jnp.bfloat16)


def solution(mesh):
    sec, batch, head = mesh.shape["sec"], mesh.shape["batch"], mesh.shape["head"]
    devices = mesh.devices.reshape(sec, batch // 2, 2, head)
    split = Mesh(devices, ("sec", "chip", "core", "head"))
    tokens = ("chip", "core")
    in_specs = (
        P(tokens, None),
        P(tokens, GROUP, None),
        P(tokens, None, None),
        P(tokens, None),
        P(tokens),
        P(GROUP, None, None),
        P(GROUP, tokens),
        P(),
        P(),
        P(tokens, None),
        P(tokens, None, None, GROUP),
        P(tokens, GROUP, None),
    )
    out_specs = P(tokens, GROUP)
    return jax.shard_map(body, mesh=split, in_specs=in_specs, out_specs=out_specs, check_vma=False)
```

```python
import functools

import jax
import jax.numpy as jnp
from jax import lax
from jax.experimental import pallas as pl
from jax.experimental.pallas import tpu as pltpu
from jax.sharding import Mesh, PartitionSpec as P

QKD = 192
TOP = 8

norm_epsilon = 1e-06
route_scale = 2.5

GROUP = ("sec", "head")
SWAP = [(0, 1), (1, 0)]
STREAMS = 2
VMEM = 56 * 1024 * 1024
NT = (((1,), (1,)), ((), ()))
ANY = pl.BlockSpec(memory_space=pl.ANY)
IN_HBM = pl.BlockSpec(memory_space=pltpu.HBM)
IN_VMEM = pl.BlockSpec(memory_space=pltpu.VMEM)
IN_SMEM = pl.BlockSpec(memory_space=pltpu.SMEM)


def attend(queries, latent_cache, new_latent, cache_lengths, value_up):
    row_count = queries.shape[0]
    latent_width = value_up.shape[1]
    cache_depth = latent_cache.shape[1]
    score_scale = QKD ** (-0.5)
    scores = (
        jnp.einsum("thk,tjk->thj", queries, latent_cache, preferred_element_type=jnp.float32)
        * score_scale
    )
    own_score = (
        jnp.einsum("thk,tk->th", queries, new_latent, preferred_element_type=jnp.float32)
        * score_scale
    )
    positions = lax.broadcasted_iota(jnp.int32, (1, 1, cache_depth), 2)
    in_cache = positions < cache_lengths[:, None, None]
    scores = jnp.where(in_cache, scores, -jnp.inf)
    top_score = jnp.maximum(jnp.max(scores, axis=2), own_score)
    cache_exp = jnp.exp(scores - top_score[:, :, None])
    own_exp = jnp.exp(own_score - top_score)
    softmax_sum = jnp.sum(cache_exp, axis=2) + own_exp
    cache_weights = (cache_exp / softmax_sum[:, :, None]).astype(jnp.bfloat16)
    own_weights = (own_exp / softmax_sum).astype(jnp.bfloat16)
    latent_out = jnp.einsum(
        "thj,tjc->thc",
        cache_weights,
        latent_cache[:, :, :latent_width],
        preferred_element_type=jnp.float32,
    )
    latent_out = latent_out + own_weights.astype(jnp.float32)[:, :, None] * new_latent[
        :, None, :latent_width
    ].astype(jnp.float32)
    latent_out = latent_out.astype(jnp.bfloat16)
    head_out = jnp.einsum(
        "thc,hcd->thd", latent_out, value_up, preferred_element_type=jnp.float32
    ).astype(jnp.bfloat16)
    return head_out.reshape(row_count, -1)


def place_of(chip, chips):
    return jnp.where(chip % 2 == 0, chip // 2, chips - 1 - chip // 2)


def chip_at(place, chips):
    place = place % chips
    return jnp.where(place < chips // 2, 2 * place, 2 * (chips - 1 - place) + 1)


def ring_step(block):
    chips = lax.axis_size("chip")
    ring = list(range(0, chips, 2)) + list(range(chips - 1, 0, -2))
    pairs = []
    for i in range(chips):
        here, there = ring[i], ring[(i + 1) % chips]
        pairs += [(2 * here, 2 * there), (2 * there + 1, 2 * here + 1)]
    return lax.ppermute(block, ("chip", "core"), pairs)


def swap_cores(block):
    return lax.ppermute(block, "core", SWAP)


def by_core(core, first, second):
    return jnp.where(core == 0, first, second), jnp.where(core == 0, second, first)


def ring_gather(blocks, between):
    chips = lax.axis_size("chip")
    core = lax.axis_index("core")
    pieces, moving = [[block] for block in blocks], list(blocks)
    for i in range(chips // 2 - 1):
        for s in range(STREAMS):
            moving[s] = ring_step(between(s, i, moving[s], pieces))
            if i < chips // 2 - 2:
                pieces[s] += [moving[s], swap_cores(moving[s])]
    moving = between(STREAMS - 1, None, moving, pieces)
    for s in range(STREAMS):
        pieces[s] += [moving[s], swap_cores(moving[s])]
    last = between(None, chips // 2 - 1, jnp.where(core == 0, moving[0], moving[1]), pieces)
    last = between(None, None, ring_step(last), pieces)
    for s, piece in enumerate(by_core(core, last, swap_cores(last))):
        pieces[s].append(piece)
    return pieces


def ring_order():
    chips = lax.axis_size("chip")
    place = place_of(lax.axis_index("chip"), chips)
    sign = 2 * lax.axis_index("core") - 1
    places = [place]
    for d in range(1, chips // 2):
        places += [place + sign * d, place - sign * d]
    places.append(place + chips // 2)
    return [chip_at(p, chips) for p in places]


def plus(a, b):
    return a.astype(jnp.float32) + b.astype(jnp.float32)


def reduce_rows():
    chips = lax.axis_size("chip")
    core = lax.axis_index("core")
    chip = lax.axis_index("chip")
    place = place_of(chip, chips)
    far = 2 * chip_at(place + chips // 2, chips)

    def way(side, sign):
        blocks = []
        for d in range(chips // 2 - 1, 0, -1):
            at = 2 * chip_at(place + sign * d, chips)
            blocks += [at, at + 1]
        return [far + side] + blocks[:2], blocks[2:] + [2 * chip + side]

    sign = 1 - 2 * core
    keep, give = way(core, sign), way(1 - core, -sign)
    return keep[0] + give[0], keep[1] + give[1]


def ring_reduce(keep, got, between):
    core = lax.axis_index("core")
    group, groups = lax.axis_index(GROUP), lax.axis_size(GROUP)
    rows = keep[0].shape[0] // 3

    def cut(at, size, s):
        def one(parts):
            part, start = (parts[0], at) if at < 3 * rows else (parts[1], at - 3 * rows)
            half = part.shape[1] // STREAMS
            first = (group + 1 + s) % STREAMS if groups == STREAMS else s
            return lax.dynamic_slice(part, (start, first * half), (size, half))

        return plus(one(keep), one(got))

    moving = [ring_step(cut(0, rows, s).astype(jnp.bfloat16)) for s in range(STREAMS)]
    moving = [
        jnp.concatenate([jnp.where(core == 0, m, 0), jnp.where(core == 0, 0, m)], axis=0)
        for m in moving
    ]
    at, ahead, ready = rows, None, None
    total = 3 * rows + keep[1].shape[0]
    while at < total - rows:
        for s in range(STREAMS):
            if ahead is not None:
                moving[s], _ = lax.optimization_barrier((moving[s], ahead))
            ahead = plus(cut(at, 2 * rows, s), moving[s]).astype(jnp.bfloat16)
            if at == rows and s == STREAMS - 1:
                ready = between(ahead)
            if at > rows and s == STREAMS - 1:
                ahead, ready = lax.optimization_barrier((ahead, ready))
            moving[s] = ring_step(ahead)
        at += 2 * rows
    sums = []
    for s in range(STREAMS):
        if sums:
            moving[s], _ = lax.optimization_barrier((moving[s], sums[0]))
        mine, theirs = by_core(core, moving[s][:rows], moving[s][rows:])
        added = plus(cut(at, rows, s), plus(mine, swap_cores(theirs)))
        if groups == STREAMS and s == 0:
            added = lax.ppermute(added.astype(jnp.bfloat16), "sec", SWAP)
        sums.append(added)
    return sums, ready


def stream(count, ahead, copy):
    for k in range(min(ahead, count)):
        copy(k).start()

    def ready(k):
        copy(k).wait()

        @pl.when(k + ahead < count)
        def _():
            copy(k + ahead).start()

    return ready


def project_kernel(steps, ahead, count, weight, *refs):
    pieces, (out, rows, held, turned, piece_sems, weight_sems) = refs[:-6], refs[-6:]
    few = out.shape[0] <= 128
    depth = held.shape[2]
    block, half = pieces[0].shape
    copies = []
    for i, piece in enumerate(pieces):
        at, s = i % count, i // count
        target = rows.at[pl.ds(at * block, block), pl.ds(s * half, half)]
        copies.append(pltpu.make_async_copy(piece, target, piece_sems.at[i]))
    for copy in copies:
        copy.start()

    def weight_copy(k):
        columns = pl.ds(pl.multiple_of(k * depth, depth), depth)
        slot = k % (ahead + 1)
        return pltpu.make_async_copy(weight.at[:, columns], held.at[slot], weight_sems.at[slot])

    ready = stream(steps, ahead, weight_copy)
    for copy in copies:
        copy.wait()
    total = turned if few else out
    total[...] = jnp.zeros_like(total)

    @pl.loop(0, steps)
    def _(k):
        ready(k)
        columns = pl.ds(pl.multiple_of(k * depth, depth), depth)
        left, right = rows[:, columns], held[k % (ahead + 1)]
        if few:
            left, right = right, left
        total[...] += lax.dot_general(left, right, NT, preferred_element_type=jnp.float32)

    if few:
        out[...] = turned[...].T


def project(pieces, weight, ahead, grant):
    count = len(pieces[0])
    rows, half = pieces[0][0].shape
    depth = STREAMS * half
    columns = weight.shape[0]
    steps = 8
    total = count * rows
    return pl.pallas_call(
        functools.partial(project_kernel, steps, ahead, count),
        out_shape=jax.ShapeDtypeStruct((total, columns), jnp.float32),
        in_specs=[ANY] * (1 + STREAMS * count),
        out_specs=IN_VMEM,
        scratch_shapes=[
            pltpu.VMEM((total, depth), jnp.bfloat16),
            pltpu.VMEM((ahead + 1, columns, depth // steps), jnp.bfloat16),
            pltpu.VMEM((columns, total) if total <= 128 else (8, 128), jnp.float32),
            pltpu.SemaphoreType.DMA((STREAMS * count,)),
            pltpu.SemaphoreType.DMA((ahead + 1,)),
        ],
        compiler_params=pltpu.CompilerParams(vmem_limit_bytes=grant),
        cost_estimate=pl.CostEstimate(
            flops=2 * total * depth * columns,
            bytes_accessed=2 * depth * (total + columns) + 4 * total * columns,
            transcendentals=0,
        ),
    )(weight, *[piece for part in pieces for piece in part])


def finish_kernel(count, meta, arrived, gain, router, *refs):
    parts, got, (out, stats) = refs[:count], refs[count : 2 * count], refs[2 * count :]
    chips, rows, columns = out.shape
    names = router.shape[0]
    core = meta[chips] % 2
    i = 0
    for part, other in zip(parts, got):
        for j in range(part.shape[0] // rows):
            at = meta[i]
            block = part[j * rows : (j + 1) * rows, :] + other[j * rows : (j + 1) * rows, :].astype(jnp.float32)
            hidden = arrived[at].astype(jnp.float32)
            hidden = jnp.where(core == 0, hidden[:, :columns], hidden[:, columns : 2 * columns])
            block = hidden + block
            scaled = (block * gain[...]).astype(jnp.bfloat16)
            out[at] = scaled
            stats[at, :, :names] = lax.dot_general(
                scaled, router[...], NT, preferred_element_type=jnp.float32
            )
            stats[at, :, names : names + 1] = jnp.sum(block * block, axis=1, keepdims=True)
            i += 1


def finish(meta, parts, got, arrived, gain, router):
    columns = parts[0].shape[1]
    chips, rows, _ = arrived.shape
    return pl.pallas_call(
        functools.partial(finish_kernel, len(parts)),
        out_shape=(
            jax.ShapeDtypeStruct((chips, rows, columns), jnp.bfloat16),
            jax.ShapeDtypeStruct((chips, rows, router.shape[0] + 1), jnp.float32),
        ),
        in_specs=[IN_SMEM] + [IN_VMEM] * (3 + 2 * len(parts)),
        out_specs=(IN_VMEM, IN_VMEM),
        compiler_params=pltpu.CompilerParams(vmem_limit_bytes=16 * 1024 * 1024),
    )(meta, arrived, gain, router, *parts, *got)


def own_kernel(count, meta, *refs):
    pieces, (out, sems) = refs[:-2], refs[-2:]
    chips, share, _ = out.shape
    half = chips * share
    place = meta[chips]
    for s in range(STREAMS):

        @pl.when(place * share // half == s)
        def _():
            at = pl.ds(pl.multiple_of(place * share - s * half, share), share)
            copies = [
                pltpu.make_async_copy(pieces[s * count + i].at[at, :], out.at[meta[i]], sems.at[i])
                for i in range(count)
            ]
            for copy in copies:
                copy.start()
            for copy in copies:
                copy.wait()


def own_residual(meta, pieces, share):
    chips = len(pieces[0])
    depth = pieces[0][0].shape[1]
    return pl.pallas_call(
        functools.partial(own_kernel, chips),
        out_shape=jax.ShapeDtypeStruct((chips, share, depth), jnp.bfloat16),
        in_specs=[IN_SMEM] + [ANY] * (STREAMS * chips),
        out_specs=IN_VMEM,
        scratch_shapes=[pltpu.SemaphoreType.DMA((chips,))],
        compiler_params=pltpu.CompilerParams(vmem_limit_bytes=VMEM),
    )(meta, *[piece for part in pieces for piece in part])


def piece_starts(pieces, count, held, sems):
    half = held.shape[1] // STREAMS
    depth = pieces[0].shape[1]
    for i in range(count):
        for s in range(STREAMS):
            at = i // (held.shape[2] // depth)
            target = held.at[at, pl.ds(s * half, half), :]
            if held.shape[2] != depth:
                target = target.at[:, pl.ds(i % 2 * depth, depth)]
            source = pieces[s * count + i].at[pl.ds(0, half), :]
            pltpu.make_async_copy(source, target, sems.at[i]).start()


def add_products(count, depth, held, weight, total, piece_sems, weight_sems):
    per = held.shape[2] // depth

    def ready(k, at):
        block = held.at[k] if per == 1 else held.at[k, :, pl.ds(at * depth, depth)]
        wait_for(block, piece_sems.at[per * k + at])
        wait_for(weight.at[k, pl.ds(at * depth, depth), :], weight_sems.at[per * k + at])

    def add(k, deep):
        for at in range(0, total.shape[1], 256):
            total[:, at : at + 256] += jnp.dot(
                held[k, :, :deep],
                weight[k, :deep, at : at + 256],
                preferred_element_type=jnp.float32,
            )

    total[...] = jnp.zeros_like(total)

    @pl.loop(0, count // per)
    def _(k):
        for at in range(per):
            ready(k, at)
        add(k, per * depth)

    if count % per:
        ready(count // per, 0)
        add(count // per, depth)


def weight_start(at, gate_up, depth, per, target, sem):
    for p, part in enumerate(gate_up):

        @pl.when(at // per == p)
        def _():
            span = pl.ds(pl.multiple_of(at % per * depth, 16), depth)
            pltpu.make_async_copy(part.at[span, :], target, sem).start()


def wait_for(ref, sem):
    pltpu.make_async_copy(ref, ref, sem).wait()


def gate_kernel(parts, first, count, chips, meta, *refs):
    gate_up, pieces = refs[:parts], refs[parts:-5]
    total, held, weight, piece_sems, weight_sems = refs[-5:]
    depth = pieces[0].shape[1]
    for k in range(count):
        side = held.shape[2] // depth
        target = weight.at[k // side, pl.ds(k % side * depth, depth), :]
        weight_start(meta[first + k], gate_up, depth, chips // parts, target, weight_sems.at[k])
        if k == 0:
            piece_starts(pieces, count, held, piece_sems)

    add_products(count, depth, held, weight, total, piece_sems, weight_sems)


def gate(meta, first, pieces, rows, gate_up, chips):
    count = len(pieces[0])
    depth = pieces[0][0].shape[1]
    side = 1 if depth % 128 else 2
    wide = gate_up[0].shape[1]
    return pl.pallas_call(
        functools.partial(gate_kernel, len(gate_up), first, count, chips),
        out_shape=jax.ShapeDtypeStruct((rows, wide), jnp.float32),
        in_specs=[IN_SMEM] + [IN_HBM] * len(gate_up) + [ANY] * (STREAMS * count),
        out_specs=IN_VMEM,
        scratch_shapes=[
            pltpu.VMEM((-(-count // side), rows, side * depth), jnp.bfloat16),
            pltpu.VMEM((-(-count // side), side * depth, wide), jnp.bfloat16),
            pltpu.SemaphoreType.DMA((count,)),
            pltpu.SemaphoreType.DMA((count,)),
        ],
        compiler_params=pltpu.CompilerParams(vmem_limit_bytes=VMEM),
        cost_estimate=pl.CostEstimate(
            flops=2 * rows * count * depth * wide,
            bytes_accessed=2 * count * depth * (wide + rows),
            transcendentals=0,
        ),
    )(meta, *gate_up, *[piece for part in pieces for piece in part])


def tail_kernel(parts, first, count, chips, meta, factors, before, down, *refs):
    gate_up, pieces = refs[:parts], refs[parts : parts + STREAMS * count]
    rest = refs[parts + STREAMS * count :]
    outs = rest[:4]
    held, weight, total, earlier, active, ordered, second, staged = rest[4:12]
    piece_sems, weight_sems, earlier_sem, second_sems, out_sems = rest[12:]
    rows = held.shape[1]
    depth = pieces[0].shape[1]
    hidden = active.shape[1]
    steps, _, span = second.shape
    for k in range(count):
        side = held.shape[2] // depth
        target = weight.at[k // side, pl.ds(k % side * depth, depth), :]
        weight_start(meta[first + k], gate_up, depth, chips // parts, target, weight_sems.at[k])
        if k == 0:
            piece_starts(pieces, count, held, piece_sems)
    pltpu.make_async_copy(before, earlier, earlier_sem).start()

    def columns(n):
        return pl.ds(pl.multiple_of(n * span, span), span)

    @pl.loop(0, steps)
    def _(n):
        pltpu.make_async_copy(down.at[:, columns(n)], second.at[n], second_sems.at[n]).start()

    add_products(count, depth, held, weight, total, piece_sems, weight_sems)

    pltpu.make_async_copy(before, earlier, earlier_sem).wait()
    columns_of = jnp.concatenate([factors[...], jnp.zeros((6, rows), jnp.float32)], axis=0).T
    norm, scale = columns_of[:, 0:1], columns_of[:, 1:2]
    gate = (total[:, :hidden] + earlier[:, :hidden]) * norm
    up = (total[:, hidden:] + earlier[:, hidden:]) * (norm * scale)
    active[...] = (gate * jax.nn.sigmoid(gate) * up).astype(jnp.bfloat16)
    share = rows // (2 * chips)
    for i in range(2 * chips):
        at = pl.ds(pl.multiple_of(meta[chips + 1 + i] * share, share), share)
        ordered[i * share : (i + 1) * share, :] = active[at, :]

    def out_copies(n):
        copies, at = [], 0
        slot = n % 2
        for i, out in enumerate(outs):
            size = out.shape[0]
            source = staged.at[slot, pl.ds(at, size), :]
            copies.append(
                pltpu.make_async_copy(source, out.at[:, columns(n)], out_sems.at[slot, i])
            )
            at += size
        return copies

    @pl.loop(0, steps)
    def _(n):
        pltpu.make_async_copy(down.at[:, columns(n)], second.at[n], second_sems.at[n]).wait()

        @pl.when(n >= 2)
        def _():
            for copy in out_copies(n - 2):
                copy.wait()

        result = jnp.dot(ordered[...], second[n], preferred_element_type=jnp.float32)
        staged[n % 2] = result.astype(jnp.bfloat16)
        for copy in out_copies(n):
            copy.start()

    for n in range(max(0, steps - 2), steps):
        for copy in out_copies(n):
            copy.wait()


def tail(meta, first, pieces, rows, gate_up, before, factors, down, chips):
    count = len(pieces[0])
    depth = pieces[0][0].shape[1]
    side = 1 if depth % 128 else 2
    wide = gate_up[0].shape[1]
    hidden, width = down.shape
    share = rows // (2 * chips)
    steps = max(1, width // 1024)
    shapes = [3 * share, 3 * share, rows // 2 - 3 * share, rows // 2 - 3 * share]
    return pl.pallas_call(
        functools.partial(tail_kernel, len(gate_up), first, count, chips),
        out_shape=tuple(jax.ShapeDtypeStruct((n, width), jnp.bfloat16) for n in shapes),
        in_specs=[IN_SMEM, IN_VMEM, ANY, IN_HBM]
        + [IN_HBM] * len(gate_up)
        + [ANY] * (STREAMS * count),
        out_specs=(ANY,) * 4,
        scratch_shapes=[
            pltpu.VMEM((-(-count // side), rows, side * depth), jnp.bfloat16),
            pltpu.VMEM((-(-count // side), side * depth, wide), jnp.bfloat16),
            pltpu.VMEM((rows, wide), jnp.float32),
            pltpu.VMEM((rows, wide), jnp.float32),
            pltpu.VMEM((rows, hidden), jnp.bfloat16),
            pltpu.VMEM((rows, hidden), jnp.bfloat16),
            pltpu.VMEM((steps, hidden, width // steps), jnp.bfloat16),
            pltpu.VMEM((2, rows, width // steps), jnp.bfloat16),
            pltpu.SemaphoreType.DMA((count,)),
            pltpu.SemaphoreType.DMA((count,)),
            pltpu.SemaphoreType.DMA(()),
            pltpu.SemaphoreType.DMA((steps,)),
            pltpu.SemaphoreType.DMA((2, 4)),
        ],
        compiler_params=pltpu.CompilerParams(vmem_limit_bytes=VMEM),
        cost_estimate=pl.CostEstimate(
            flops=2 * rows * (count * depth * wide + hidden * width),
            bytes_accessed=2 * (count * depth * (wide + rows) + width * (hidden + rows)),
            transcendentals=rows * wide,
        ),
    )(meta, factors, before, down, *gate_up, *[piece for part in pieces for piece in part])


def body(
    hidden_in,
    queries,
    latent_cache,
    new_latent,
    cache_lengths,
    value_up,
    out_proj,
    norm_gain,
    router,
    expert_ids,
    w_gate_up,
    w_down,
):
    rows = hidden_in.shape[0]
    width = hidden_in.shape[1]
    chips = lax.axis_size("chip")
    cores = lax.axis_size("core")
    groups = lax.axis_size(GROUP)
    core = lax.axis_index("core")
    chip = lax.axis_index("chip")
    group = lax.axis_index(GROUP)
    place = chip * cores + core
    chip_cols = width // chips
    own_cols = chip_cols // cores
    expert_count = router.shape[1]
    total = chips * cores * rows
    order = ring_order()

    outgoing = hidden_in.reshape(rows, chips, chip_cols).transpose(1, 0, 2)
    names = jnp.broadcast_to(expert_ids.astype(jnp.bfloat16)[None], (chips, rows, TOP))
    arrived = lax.all_to_all(
        jnp.concatenate([outgoing, names], axis=2), "chip", split_axis=0, concat_axis=0, tiled=True
    )

    parts = 4
    span = width // parts
    gate_up = []
    stages = [None, (0, 0), (1, 0), (0, 1)]
    final = chips // 2 - 1
    ends = [(1, 1), (0, 2), (1, 2), (None, final)]
    projected = []

    def during_first(s, i, moving, pieces):
        if (s, i) == (None, None):
            part = project([piece[: chips - 1] for piece in pieces], out_proj.T, 2, 20 * 1024 * 1024)
            moving, part = lax.optimization_barrier((moving, part))
            projected.append(part)
        if (s, i) in ends:
            p = ends.index((s, i))
            raw = w_gate_up
            if stages[p] is not None:
                raw, _ = lax.optimization_barrier((raw, pieces[stages[p][0]][1 + 2 * stages[p][1]]))
            quarter = raw[0, p * span : (p + 1) * span].reshape(span, -1)
            moving, quarter = lax.optimization_barrier((moving, quarter))
            gate_up.append(quarter)
        return moving

    own_gain = lax.dynamic_slice_in_dim(norm_gain, place * own_cols, own_cols, 0)[None]
    own_router = lax.dynamic_slice_in_dim(router.T, place * own_cols, own_cols, 1)
    first_rows, then_rows = reduce_rows()
    meta = jnp.stack(order + [place] + first_rows + then_rows).astype(jnp.int32)

    head_out = attend(queries, latent_cache, new_latent, cache_lengths, value_up)
    head_out, arrived = lax.optimization_barrier((head_out, arrived))
    other_arrived = swap_cores(arrived)
    low, high = by_core(core, head_out, swap_cores(head_out))
    block = jnp.concatenate([low, high], axis=0)
    half = block.shape[1] // STREAMS
    pieces = ring_gather([block[:, s * half : (s + 1) * half] for s in range(STREAMS)], during_first)
    projected.append(project([piece[chips - 1 :] for piece in pieces], out_proj.T, 8, VMEM))
    parts, got = [], []
    for part in projected:
        if groups == 2:
            parts.append(part)
            got.append(lax.ppermute(part.astype(jnp.bfloat16), "sec", SWAP))
        else:
            parts.append(lax.psum(part, GROUP))
            got.append(jnp.zeros(part.shape, jnp.bfloat16))
    arrived = jnp.stack(by_core(core, arrived, other_arrived), axis=1)
    arrived = arrived.reshape(chips, cores * rows, chip_cols + TOP)
    residual, stats = finish(meta, parts, got, arrived, own_gain, own_router)
    residual = residual.reshape(total, own_cols)
    stats = stats.reshape(total, expert_count + 1).T
    stats = stats + swap_cores(stats)
    low, high = by_core(core, residual, swap_cores(residual))
    block = jnp.concatenate([low, high], axis=1)
    half = total // STREAMS

    ids = arrived[:, :, chip_cols:].reshape(total, TOP).T.astype(jnp.int32)
    grid = lax.broadcasted_iota(jnp.int32, (1, expert_count, 1), 1)
    chosen = jnp.any(ids[:, None, :] == grid, axis=0)

    def packed(sums):
        high = lax.reduce_precision(sums, 8, 7)
        flat = jnp.stack([high, sums - high]).astype(jnp.bfloat16).reshape(-1)
        extra = -(-flat.size // (16 * chip_cols)) * 16
        return jnp.pad(flat, (0, extra * chip_cols - flat.size)).reshape(extra, chip_cols)

    def unpacked(pieces):
        count = expert_count + 1
        added = sum(piece[half:].astype(jnp.float32) for piece in pieces).reshape(-1)
        return jnp.sum(added[: 2 * count * half].reshape(2, count, half), axis=0)

    blocks = []
    for s in range(STREAMS):
        span = slice(s * half, (s + 1) * half)
        blocks.append(jnp.concatenate([block[span], packed(stats[:, span])], axis=0))

    def route(stats):
        norm = lax.rsqrt(stats[expert_count:] / width + norm_epsilon)
        affinity = jnp.where(chosen, jax.nn.sigmoid(stats[:expert_count] * norm), 0.0)
        scale = jnp.sum(jnp.where(grid[0] == place, affinity, 0.0), axis=0, keepdims=True)
        scale = route_scale * scale / jnp.sum(affinity, axis=0, keepdims=True)
        return jnp.concatenate([norm, scale], axis=0)

    sums = []
    def during_second(s, i, moving, pieces):
        if (s, i) == (STREAMS - 1, None):
            moving, sums[0] = lax.optimization_barrier((moving, sums[0]))
        if (s, i) == (STREAMS - 1, final - 1):
            blocks = [piece[: chips - 3] for piece in pieces]
            blocks, _ = lax.optimization_barrier((blocks, moving))
            sums.append(gate(meta, 0, blocks, total, gate_up, chips))
        return moving

    pieces = ring_gather(blocks, during_second)
    stats = jnp.concatenate([unpacked(part) for part in pieces], axis=1)
    keep_first, give_first, keep_then, give_then = tail(
        meta,
        chips - 3,
        [piece[chips - 3 :] for piece in pieces],
        total,
        gate_up,
        sums[0],
        route(stats),
        w_down[0],
        chips,
    )

    got = [swap_cores(give_first), swap_cores(give_then)]

    def own_columns(block):
        held, _ = lax.optimization_barrier((pieces, block))
        own = own_residual(meta, held, rows).reshape(groups, chips // groups, rows, chip_cols)
        own = lax.dynamic_index_in_dim(own, group, 0, keepdims=False)
        own = own.transpose(1, 0, 2).reshape(rows, width // groups).astype(jnp.float32)
        span = width // groups
        return own / lax.dynamic_slice_in_dim(norm_gain, group * span, span, 0)

    mixture, own = ring_reduce([keep_first, keep_then], got, own_columns)
    if groups == 2:
        mixture = plus(*mixture)
    else:
        mixture = jnp.concatenate(mixture, axis=1).reshape(rows, groups, width // groups)
        mixture = lax.psum_scatter(mixture, GROUP, scatter_dimension=1, tiled=False)
    return plus(own, mixture).astype(jnp.bfloat16)


def solution(mesh):
    sec, batch, head = mesh.shape["sec"], mesh.shape["batch"], mesh.shape["head"]
    devices = mesh.devices.reshape(sec, batch // 2, 2, head)
    split = Mesh(devices, ("sec", "chip", "core", "head"))
    tokens = ("chip", "core")
    in_specs = (
        P(tokens, None),
        P(tokens, GROUP, None),
        P(tokens, None, None),
        P(tokens, None),
        P(tokens),
        P(GROUP, None, None),
        P(GROUP, tokens),
        P(),
        P(),
        P(tokens, None),
        P(tokens, None, None, GROUP),
        P(tokens, GROUP, None),
    )
    out_specs = P(tokens, GROUP)
    return jax.shard_map(body, mesh=split, in_specs=in_specs, out_specs=out_specs, check_vma=False)
```

```python
import functools

import jax
import jax.numpy as jnp
from jax import lax
from jax.experimental import pallas as pl
from jax.experimental.pallas import tpu as pltpu
from jax.sharding import Mesh, PartitionSpec as P

QKD = 192
TOP = 8

norm_epsilon = 1e-06
route_scale = 2.5

GROUP = ("sec", "head")
SWAP = [(0, 1), (1, 0)]
STREAMS = 2
VMEM = 56 * 1024 * 1024
NT = (((1,), (1,)), ((), ()))
ANY = pl.BlockSpec(memory_space=pl.ANY)
IN_HBM = pl.BlockSpec(memory_space=pltpu.HBM)
IN_VMEM = pl.BlockSpec(memory_space=pltpu.VMEM)
IN_SMEM = pl.BlockSpec(memory_space=pltpu.SMEM)


def attend(queries, latent_cache, new_latent, cache_lengths, value_up):
    row_count = queries.shape[0]
    latent_width = value_up.shape[1]
    cache_depth = latent_cache.shape[1]
    score_scale = QKD ** (-0.5)
    scores = (
        jnp.einsum("thk,tjk->thj", queries, latent_cache, preferred_element_type=jnp.float32)
        * score_scale
    )
    own_score = (
        jnp.einsum("thk,tk->th", queries, new_latent, preferred_element_type=jnp.float32)
        * score_scale
    )
    positions = lax.broadcasted_iota(jnp.int32, (1, 1, cache_depth), 2)
    in_cache = positions < cache_lengths[:, None, None]
    scores = jnp.where(in_cache, scores, -jnp.inf)
    top_score = jnp.maximum(jnp.max(scores, axis=2), own_score)
    cache_exp = jnp.exp(scores - top_score[:, :, None])
    own_exp = jnp.exp(own_score - top_score)
    softmax_sum = jnp.sum(cache_exp, axis=2) + own_exp
    cache_weights = (cache_exp / softmax_sum[:, :, None]).astype(jnp.bfloat16)
    own_weights = (own_exp / softmax_sum).astype(jnp.bfloat16)
    latent_out = jnp.einsum(
        "thj,tjc->thc",
        cache_weights,
        latent_cache[:, :, :latent_width],
        preferred_element_type=jnp.float32,
    )
    latent_out = latent_out + own_weights.astype(jnp.float32)[:, :, None] * new_latent[
        :, None, :latent_width
    ].astype(jnp.float32)
    latent_out = latent_out.astype(jnp.bfloat16)
    head_out = jnp.einsum(
        "thc,hcd->thd", latent_out, value_up, preferred_element_type=jnp.float32
    ).astype(jnp.bfloat16)
    return head_out.reshape(row_count, -1)


def place_of(chip, chips):
    return jnp.where(chip % 2 == 0, chip // 2, chips - 1 - chip // 2)


def chip_at(place, chips):
    place = place % chips
    return jnp.where(place < chips // 2, 2 * place, 2 * (chips - 1 - place) + 1)


def ring_step(block):
    chips = lax.axis_size("chip")
    ring = list(range(0, chips, 2)) + list(range(chips - 1, 0, -2))
    pairs = []
    for i in range(chips):
        here, there = ring[i], ring[(i + 1) % chips]
        pairs += [(2 * here, 2 * there), (2 * there + 1, 2 * here + 1)]
    return lax.ppermute(block, ("chip", "core"), pairs)


def swap_cores(block):
    return lax.ppermute(block, "core", SWAP)


def by_core(core, first, second):
    return jnp.where(core == 0, first, second), jnp.where(core == 0, second, first)


def ring_gather(blocks, between):
    chips = lax.axis_size("chip")
    core = lax.axis_index("core")
    pieces, moving = [[block] for block in blocks], list(blocks)
    for i in range(chips // 2 - 1):
        for s in range(STREAMS):
            moving[s] = ring_step(between(s, i, moving[s], pieces))
            if 0 < i < chips // 2 - 2:
                moving[s], pieces[s][-1] = lax.optimization_barrier((moving[s], pieces[s][-1]))
            if i < chips // 2 - 2:
                pieces[s] += [moving[s], swap_cores(moving[s])]
    moving = between(STREAMS - 1, None, moving, pieces)
    for s in range(STREAMS):
        pieces[s] += [moving[s], swap_cores(moving[s])]
    last = between(None, chips // 2 - 1, jnp.where(core == 0, moving[0], moving[1]), pieces)
    last = between(None, None, ring_step(last), pieces)
    for s, piece in enumerate(by_core(core, last, swap_cores(last))):
        pieces[s].append(piece)
    return pieces


def ring_order():
    chips = lax.axis_size("chip")
    place = place_of(lax.axis_index("chip"), chips)
    sign = 2 * lax.axis_index("core") - 1
    places = [place]
    for d in range(1, chips // 2):
        places += [place + sign * d, place - sign * d]
    places.append(place + chips // 2)
    return [chip_at(p, chips) for p in places]


def plus(a, b):
    return a.astype(jnp.float32) + b.astype(jnp.float32)


def reduce_rows():
    chips = lax.axis_size("chip")
    core = lax.axis_index("core")
    chip = lax.axis_index("chip")
    place = place_of(chip, chips)
    far = 2 * chip_at(place + chips // 2, chips)

    def way(side, sign):
        blocks = []
        for d in range(chips // 2 - 1, 0, -1):
            at = 2 * chip_at(place + sign * d, chips)
            blocks += [at, at + 1]
        return [far + side] + blocks[:2], blocks[2:] + [2 * chip + side]

    sign = 1 - 2 * core
    keep, give = way(core, sign), way(1 - core, -sign)
    return keep[0] + give[0], keep[1] + give[1]


def ring_reduce(keep, got, between):
    core = lax.axis_index("core")
    group, groups = lax.axis_index(GROUP), lax.axis_size(GROUP)
    rows = keep[0].shape[0] // 3

    def cut(at, size, s):
        def one(parts):
            part, start = (parts[0], at) if at < 3 * rows else (parts[1], at - 3 * rows)
            half = part.shape[1] // STREAMS
            first = (group + 1 + s) % STREAMS if groups == STREAMS else s
            return lax.dynamic_slice(part, (start, first * half), (size, half))

        return plus(one(keep), one(got))

    moving = [ring_step(cut(0, rows, s).astype(jnp.bfloat16)) for s in range(STREAMS)]
    moving = [
        jnp.concatenate([jnp.where(core == 0, m, 0), jnp.where(core == 0, 0, m)], axis=0)
        for m in moving
    ]
    at, ahead, ready = rows, None, None
    total = 3 * rows + keep[1].shape[0]
    while at < total - rows:
        for s in range(STREAMS):
            if ahead is not None:
                moving[s], _ = lax.optimization_barrier((moving[s], ahead))
            ahead = plus(cut(at, 2 * rows, s), moving[s]).astype(jnp.bfloat16)
            if at == rows and s == STREAMS - 1:
                ready = between(ahead)
            if at > rows and s == STREAMS - 1:
                ahead, ready = lax.optimization_barrier((ahead, ready))
            moving[s] = ring_step(ahead)
        at += 2 * rows
    sums = []
    for s in range(STREAMS):
        moving[s], _ = lax.optimization_barrier((moving[s], sums[0] if sums else ahead))
        mine, theirs = by_core(core, moving[s][:rows], moving[s][rows:])
        added = plus(cut(at, rows, s), plus(mine, swap_cores(theirs)))
        if groups == STREAMS and s == 0:
            added = lax.ppermute(added.astype(jnp.bfloat16), "sec", SWAP)
        sums.append(added)
    return sums, ready


def stream(count, ahead, copy):
    for k in range(min(ahead, count)):
        copy(k).start()

    def ready(k):
        copy(k).wait()

        @pl.when(k + ahead < count)
        def _():
            copy(k + ahead).start()

    return ready


def project_kernel(steps, count, weight, *refs):
    pieces, (out, rows, held, piece_sems, weight_sems) = refs[:-5], refs[-5:]
    depth = held.shape[2]
    block, half = pieces[0].shape
    copies = []
    for i, piece in enumerate(pieces):
        at, s = i % count, i // count
        target = rows.at[pl.ds(at * block, block), pl.ds(s * half, half)]
        copies.append(pltpu.make_async_copy(piece, target, piece_sems.at[i]))
    for copy in copies:
        copy.start()

    def weight_copy(k):
        columns = pl.ds(pl.multiple_of(k * depth, depth), depth)
        slot = k % 3
        return pltpu.make_async_copy(weight.at[:, columns], held.at[slot], weight_sems.at[slot])

    ready = stream(steps, 2, weight_copy)
    for copy in copies:
        copy.wait()
    out[...] = jnp.zeros_like(out)

    @pl.loop(0, steps)
    def _(k):
        ready(k)
        columns = pl.ds(pl.multiple_of(k * depth, depth), depth)
        out[...] += lax.dot_general(
            rows[:, columns], held[k % 3], NT, preferred_element_type=jnp.float32
        )


def project_few_kernel(steps, weight, *refs):
    pieces, (out, rows, held, turned, piece_sems, weight_sems) = refs[:-6], refs[-6:]
    half = pieces[0].shape[1]
    parts = weight_sems.shape[0]
    size = held.shape[0] // parts
    copies = []
    for p in range(parts):
        span = pl.ds(p * size, size)
        copies.append(
            pltpu.make_async_copy(weight.at[span, :], held.at[span, :], weight_sems.at[p])
        )
    for s, piece in enumerate(pieces):
        target = rows.at[:, pl.ds(s * half, half)]
        copies.append(pltpu.make_async_copy(piece, target, piece_sems.at[s]))
    for copy in copies:
        copy.start()
    for copy in copies:
        copy.wait()
    turned[...] = jnp.zeros_like(turned)
    depth = rows.shape[1] // steps

    @pl.loop(0, steps)
    def _(k):
        columns = pl.ds(pl.multiple_of(k * depth, depth), depth)
        turned[...] += lax.dot_general(
            held[:, columns], rows[:, columns], NT, preferred_element_type=jnp.float32
        )

    out[...] = turned[...].T


def project(pieces, weight):
    count = len(pieces[0])
    rows, half = pieces[0][0].shape
    depth = STREAMS * half
    columns = weight.shape[0]
    steps = 8
    total = count * rows
    few = count == 1
    if few:
        kernel = functools.partial(project_few_kernel, steps)
        held = [
            pltpu.VMEM((columns, depth), jnp.bfloat16),
            pltpu.VMEM((columns, total), jnp.float32),
        ]
        weight_sems = 2
    else:
        kernel = functools.partial(project_kernel, steps, count)
        held = [pltpu.VMEM((3, columns, depth // steps), jnp.bfloat16)]
        weight_sems = 3
    return pl.pallas_call(
        kernel,
        out_shape=jax.ShapeDtypeStruct((total, columns), jnp.float32),
        in_specs=[ANY] * (1 + STREAMS * count),
        out_specs=IN_VMEM,
        scratch_shapes=[pltpu.VMEM((total, depth), jnp.bfloat16)]
        + held
        + [
            pltpu.SemaphoreType.DMA((STREAMS * count,)),
            pltpu.SemaphoreType.DMA((weight_sems,)),
        ],
        compiler_params=pltpu.CompilerParams(
            vmem_limit_bytes=VMEM if few else 20 * 1024 * 1024
        ),
        cost_estimate=pl.CostEstimate(
            flops=2 * total * depth * columns,
            bytes_accessed=2 * depth * (total + columns) + 4 * total * columns,
            transcendentals=0,
        ),
    )(weight, *[piece for part in pieces for piece in part])


def finish_kernel(count, meta, arrived, gain, router, *refs):
    parts, got, (out, stats) = refs[:count], refs[count : 2 * count], refs[2 * count :]
    chips, rows, columns = out.shape
    names = router.shape[0]
    core = meta[chips] % 2
    i = 0
    for part, other in zip(parts, got):
        for j in range(part.shape[0] // rows):
            at = meta[i]
            block = part[j * rows : (j + 1) * rows, :] + other[j * rows : (j + 1) * rows, :].astype(jnp.float32)
            hidden = arrived[at].astype(jnp.float32)
            hidden = jnp.where(core == 0, hidden[:, :columns], hidden[:, columns : 2 * columns])
            block = hidden + block
            scaled = (block * gain[...]).astype(jnp.bfloat16)
            out[at] = scaled
            stats[at, :, :names] = lax.dot_general(
                scaled, router[...], NT, preferred_element_type=jnp.float32
            )
            stats[at, :, names : names + 1] = jnp.sum(block * block, axis=1, keepdims=True)
            i += 1


def finish(meta, parts, got, arrived, gain, router):
    columns = parts[0].shape[1]
    chips, rows, _ = arrived.shape
    return pl.pallas_call(
        functools.partial(finish_kernel, len(parts)),
        out_shape=(
            jax.ShapeDtypeStruct((chips, rows, columns), jnp.bfloat16),
            jax.ShapeDtypeStruct((chips, rows, router.shape[0] + 1), jnp.float32),
        ),
        in_specs=[IN_SMEM] + [IN_VMEM] * (3 + 2 * len(parts)),
        out_specs=(IN_VMEM, IN_VMEM),
        compiler_params=pltpu.CompilerParams(vmem_limit_bytes=16 * 1024 * 1024),
    )(meta, arrived, gain, router, *parts, *got)


def own_kernel(count, meta, *refs):
    pieces, (out, sems) = refs[:-2], refs[-2:]
    chips, share, _ = out.shape
    half = chips * share
    place = meta[chips]
    for s in range(STREAMS):

        @pl.when(place * share // half == s)
        def _():
            at = pl.ds(pl.multiple_of(place * share - s * half, share), share)
            copies = [
                pltpu.make_async_copy(pieces[s * count + i].at[at, :], out.at[meta[i]], sems.at[i])
                for i in range(count)
            ]
            for copy in copies:
                copy.start()
            for copy in copies:
                copy.wait()


def own_residual(meta, pieces, share):
    chips = len(pieces[0])
    depth = pieces[0][0].shape[1]
    return pl.pallas_call(
        functools.partial(own_kernel, chips),
        out_shape=jax.ShapeDtypeStruct((chips, share, depth), jnp.bfloat16),
        in_specs=[IN_SMEM] + [ANY] * (STREAMS * chips),
        out_specs=IN_VMEM,
        scratch_shapes=[pltpu.SemaphoreType.DMA((chips,))],
        compiler_params=pltpu.CompilerParams(vmem_limit_bytes=VMEM),
    )(meta, *[piece for part in pieces for piece in part])


def piece_starts(pieces, count, held, sems):
    half = held.shape[1] // STREAMS
    depth = pieces[0].shape[1]
    for i in range(count):
        for s in range(STREAMS):
            at = i // (held.shape[2] // depth)
            target = held.at[at, pl.ds(s * half, half), :]
            if held.shape[2] != depth:
                target = target.at[:, pl.ds(i % 2 * depth, depth)]
            source = pieces[s * count + i].at[pl.ds(0, half), :]
            pltpu.make_async_copy(source, target, sems.at[i]).start()


def add_products(count, depth, held, weight, total, piece_sems, weight_sems):
    per = held.shape[2] // depth

    def ready(k, at):
        block = held.at[k] if per == 1 else held.at[k, :, pl.ds(at * depth, depth)]
        wait_for(block, piece_sems.at[per * k + at])
        wait_for(weight.at[k, pl.ds(at * depth, depth), :], weight_sems.at[per * k + at])

    def add(k, deep):
        for at in range(0, total.shape[1], 256):
            total[:, at : at + 256] += jnp.dot(
                held[k, :, :deep],
                weight[k, :deep, at : at + 256],
                preferred_element_type=jnp.float32,
            )

    total[...] = jnp.zeros_like(total)

    @pl.loop(0, count // per)
    def _(k):
        for at in range(per):
            ready(k, at)
        add(k, per * depth)

    if count % per:
        ready(count // per, 0)
        add(count // per, depth)


def weight_start(at, gate_up, depth, per, target, sem):
    for p, part in enumerate(gate_up):

        @pl.when(at // per == p)
        def _():
            span = pl.ds(pl.multiple_of(at % per * depth, 16), depth)
            pltpu.make_async_copy(part.at[span, :], target, sem).start()


def wait_for(ref, sem):
    pltpu.make_async_copy(ref, ref, sem).wait()


def gate_kernel(parts, first, count, chips, meta, *refs):
    gate_up, pieces = refs[:parts], refs[parts:-5]
    total, held, weight, piece_sems, weight_sems = refs[-5:]
    depth = pieces[0].shape[1]
    for k in range(count):
        side = held.shape[2] // depth
        target = weight.at[k // side, pl.ds(k % side * depth, depth), :]
        weight_start(meta[first + k], gate_up, depth, chips // parts, target, weight_sems.at[k])
        if k == 0:
            piece_starts(pieces, count, held, piece_sems)

    add_products(count, depth, held, weight, total, piece_sems, weight_sems)


def gate(meta, first, pieces, rows, gate_up, chips):
    count = len(pieces[0])
    depth = pieces[0][0].shape[1]
    side = 1 if depth % 128 else 2
    wide = gate_up[0].shape[1]
    return pl.pallas_call(
        functools.partial(gate_kernel, len(gate_up), first, count, chips),
        out_shape=jax.ShapeDtypeStruct((rows, wide), jnp.float32),
        in_specs=[IN_SMEM] + [IN_HBM] * len(gate_up) + [ANY] * (STREAMS * count),
        out_specs=IN_VMEM,
        scratch_shapes=[
            pltpu.VMEM((-(-count // side), rows, side * depth), jnp.bfloat16),
            pltpu.VMEM((-(-count // side), side * depth, wide), jnp.bfloat16),
            pltpu.SemaphoreType.DMA((count,)),
            pltpu.SemaphoreType.DMA((count,)),
        ],
        compiler_params=pltpu.CompilerParams(vmem_limit_bytes=VMEM),
        cost_estimate=pl.CostEstimate(
            flops=2 * rows * count * depth * wide,
            bytes_accessed=2 * count * depth * (wide + rows),
            transcendentals=0,
        ),
    )(meta, *gate_up, *[piece for part in pieces for piece in part])


def tail_kernel(parts, first, count, chips, meta, factors, before, down, *refs):
    gate_up, pieces = refs[:parts], refs[parts : parts + STREAMS * count]
    rest = refs[parts + STREAMS * count :]
    outs = rest[:4]
    held, weight, total, earlier, active, ordered, second, staged = rest[4:12]
    piece_sems, weight_sems, earlier_sem, second_sems, out_sems = rest[12:]
    rows = held.shape[1]
    depth = pieces[0].shape[1]
    hidden = active.shape[1]
    span = staged.shape[2]
    steps = second.shape[1] // span
    for k in range(count):
        side = held.shape[2] // depth
        target = weight.at[k // side, pl.ds(k % side * depth, depth), :]
        weight_start(meta[first + k], gate_up, depth, chips // parts, target, weight_sems.at[k])
        if k == 0:
            piece_starts(pieces, count, held, piece_sems)
    pltpu.make_async_copy(before, earlier, earlier_sem).start()

    def columns(n):
        return pl.ds(pl.multiple_of(n * span, span), span)

    def second_copy(n):
        size = hidden // second_sems.shape[0]
        span_rows = pl.ds(n * size, size)
        return pltpu.make_async_copy(
            down.at[span_rows, :], second.at[span_rows, :], second_sems.at[n]
        )

    for n in range(second_sems.shape[0]):
        second_copy(n).start()

    add_products(count, depth, held, weight, total, piece_sems, weight_sems)

    pltpu.make_async_copy(before, earlier, earlier_sem).wait()
    columns_of = jnp.concatenate([factors[...], jnp.zeros((6, rows), jnp.float32)], axis=0).T
    norm, scale = columns_of[:, 0:1], columns_of[:, 1:2]
    gate = (total[:, :hidden] + earlier[:, :hidden]) * norm
    up = (total[:, hidden:] + earlier[:, hidden:]) * (norm * scale)
    active[...] = (gate * jax.nn.sigmoid(gate) * up).astype(jnp.bfloat16)
    share = rows // (2 * chips)
    for i in range(2 * chips):
        at = pl.ds(pl.multiple_of(meta[chips + 1 + i] * share, share), share)
        ordered[i * share : (i + 1) * share, :] = active[at, :]

    for n in range(second_sems.shape[0]):
        second_copy(n).wait()

    def out_copies(n):
        copies, at = [], 0
        slot = n % 2
        for i, out in enumerate(outs):
            size = out.shape[0]
            source = staged.at[slot, pl.ds(at, size), :]
            copies.append(
                pltpu.make_async_copy(source, out.at[:, columns(n)], out_sems.at[slot, i])
            )
            at += size
        return copies

    @pl.loop(0, steps)
    def _(n):
        @pl.when(n >= 2)
        def _():
            for copy in out_copies(n - 2):
                copy.wait()

        result = jnp.dot(
            ordered[...], second[:, columns(n)], preferred_element_type=jnp.float32
        )
        staged[n % 2] = result.astype(jnp.bfloat16)
        for copy in out_copies(n):
            copy.start()

    for n in range(max(0, steps - 2), steps):
        for copy in out_copies(n):
            copy.wait()


def tail(meta, first, pieces, rows, gate_up, before, factors, down, chips):
    count = len(pieces[0])
    depth = pieces[0][0].shape[1]
    side = 1 if depth % 128 else 2
    wide = gate_up[0].shape[1]
    hidden, width = down.shape
    share = rows // (2 * chips)
    steps = max(1, width // 1024)
    shapes = [3 * share, 3 * share, rows // 2 - 3 * share, rows // 2 - 3 * share]
    return pl.pallas_call(
        functools.partial(tail_kernel, len(gate_up), first, count, chips),
        out_shape=tuple(jax.ShapeDtypeStruct((n, width), jnp.bfloat16) for n in shapes),
        in_specs=[IN_SMEM, IN_VMEM, ANY, IN_HBM]
        + [IN_HBM] * len(gate_up)
        + [ANY] * (STREAMS * count),
        out_specs=(ANY,) * 4,
        scratch_shapes=[
            pltpu.VMEM((-(-count // side), rows, side * depth), jnp.bfloat16),
            pltpu.VMEM((-(-count // side), side * depth, wide), jnp.bfloat16),
            pltpu.VMEM((rows, wide), jnp.float32),
            pltpu.VMEM((rows, wide), jnp.float32),
            pltpu.VMEM((rows, hidden), jnp.bfloat16),
            pltpu.VMEM((rows, hidden), jnp.bfloat16),
            pltpu.VMEM((hidden, width), jnp.bfloat16),
            pltpu.VMEM((2, rows, width // steps), jnp.bfloat16),
            pltpu.SemaphoreType.DMA((count,)),
            pltpu.SemaphoreType.DMA((count,)),
            pltpu.SemaphoreType.DMA(()),
            pltpu.SemaphoreType.DMA((4,)),
            pltpu.SemaphoreType.DMA((2, 4)),
        ],
        compiler_params=pltpu.CompilerParams(vmem_limit_bytes=VMEM),
        cost_estimate=pl.CostEstimate(
            flops=2 * rows * (count * depth * wide + hidden * width),
            bytes_accessed=2 * (count * depth * (wide + rows) + width * (hidden + rows)),
            transcendentals=rows * wide,
        ),
    )(meta, factors, before, down, *gate_up, *[piece for part in pieces for piece in part])


def body(
    hidden_in,
    queries,
    latent_cache,
    new_latent,
    cache_lengths,
    value_up,
    out_proj,
    norm_gain,
    router,
    expert_ids,
    w_gate_up,
    w_down,
):
    rows = hidden_in.shape[0]
    width = hidden_in.shape[1]
    chips = lax.axis_size("chip")
    cores = lax.axis_size("core")
    groups = lax.axis_size(GROUP)
    core = lax.axis_index("core")
    chip = lax.axis_index("chip")
    group = lax.axis_index(GROUP)
    place = chip * cores + core
    chip_cols = width // chips
    own_cols = chip_cols // cores
    expert_count = router.shape[1]
    total = chips * cores * rows
    order = ring_order()

    outgoing = hidden_in.reshape(rows, chips, chip_cols).transpose(1, 0, 2)
    names = jnp.broadcast_to(expert_ids.astype(jnp.bfloat16)[None], (chips, rows, TOP))
    arrived = lax.all_to_all(
        jnp.concatenate([outgoing, names], axis=2), "chip", split_axis=0, concat_axis=0, tiled=True
    )

    parts = 4
    quarter_rows = width // parts
    gate_up = []
    final = chips // 2 - 1
    projected = []

    def quarter(moving, after):
        p = len(gate_up)
        raw, _ = lax.optimization_barrier((w_gate_up, after))
        part = raw[0, p * quarter_rows : (p + 1) * quarter_rows].reshape(quarter_rows, -1)
        moving, part = lax.optimization_barrier((moving, part))
        gate_up.append(part)
        return moving

    def during_first(s, i, moving, pieces):
        if (s, i) == (None, None):
            part = project([piece[: chips - 1] for piece in pieces], out_proj.T)
            moving, part = lax.optimization_barrier((moving, part))
            projected.append(part)
        if (s, i) == (1, 1):
            for t in range(STREAMS):
                moving = quarter(moving, pieces[t][0])
        return moving

    own_gain = lax.dynamic_slice_in_dim(norm_gain, place * own_cols, own_cols, 0)[None]
    own_router = lax.dynamic_slice_in_dim(router.T, place * own_cols, own_cols, 1)
    first_rows, then_rows = reduce_rows()
    meta = jnp.stack(order + [place] + first_rows + then_rows).astype(jnp.int32)

    head_out = attend(queries, latent_cache, new_latent, cache_lengths, value_up)
    head_out, arrived = lax.optimization_barrier((head_out, arrived))
    other_arrived = swap_cores(arrived)
    low, high = by_core(core, head_out, swap_cores(head_out))
    block = jnp.concatenate([low, high], axis=0)
    half = block.shape[1] // STREAMS
    pieces = ring_gather([block[:, s * half : (s + 1) * half] for s in range(STREAMS)], during_first)
    projected.append(project([piece[chips - 1 :] for piece in pieces], out_proj.T))
    parts, got = [], []
    for part in projected:
        if groups == 2:
            parts.append(part)
            got.append(lax.ppermute(part.astype(jnp.bfloat16), "sec", SWAP))
        else:
            parts.append(lax.psum(part, GROUP))
            got.append(jnp.zeros(part.shape, jnp.bfloat16))
    arrived = jnp.stack(by_core(core, arrived, other_arrived), axis=1)
    arrived = arrived.reshape(chips, cores * rows, chip_cols + TOP)
    residual, stats = finish(meta, parts, got, arrived, own_gain, own_router)
    residual = residual.reshape(total, own_cols)
    stats = stats.reshape(total, expert_count + 1).T
    stats = stats + swap_cores(stats)
    low, high = by_core(core, residual, swap_cores(residual))
    block = jnp.concatenate([low, high], axis=1)
    half = total // STREAMS

    ids = arrived[:, :, chip_cols:].reshape(total, TOP).T.astype(jnp.int32)
    grid = lax.broadcasted_iota(jnp.int32, (1, expert_count, 1), 1)
    chosen = jnp.any(ids[:, None, :] == grid, axis=0)

    def packed(sums):
        high = lax.reduce_precision(sums, 8, 7)
        flat = jnp.stack([high, sums - high]).astype(jnp.bfloat16).reshape(-1)
        extra = -(-flat.size // (16 * chip_cols)) * 16
        return jnp.pad(flat, (0, extra * chip_cols - flat.size)).reshape(extra, chip_cols)

    def unpacked(pieces):
        count = expert_count + 1
        added = sum(piece[half:].astype(jnp.float32) for piece in pieces).reshape(-1)
        return jnp.sum(added[: 2 * count * half].reshape(2, count, half), axis=0)

    blocks = []
    for s in range(STREAMS):
        span = slice(s * half, (s + 1) * half)
        blocks.append(jnp.concatenate([block[span], packed(stats[:, span])], axis=0))

    def route(stats):
        norm = lax.rsqrt(stats[expert_count:] / width + norm_epsilon)
        affinity = jnp.where(chosen, jax.nn.sigmoid(stats[:expert_count] * norm), 0.0)
        scale = jnp.sum(jnp.where(grid[0] == place, affinity, 0.0), axis=0, keepdims=True)
        scale = route_scale * scale / jnp.sum(affinity, axis=0, keepdims=True)
        return jnp.concatenate([norm, scale], axis=0)

    sums = []
    def during_second(s, i, moving, pieces):
        if (s, i) == (STREAMS - 1, None):
            moving, sums[0] = lax.optimization_barrier((moving, sums[0]))
        if (s, i) == (1, 1):
            for t in range(STREAMS):
                moving = quarter(moving, pieces[t][0])
        if (s, i) == (STREAMS - 1, final - 1):
            blocks = [piece[: chips - 3] for piece in pieces]
            blocks, _ = lax.optimization_barrier((blocks, moving))
            sums.append(gate(meta, 0, blocks, total, gate_up, chips))
        return moving

    pieces = ring_gather(blocks, during_second)
    stats = jnp.concatenate([unpacked(part) for part in pieces], axis=1)
    keep_first, give_first, keep_then, give_then = tail(
        meta,
        chips - 3,
        [piece[chips - 3 :] for piece in pieces],
        total,
        gate_up,
        sums[0],
        route(stats),
        w_down[0],
        chips,
    )

    got = [swap_cores(give_first), swap_cores(give_then)]

    def own_columns(block):
        held, _ = lax.optimization_barrier((pieces, block))
        own = own_residual(meta, held, rows).reshape(groups, chips // groups, rows, chip_cols)
        own = lax.dynamic_index_in_dim(own, group, 0, keepdims=False)
        own = own.transpose(1, 0, 2).reshape(rows, width // groups).astype(jnp.float32)
        span = width // groups
        return own / lax.dynamic_slice_in_dim(norm_gain, group * span, span, 0)

    mixture, own = ring_reduce([keep_first, keep_then], got, own_columns)
    if groups == 2:
        mixture = plus(*mixture)
    else:
        mixture = jnp.concatenate(mixture, axis=1).reshape(rows, groups, width // groups)
        mixture = lax.psum_scatter(mixture, GROUP, scatter_dimension=1, tiled=False)
    return plus(own, mixture).astype(jnp.bfloat16)


def solution(mesh):
    sec, batch, head = mesh.shape["sec"], mesh.shape["batch"], mesh.shape["head"]
    devices = mesh.devices.reshape(sec, batch // 2, 2, head)
    split = Mesh(devices, ("sec", "chip", "core", "head"))
    tokens = ("chip", "core")
    in_specs = (
        P(tokens, None),
        P(tokens, GROUP, None),
        P(tokens, None, None),
        P(tokens, None),
        P(tokens),
        P(GROUP, None, None),
        P(GROUP, tokens),
        P(),
        P(),
        P(tokens, None),
        P(tokens, None, None, GROUP),
        P(tokens, GROUP, None),
    )
    out_specs = P(tokens, GROUP)
    return jax.shard_map(body, mesh=split, in_specs=in_specs, out_specs=out_specs, check_vma=False)
```

```python
import functools

import jax
import jax.numpy as jnp
from jax import lax
from jax.experimental import pallas as pl
from jax.experimental.pallas import tpu as pltpu
from jax.sharding import Mesh, PartitionSpec as P

QKD = 192
TOP = 8

norm_epsilon = 1e-06
route_scale = 2.5

GROUP = ("sec", "head")
SWAP = [(0, 1), (1, 0)]
STREAMS = 2
VMEM = 56 * 1024 * 1024
NT = (((1,), (1,)), ((), ()))
ANY = pl.BlockSpec(memory_space=pl.ANY)
IN_HBM = pl.BlockSpec(memory_space=pltpu.HBM)
IN_VMEM = pl.BlockSpec(memory_space=pltpu.VMEM)
IN_SMEM = pl.BlockSpec(memory_space=pltpu.SMEM)


def attend(queries, latent_cache, new_latent, cache_lengths, value_up):
    row_count = queries.shape[0]
    latent_width = value_up.shape[1]
    cache_depth = latent_cache.shape[1]
    score_scale = QKD ** (-0.5)
    scores = (
        jnp.einsum("thk,tjk->thj", queries, latent_cache, preferred_element_type=jnp.float32)
        * score_scale
    )
    own_score = (
        jnp.einsum("thk,tk->th", queries, new_latent, preferred_element_type=jnp.float32)
        * score_scale
    )
    positions = lax.broadcasted_iota(jnp.int32, (1, 1, cache_depth), 2)
    in_cache = positions < cache_lengths[:, None, None]
    scores = jnp.where(in_cache, scores, -jnp.inf)
    top_score = jnp.maximum(jnp.max(scores, axis=2), own_score)
    cache_exp = jnp.exp(scores - top_score[:, :, None])
    own_exp = jnp.exp(own_score - top_score)
    softmax_sum = jnp.sum(cache_exp, axis=2) + own_exp
    cache_weights = (cache_exp / softmax_sum[:, :, None]).astype(jnp.bfloat16)
    own_weights = (own_exp / softmax_sum).astype(jnp.bfloat16)
    latent_out = jnp.einsum(
        "thj,tjc->thc",
        cache_weights,
        latent_cache[:, :, :latent_width],
        preferred_element_type=jnp.float32,
    )
    latent_out = latent_out + own_weights.astype(jnp.float32)[:, :, None] * new_latent[
        :, None, :latent_width
    ].astype(jnp.float32)
    latent_out = latent_out.astype(jnp.bfloat16)
    head_out = jnp.einsum(
        "thc,hcd->thd", latent_out, value_up, preferred_element_type=jnp.float32
    ).astype(jnp.bfloat16)
    return head_out.reshape(row_count, -1)


def place_of(chip, chips):
    return jnp.where(chip % 2 == 0, chip // 2, chips - 1 - chip // 2)


def chip_at(place, chips):
    place = place % chips
    return jnp.where(place < chips // 2, 2 * place, 2 * (chips - 1 - place) + 1)


def ring_step(block):
    chips = lax.axis_size("chip")
    ring = list(range(0, chips, 2)) + list(range(chips - 1, 0, -2))
    pairs = []
    for i in range(chips):
        here, there = ring[i], ring[(i + 1) % chips]
        pairs += [(2 * here, 2 * there), (2 * there + 1, 2 * here + 1)]
    return lax.ppermute(block, ("chip", "core"), pairs)


def swap_cores(block):
    return lax.ppermute(block, "core", SWAP)


def by_core(core, first, second):
    return jnp.where(core == 0, first, second), jnp.where(core == 0, second, first)


def ring_gather(blocks, between):
    chips = lax.axis_size("chip")
    core = lax.axis_index("core")
    pieces, moving = [[block] for block in blocks], list(blocks)
    for i in range(chips // 2 - 1):
        for s in range(STREAMS):
            moving[s] = ring_step(between(s, i, moving[s], pieces))
            if 0 < i < chips // 2 - 2:
                moving[s], pieces[s][-1] = lax.optimization_barrier((moving[s], pieces[s][-1]))
            if i < chips // 2 - 2:
                pieces[s] += [moving[s], swap_cores(moving[s])]
    moving = between(STREAMS - 1, None, moving, pieces)
    for s in range(STREAMS):
        pieces[s] += [moving[s], swap_cores(moving[s])]
    last = between(None, chips // 2 - 1, jnp.where(core == 0, moving[0], moving[1]), pieces)
    last = between(None, None, ring_step(last), pieces)
    for s, piece in enumerate(by_core(core, last, swap_cores(last))):
        pieces[s].append(piece)
    return pieces


def ring_order():
    chips = lax.axis_size("chip")
    place = place_of(lax.axis_index("chip"), chips)
    sign = 2 * lax.axis_index("core") - 1
    places = [place]
    for d in range(1, chips // 2):
        places += [place + sign * d, place - sign * d]
    places.append(place + chips // 2)
    return [chip_at(p, chips) for p in places]


def plus(a, b):
    return a.astype(jnp.float32) + b.astype(jnp.float32)


def reduce_rows():
    chips = lax.axis_size("chip")
    core = lax.axis_index("core")
    chip = lax.axis_index("chip")
    place = place_of(chip, chips)
    far = 2 * chip_at(place + chips // 2, chips)

    def way(side, sign):
        blocks = []
        for d in range(chips // 2 - 1, 0, -1):
            at = 2 * chip_at(place + sign * d, chips)
            blocks += [at, at + 1]
        return [far + side] + blocks[:2], blocks[2:] + [2 * chip + side]

    sign = 1 - 2 * core
    keep, give = way(core, sign), way(1 - core, -sign)
    return keep[0] + give[0], keep[1] + give[1]


def ring_reduce(keep, got, between):
    core = lax.axis_index("core")
    group, groups = lax.axis_index(GROUP), lax.axis_size(GROUP)
    rows = keep[0].shape[0] // 3

    def cut(at, size, s):
        def one(parts):
            part, start = (parts[0], at) if at < 3 * rows else (parts[1], at - 3 * rows)
            half = part.shape[1] // STREAMS
            first = (group + 1 + s) % STREAMS if groups == STREAMS else s
            return lax.dynamic_slice(part, (start, first * half), (size, half))

        return plus(one(keep), one(got))

    moving = [ring_step(cut(0, rows, s).astype(jnp.bfloat16)) for s in range(STREAMS)]
    moving = [
        jnp.concatenate([jnp.where(core == 0, m, 0), jnp.where(core == 0, 0, m)], axis=0)
        for m in moving
    ]
    at, ahead, ready = rows, None, None
    total = 3 * rows + keep[1].shape[0]
    while at < total - rows:
        for s in range(STREAMS):
            if ahead is not None:
                moving[s], _ = lax.optimization_barrier((moving[s], ahead))
            ahead = plus(cut(at, 2 * rows, s), moving[s]).astype(jnp.bfloat16)
            if at == rows and s == STREAMS - 1:
                ready = between(ahead)
            if at > rows and s == STREAMS - 1:
                ahead, ready = lax.optimization_barrier((ahead, ready))
            moving[s] = ring_step(ahead)
        at += 2 * rows
    sums = []
    for s in range(STREAMS):
        moving[s], _ = lax.optimization_barrier((moving[s], sums[0] if sums else ahead))
        mine, theirs = by_core(core, moving[s][:rows], moving[s][rows:])
        added = plus(cut(at, rows, s), plus(mine, swap_cores(theirs)))
        if groups == STREAMS and s == 0:
            added = lax.ppermute(added.astype(jnp.bfloat16), "sec", SWAP)
        sums.append(added)
    return sums, ready


def stream(count, ahead, copy):
    for k in range(min(ahead, count)):
        copy(k).start()

    def ready(k):
        copy(k).wait()

        @pl.when(k + ahead < count)
        def _():
            copy(k + ahead).start()

    return ready


def project_kernel(steps, count, weight, *refs):
    pieces, (out, rows, held, piece_sems, weight_sems) = refs[:-5], refs[-5:]
    depth = held.shape[2]
    block, half = pieces[0].shape
    copies = []
    for i, piece in enumerate(pieces):
        at, s = i % count, i // count
        target = rows.at[pl.ds(at * block, block), pl.ds(s * half, half)]
        copies.append(pltpu.make_async_copy(piece, target, piece_sems.at[i]))
    for copy in copies:
        copy.start()

    def weight_copy(k):
        columns = pl.ds(pl.multiple_of(k * depth, depth), depth)
        slot = k % 3
        return pltpu.make_async_copy(weight.at[:, columns], held.at[slot], weight_sems.at[slot])

    ready = stream(steps, 2, weight_copy)
    for copy in copies:
        copy.wait()
    out[...] = jnp.zeros_like(out)

    @pl.loop(0, steps)
    def _(k):
        ready(k)
        columns = pl.ds(pl.multiple_of(k * depth, depth), depth)
        out[...] += lax.dot_general(
            rows[:, columns], held[k % 3], NT, preferred_element_type=jnp.float32
        )


def project_few_kernel(steps, weight, *refs):
    pieces, (out, rows, held, turned, piece_sems, weight_sems) = refs[:-6], refs[-6:]
    half = pieces[0].shape[1]
    parts = weight_sems.shape[0]
    size = held.shape[0] // parts
    copies = []
    for p in range(parts):
        span = pl.ds(p * size, size)
        copies.append(
            pltpu.make_async_copy(weight.at[span, :], held.at[span, :], weight_sems.at[p])
        )
    for s, piece in enumerate(pieces):
        target = rows.at[:, pl.ds(s * half, half)]
        copies.append(pltpu.make_async_copy(piece, target, piece_sems.at[s]))
    for copy in copies:
        copy.start()
    for copy in copies:
        copy.wait()
    turned[...] = jnp.zeros_like(turned)
    depth = rows.shape[1] // steps

    @pl.loop(0, steps)
    def _(k):
        columns = pl.ds(pl.multiple_of(k * depth, depth), depth)
        turned[...] += lax.dot_general(
            held[:, columns], rows[:, columns], NT, preferred_element_type=jnp.float32
        )

    out[...] = turned[...].T


def project(pieces, weight):
    count = len(pieces[0])
    rows, half = pieces[0][0].shape
    depth = STREAMS * half
    columns = weight.shape[0]
    steps = 8
    total = count * rows
    few = count == 1
    if few:
        kernel = functools.partial(project_few_kernel, steps)
        held = [
            pltpu.VMEM((columns, depth), jnp.bfloat16),
            pltpu.VMEM((columns, total), jnp.float32),
        ]
        weight_sems = 2
    else:
        kernel = functools.partial(project_kernel, steps, count)
        held = [pltpu.VMEM((3, columns, depth // steps), jnp.bfloat16)]
        weight_sems = 3
    return pl.pallas_call(
        kernel,
        out_shape=jax.ShapeDtypeStruct((total, columns), jnp.float32),
        in_specs=[ANY] * (1 + STREAMS * count),
        out_specs=IN_VMEM,
        scratch_shapes=[pltpu.VMEM((total, depth), jnp.bfloat16)]
        + held
        + [
            pltpu.SemaphoreType.DMA((STREAMS * count,)),
            pltpu.SemaphoreType.DMA((weight_sems,)),
        ],
        compiler_params=pltpu.CompilerParams(
            vmem_limit_bytes=VMEM if few else 20 * 1024 * 1024
        ),
        cost_estimate=pl.CostEstimate(
            flops=2 * total * depth * columns,
            bytes_accessed=2 * depth * (total + columns) + 4 * total * columns,
            transcendentals=0,
        ),
    )(weight, *[piece for part in pieces for piece in part])


def finish_kernel(count, meta, arrived, gain, router, *refs):
    parts, got, (out, stats) = refs[:count], refs[count : 2 * count], refs[2 * count :]
    chips, rows, columns = out.shape
    names = router.shape[0]
    core = meta[chips] % 2
    i = 0
    for part, other in zip(parts, got):
        for j in range(part.shape[0] // rows):
            at = meta[i]
            block = part[j * rows : (j + 1) * rows, :] + other[j * rows : (j + 1) * rows, :].astype(jnp.float32)
            hidden = arrived[at].astype(jnp.float32)
            hidden = jnp.where(core == 0, hidden[:, :columns], hidden[:, columns : 2 * columns])
            block = hidden + block
            scaled = (block * gain[...]).astype(jnp.bfloat16)
            out[at] = scaled
            stats[at, :, :names] = lax.dot_general(
                scaled, router[...], NT, preferred_element_type=jnp.float32
            )
            stats[at, :, names : names + 1] = jnp.sum(block * block, axis=1, keepdims=True)
            i += 1


def finish(meta, parts, got, arrived, gain, router):
    columns = parts[0].shape[1]
    chips, rows, _ = arrived.shape
    return pl.pallas_call(
        functools.partial(finish_kernel, len(parts)),
        out_shape=(
            jax.ShapeDtypeStruct((chips, rows, columns), jnp.bfloat16),
            jax.ShapeDtypeStruct((chips, rows, router.shape[0] + 1), jnp.float32),
        ),
        in_specs=[IN_SMEM] + [IN_VMEM] * (3 + 2 * len(parts)),
        out_specs=(IN_VMEM, IN_VMEM),
        compiler_params=pltpu.CompilerParams(vmem_limit_bytes=16 * 1024 * 1024),
    )(meta, arrived, gain, router, *parts, *got)


def own_kernel(count, meta, *refs):
    pieces, (out, sems) = refs[:-2], refs[-2:]
    chips, share, _ = out.shape
    half = chips * share
    place = meta[chips]
    for s in range(STREAMS):

        @pl.when(place * share // half == s)
        def _():
            at = pl.ds(pl.multiple_of(place * share - s * half, share), share)
            copies = [
                pltpu.make_async_copy(pieces[s * count + i].at[at, :], out.at[meta[i]], sems.at[i])
                for i in range(count)
            ]
            for copy in copies:
                copy.start()
            for copy in copies:
                copy.wait()


def own_residual(meta, pieces, share):
    chips = len(pieces[0])
    depth = pieces[0][0].shape[1]
    return pl.pallas_call(
        functools.partial(own_kernel, chips),
        out_shape=jax.ShapeDtypeStruct((chips, share, depth), jnp.bfloat16),
        in_specs=[IN_SMEM] + [ANY] * (STREAMS * chips),
        out_specs=IN_VMEM,
        scratch_shapes=[pltpu.SemaphoreType.DMA((chips,))],
        compiler_params=pltpu.CompilerParams(vmem_limit_bytes=VMEM),
    )(meta, *[piece for part in pieces for piece in part])


def piece_starts(pieces, count, held, sems):
    half = held.shape[1] // STREAMS
    depth = pieces[0].shape[1]
    for i in range(count):
        for s in range(STREAMS):
            at = i // (held.shape[2] // depth)
            target = held.at[at, pl.ds(s * half, half), :]
            if held.shape[2] != depth:
                target = target.at[:, pl.ds(i % 2 * depth, depth)]
            source = pieces[s * count + i].at[pl.ds(0, half), :]
            pltpu.make_async_copy(source, target, sems.at[i]).start()


def add_products(count, depth, held, weight, total, piece_sems, weight_sems):
    per = held.shape[2] // depth

    def ready(k, at):
        block = held.at[k] if per == 1 else held.at[k, :, pl.ds(at * depth, depth)]
        wait_for(block, piece_sems.at[per * k + at])
        wait_for(weight.at[k, pl.ds(at * depth, depth), :], weight_sems.at[per * k + at])

    def add(k, deep):
        for at in range(0, total.shape[1], 256):
            total[:, at : at + 256] += jnp.dot(
                held[k, :, :deep],
                weight[k, :deep, at : at + 256],
                preferred_element_type=jnp.float32,
            )

    total[...] = jnp.zeros_like(total)

    @pl.loop(0, count // per)
    def _(k):
        for at in range(per):
            ready(k, at)
        add(k, per * depth)

    if count % per:
        ready(count // per, 0)
        add(count // per, depth)


def weight_start(at, gate_up, depth, per, target, sem):
    for p, part in enumerate(gate_up):

        @pl.when(at // per == p)
        def _():
            span = pl.ds(pl.multiple_of(at % per * depth, 16), depth)
            pltpu.make_async_copy(part.at[span, :], target, sem).start()


def wait_for(ref, sem):
    pltpu.make_async_copy(ref, ref, sem).wait()


def gate_kernel(parts, first, count, chips, meta, *refs):
    gate_up, pieces = refs[:parts], refs[parts:-5]
    total, held, weight, piece_sems, weight_sems = refs[-5:]
    depth = pieces[0].shape[1]
    for k in range(count):
        side = held.shape[2] // depth
        target = weight.at[k // side, pl.ds(k % side * depth, depth), :]
        weight_start(meta[first + k], gate_up, depth, chips // parts, target, weight_sems.at[k])
        if k == 0:
            piece_starts(pieces, count, held, piece_sems)

    add_products(count, depth, held, weight, total, piece_sems, weight_sems)


def gate(meta, first, pieces, rows, gate_up, chips):
    count = len(pieces[0])
    depth = pieces[0][0].shape[1]
    side = 1 if depth % 128 else 2
    wide = gate_up[0].shape[1]
    return pl.pallas_call(
        functools.partial(gate_kernel, len(gate_up), first, count, chips),
        out_shape=jax.ShapeDtypeStruct((rows, wide), jnp.float32),
        in_specs=[IN_SMEM] + [IN_HBM] * len(gate_up) + [ANY] * (STREAMS * count),
        out_specs=IN_VMEM,
        scratch_shapes=[
            pltpu.VMEM((-(-count // side), rows, side * depth), jnp.bfloat16),
            pltpu.VMEM((-(-count // side), side * depth, wide), jnp.bfloat16),
            pltpu.SemaphoreType.DMA((count,)),
            pltpu.SemaphoreType.DMA((count,)),
        ],
        compiler_params=pltpu.CompilerParams(vmem_limit_bytes=VMEM),
        cost_estimate=pl.CostEstimate(
            flops=2 * rows * count * depth * wide,
            bytes_accessed=2 * count * depth * (wide + rows),
            transcendentals=0,
        ),
    )(meta, *gate_up, *[piece for part in pieces for piece in part])


def tail_kernel(parts, first, count, chips, meta, factors, before, down, *refs):
    gate_up, pieces = refs[:parts], refs[parts : parts + STREAMS * count]
    rest = refs[parts + STREAMS * count :]
    outs = rest[:4]
    held, weight, total, earlier, active, ordered, second, staged = rest[4:12]
    piece_sems, weight_sems, earlier_sem, second_sems, out_sems = rest[12:]
    rows = held.shape[1]
    depth = pieces[0].shape[1]
    hidden = active.shape[1]
    span = staged.shape[2]
    steps = second.shape[1] // span
    for k in range(count):
        side = held.shape[2] // depth
        target = weight.at[k // side, pl.ds(k % side * depth, depth), :]
        weight_start(meta[first + k], gate_up, depth, chips // parts, target, weight_sems.at[k])
        if k == 0:
            piece_starts(pieces, count, held, piece_sems)
    pltpu.make_async_copy(before, earlier, earlier_sem).start()

    def columns(n):
        return pl.ds(pl.multiple_of(n * span, span), span)

    def second_copy(n):
        size = hidden // second_sems.shape[0]
        span_rows = pl.ds(n * size, size)
        return pltpu.make_async_copy(
            down.at[span_rows, :], second.at[span_rows, :], second_sems.at[n]
        )

    for n in range(second_sems.shape[0]):
        second_copy(n).start()

    add_products(count, depth, held, weight, total, piece_sems, weight_sems)

    pltpu.make_async_copy(before, earlier, earlier_sem).wait()
    columns_of = jnp.concatenate([factors[...], jnp.zeros((6, rows), jnp.float32)], axis=0).T
    norm, scale = columns_of[:, 0:1], columns_of[:, 1:2]
    gate = (total[:, :hidden] + earlier[:, :hidden]) * norm
    up = (total[:, hidden:] + earlier[:, hidden:]) * (norm * scale)
    active[...] = (gate * jax.nn.sigmoid(gate) * up).astype(jnp.bfloat16)
    share = rows // (2 * chips)
    for i in range(2 * chips):
        at = pl.ds(pl.multiple_of(meta[chips + 1 + i] * share, share), share)
        ordered[i * share : (i + 1) * share, :] = active[at, :]

    for n in range(second_sems.shape[0]):
        second_copy(n).wait()

    def out_copies(n):
        copies, at = [], 0
        slot = n % 2
        for i, out in enumerate(outs):
            size = out.shape[0]
            source = staged.at[slot, pl.ds(at, size), :]
            copies.append(
                pltpu.make_async_copy(source, out.at[:, columns(n)], out_sems.at[slot, i])
            )
            at += size
        return copies

    @pl.loop(0, steps)
    def _(n):
        @pl.when(n >= 2)
        def _():
            for copy in out_copies(n - 2):
                copy.wait()

        result = jnp.dot(
            ordered[...], second[:, columns(n)], preferred_element_type=jnp.float32
        )
        staged[n % 2] = result.astype(jnp.bfloat16)
        for copy in out_copies(n):
            copy.start()

    for n in range(max(0, steps - 2), steps):
        for copy in out_copies(n):
            copy.wait()


def tail(meta, first, pieces, rows, gate_up, before, factors, down, chips):
    count = len(pieces[0])
    depth = pieces[0][0].shape[1]
    side = 1 if depth % 128 else 2
    wide = gate_up[0].shape[1]
    hidden, width = down.shape
    share = rows // (2 * chips)
    steps = max(1, width // 1024)
    shapes = [3 * share, 3 * share, rows // 2 - 3 * share, rows // 2 - 3 * share]
    return pl.pallas_call(
        functools.partial(tail_kernel, len(gate_up), first, count, chips),
        out_shape=tuple(jax.ShapeDtypeStruct((n, width), jnp.bfloat16) for n in shapes),
        in_specs=[IN_SMEM, IN_VMEM, ANY, IN_HBM]
        + [IN_HBM] * len(gate_up)
        + [ANY] * (STREAMS * count),
        out_specs=(ANY,) * 4,
        scratch_shapes=[
            pltpu.VMEM((-(-count // side), rows, side * depth), jnp.bfloat16),
            pltpu.VMEM((-(-count // side), side * depth, wide), jnp.bfloat16),
            pltpu.VMEM((rows, wide), jnp.float32),
            pltpu.VMEM((rows, wide), jnp.float32),
            pltpu.VMEM((rows, hidden), jnp.bfloat16),
            pltpu.VMEM((rows, hidden), jnp.bfloat16),
            pltpu.VMEM((hidden, width), jnp.bfloat16),
            pltpu.VMEM((2, rows, width // steps), jnp.bfloat16),
            pltpu.SemaphoreType.DMA((count,)),
            pltpu.SemaphoreType.DMA((count,)),
            pltpu.SemaphoreType.DMA(()),
            pltpu.SemaphoreType.DMA((4,)),
            pltpu.SemaphoreType.DMA((2, 4)),
        ],
        compiler_params=pltpu.CompilerParams(vmem_limit_bytes=VMEM),
        cost_estimate=pl.CostEstimate(
            flops=2 * rows * (count * depth * wide + hidden * width),
            bytes_accessed=2 * (count * depth * (wide + rows) + width * (hidden + rows)),
            transcendentals=rows * wide,
        ),
    )(meta, factors, before, down, *gate_up, *[piece for part in pieces for piece in part])


def body(
    hidden_in,
    queries,
    latent_cache,
    new_latent,
    cache_lengths,
    value_up,
    out_proj,
    norm_gain,
    router,
    expert_ids,
    w_gate_up,
    w_down,
):
    rows = hidden_in.shape[0]
    width = hidden_in.shape[1]
    chips = lax.axis_size("chip")
    cores = lax.axis_size("core")
    groups = lax.axis_size(GROUP)
    core = lax.axis_index("core")
    chip = lax.axis_index("chip")
    group = lax.axis_index(GROUP)
    place = chip * cores + core
    chip_cols = width // chips
    own_cols = chip_cols // cores
    expert_count = router.shape[1]
    total = chips * cores * rows
    order = ring_order()

    outgoing = hidden_in.reshape(rows, chips, chip_cols).transpose(1, 0, 2)
    names = jnp.broadcast_to(expert_ids.astype(jnp.bfloat16)[None], (chips, rows, TOP))
    arrived = lax.all_to_all(
        jnp.concatenate([outgoing, names], axis=2), "chip", split_axis=0, concat_axis=0, tiled=True
    )

    parts = 4
    quarter_rows = width // parts
    gate_up = []
    final = chips // 2 - 1
    projected = []

    def quarter(moving, after):
        p = len(gate_up)
        raw, _ = lax.optimization_barrier((w_gate_up, after))
        part = raw[0, p * quarter_rows : (p + 1) * quarter_rows].reshape(quarter_rows, -1)
        moving, part = lax.optimization_barrier((moving, part))
        gate_up.append(part)
        return moving

    def during_first(s, i, moving, pieces):
        if (s, i) == (None, None):
            part = project([piece[: chips - 1] for piece in pieces], out_proj.T)
            moving, part = lax.optimization_barrier((moving, part))
            projected.append(part)
        if (s, i) == (1, 1):
            for t in range(STREAMS):
                moving = quarter(moving, pieces[t][0])
        return moving

    own_gain = lax.dynamic_slice_in_dim(norm_gain, place * own_cols, own_cols, 0)[None]
    own_router = lax.dynamic_slice_in_dim(router.T, place * own_cols, own_cols, 1)
    first_rows, then_rows = reduce_rows()
    meta = jnp.stack(order + [place] + first_rows + then_rows).astype(jnp.int32)

    head_out = attend(queries, latent_cache, new_latent, cache_lengths, value_up)
    head_out, arrived = lax.optimization_barrier((head_out, arrived))
    other_arrived = swap_cores(arrived)
    low, high = by_core(core, head_out, swap_cores(head_out))
    block = jnp.concatenate([low, high], axis=0)
    half = block.shape[1] // STREAMS
    pieces = ring_gather([block[:, s * half : (s + 1) * half] for s in range(STREAMS)], during_first)
    projected.append(project([piece[chips - 1 :] for piece in pieces], out_proj.T))
    parts, got = [], []
    for part in projected:
        if groups == 2:
            parts.append(part)
            got.append(lax.ppermute(part.astype(jnp.bfloat16), "sec", SWAP))
        else:
            parts.append(lax.psum(part, GROUP))
            got.append(jnp.zeros(part.shape, jnp.bfloat16))
    arrived = jnp.stack(by_core(core, arrived, other_arrived), axis=1)
    arrived = arrived.reshape(chips, cores * rows, chip_cols + TOP)
    residual, stats = finish(meta, parts, got, arrived, own_gain, own_router)
    residual = residual.reshape(total, own_cols)
    stats = stats.reshape(total, expert_count + 1).T
    stats = stats + swap_cores(stats)
    low, high = by_core(core, residual, swap_cores(residual))
    block = jnp.concatenate([low, high], axis=1)
    half = total // STREAMS

    ids = arrived[:, :, chip_cols:].reshape(total, TOP).T.astype(jnp.int32)
    grid = lax.broadcasted_iota(jnp.int32, (1, expert_count, 1), 1)
    chosen = jnp.any(ids[:, None, :] == grid, axis=0)

    def packed(sums):
        high = lax.reduce_precision(sums, 8, 7)
        flat = jnp.stack([high, sums - high]).astype(jnp.bfloat16).reshape(-1)
        extra = -(-flat.size // (16 * chip_cols)) * 16
        return jnp.pad(flat, (0, extra * chip_cols - flat.size)).reshape(extra, chip_cols)

    def unpacked(pieces):
        count = expert_count + 1
        added = sum(piece[half:].astype(jnp.float32) for piece in pieces).reshape(-1)
        return jnp.sum(added[: 2 * count * half].reshape(2, count, half), axis=0)

    blocks = []
    for s in range(STREAMS):
        span = slice(s * half, (s + 1) * half)
        blocks.append(jnp.concatenate([block[span], packed(stats[:, span])], axis=0))

    def route(stats):
        norm = lax.rsqrt(stats[expert_count:] / width + norm_epsilon)
        affinity = jnp.where(chosen, jax.nn.sigmoid(stats[:expert_count] * norm), 0.0)
        scale = jnp.sum(jnp.where(grid[0] == place, affinity, 0.0), axis=0, keepdims=True)
        scale = route_scale * scale / jnp.sum(affinity, axis=0, keepdims=True)
        return jnp.concatenate([norm, scale], axis=0)

    sums = []
    def during_second(s, i, moving, pieces):
        if (s, i) == (STREAMS - 1, None):
            moving, sums[0] = lax.optimization_barrier((moving, sums[0]))
        if (s, i) == (1, 1):
            for t in range(STREAMS):
                moving = quarter(moving, pieces[t][0])
        if (s, i) == (STREAMS - 1, final - 1):
            blocks = [piece[: chips - 4] for piece in pieces]
            blocks, _ = lax.optimization_barrier((blocks, moving))
            sums.append(gate(meta, 0, blocks, total, gate_up, chips))
        return moving

    pieces = ring_gather(blocks, during_second)
    stats = jnp.concatenate([unpacked(part) for part in pieces], axis=1)
    keep_first, give_first, keep_then, give_then = tail(
        meta,
        chips - 4,
        [piece[chips - 4 :] for piece in pieces],
        total,
        gate_up,
        sums[0],
        route(stats),
        w_down[0],
        chips,
    )

    got = [swap_cores(give_first), swap_cores(give_then)]

    def own_columns(block):
        held, _ = lax.optimization_barrier((pieces, block))
        own = own_residual(meta, held, rows).reshape(groups, chips // groups, rows, chip_cols)
        own = lax.dynamic_index_in_dim(own, group, 0, keepdims=False)
        own = own.transpose(1, 0, 2).reshape(rows, width // groups).astype(jnp.float32)
        span = width // groups
        return own / lax.dynamic_slice_in_dim(norm_gain, group * span, span, 0)

    mixture, own = ring_reduce([keep_first, keep_then], got, own_columns)
    if groups == 2:
        mixture = plus(*mixture)
    else:
        mixture = jnp.concatenate(mixture, axis=1).reshape(rows, groups, width // groups)
        mixture = lax.psum_scatter(mixture, GROUP, scatter_dimension=1, tiled=False)
    return plus(own, mixture).astype(jnp.bfloat16)


def solution(mesh):
    sec, batch, head = mesh.shape["sec"], mesh.shape["batch"], mesh.shape["head"]
    devices = mesh.devices.reshape(sec, batch // 2, 2, head)
    split = Mesh(devices, ("sec", "chip", "core", "head"))
    tokens = ("chip", "core")
    in_specs = (
        P(tokens, None),
        P(tokens, GROUP, None),
        P(tokens, None, None),
        P(tokens, None),
        P(tokens),
        P(GROUP, None, None),
        P(GROUP, tokens),
        P(),
        P(),
        P(tokens, None),
        P(tokens, None, None, GROUP),
        P(tokens, GROUP, None),
    )
    out_specs = P(tokens, GROUP)
    return jax.shard_map(body, mesh=split, in_specs=in_specs, out_specs=out_specs, check_vma=False)
```
